32 devices in a mesh: dp: 8 (over y, x, core), tensor: 4 (over z).
Axes of the slice: x: 2, y: 2, z: 4, core: 2. Of those that a mesh axis runs over, the one named last changes fastest.
Arguments:
- hidden_in: bfloat16 [32768, 768], P(('dp', 'tensor')), may hold values from -6 to 6
- cotangent: bfloat16 [32768, 768], P(('dp', 'tensor')), may hold values from -6 to 6
- norm_gain: bfloat16 [768], P('dp'), may hold values from 0.099609375 to 1.8984375
- gate_proj: bfloat16 [768, 1536], P('dp', 'tensor'), may hold values from -0.21875 to 0.21875
- input_proj: bfloat16 [768, 1536], P('dp', 'tensor'), may hold values from -0.21875 to 0.21875
- step_proj: bfloat16 [768, 24], P('dp', 'tensor'), may hold values from -0.21875 to 0.21875
- shared_proj: bfloat16 [768, 256], P('dp'), may hold values from -0.21875 to 0.21875
- output_proj: bfloat16 [768, 1536], P('dp', 'tensor'), may hold values from -0.15625 to 0.15625
- conv_inner: float32 [5, 1536], P(None, 'tensor'), may hold values from -0.5 to 0.5
- conv_shared: float32 [5, 256], replicated, may hold values from -0.5 to 0.5
- step_bias: float32 [24], P('tensor'), may hold values from -8.5 to -2
- decay_log: float32 [24], P('tensor'), may hold values from -0.7 to 2.77
- skip_gain: float32 [24], P('tensor'), may hold values from 0.5 to 1.5
- gated_gain: float32 [1536], P('tensor'), may hold values from 0.1 to 1.9
Outputs:
- block_out: bfloat16 [32768, 768], P(('dp', 'tensor'))
- grad_hidden: bfloat16 [32768, 768], P(('dp', 'tensor'))
- grad_norm_gain: float32 [768], P(('dp', 'tensor'))
- grad_gate_proj: float32 [768, 1536], P('dp', 'tensor')
- grad_input_proj: float32 [768, 1536], P('dp', 'tensor')
- grad_step_proj: float32 [768, 24], P('dp', 'tensor')
- grad_shared_proj: float32 [768, 256], P(('dp', 'tensor'))
- grad_output_proj: float32 [768, 1536], P('dp', 'tensor')
- grad_conv_inner: float32 [5, 1536], P(None, 'tensor')
- grad_conv_shared: float32 [5, 256], replicated
- grad_step_bias: float32 [24], P('tensor')
- grad_decay_log: float32 [24], P('tensor')
- grad_skip_gain: float32 [24], P('tensor')
- grad_gated_gain: float32 [1536], P('tensor')
The draws below stay inside these ranges and needn't reach their ends.
All inputs are finite; a program needn't handle non-finite values.
Results may differ from the reference program's by a relative error of at most 0.015.
Values may be sent and summed in bfloat16 or wider, within the bound.
No kernel may reach another device: no remote copies, remote signals or barrier semaphores. Data moves between devices by JAX's collectives and lax.ppermute only.
A program may use at most 256 MiB of HBM per device.

```python
import jax
import jax.numpy as jnp
from jax import lax

D = 768
HEADS = 24
HEADDIM = 64
STATE = 128
CONV = 4
SPAN = 256
SEQ_LEN = 4096
INNER = 1536
TOKENS = 32768


def pick_heads(key, extra):
    places = jnp.arange(HEADS)
    offset = jax.random.randint(jax.random.fold_in(key, 101), (), 0, 3)
    chosen = jax.random.randint(jax.random.fold_in(key, 102), (HEADS,), 0, 6) < extra
    return jnp.logical_or((places + offset) % 3 == 0, chosen)


def draw_decay_log(key, part):
    marked = pick_heads(key, 1)
    low_end, high_end = (-0.4, 0.2)
    key = jax.random.fold_in(key, 11)
    unit = jax.random.uniform(key, (HEADS,), jnp.float32)
    quick = 2.77 * unit
    lasting = low_end + (high_end - low_end) * unit
    return jnp.where(marked, lasting, quick).astype(jnp.float32)


def draw_step_bias(key, part):
    marked = pick_heads(key, 1)
    low_end, high_end = (-8.2, -7.6)
    key = jax.random.fold_in(key, 23)
    unit = jax.random.uniform(key, (HEADS,), jnp.float32)
    quick = -4.0 + 2.0 * unit
    lasting = low_end + (high_end - low_end) * unit
    return jnp.where(marked, lasting, quick).astype(jnp.float32)


def shard_levels(key, dims, cuts, smallest, largest):
    gain, own = 1.0, jax.random.fold_in(key, 6)
    for axis_at, parts in cuts:
        heights = jnp.exp(jax.random.uniform(jax.random.fold_in(own, axis_at), (parts,), jnp.float32, smallest / len(cuts), largest / len(cuts)))
        gain = gain * jnp.repeat(heights, dims[axis_at] // parts).reshape([-1 if axis == axis_at else 1 for axis in range(len(dims))])
    return gain


def normal_values(key, shape, width, most, split=(), kind=jnp.bfloat16):
    entries = jax.random.normal(key, shape, jnp.float32) * width
    if len(split) > 0:
        entries = shard_levels(key, shape, split, -0.22, 0.18) * entries
    return jnp.clip(entries, min=-most, max=most).astype(kind)


def setup_inputs(seed: int = 0) -> dict:
    key_of = jax.random.split(jax.random.key(seed), 15)
    hidden_in = normal_values(key_of[0], (TOKENS, D), 1.0, 6.0, ((0, 32),))
    cotangent = normal_values(key_of[1], (TOKENS, D), 1.0, 6.0, ((0, 32),))
    norm_gain = jnp.clip(1.0 + 0.18 * jax.random.normal(key_of[2], (D,), jnp.float32), 0.099609375, 1.8984375).astype(jnp.bfloat16)
    gate_proj = normal_values(key_of[3], (D, INNER), D ** -0.5, 0.21875, ((0, 8), (1, 4)))
    input_proj = normal_values(key_of[4], (D, INNER), D ** -0.5, 0.21875, ((0, 8), (1, 4)))
    step_proj = normal_values(key_of[5], (D, HEADS), D ** -0.5, 0.21875, ((0, 8), (1, 4)))
    shared_proj = normal_values(key_of[6], (D, 2 * STATE), D ** -0.5, 0.21875, ((0, 8),))
    output_proj = normal_values(key_of[7], (D, INNER), INNER ** -0.5, 0.15625, ((0, 8), (1, 4)))
    conv_inner = jnp.clip(jax.random.uniform(key_of[8], (CONV + 1, INNER), jnp.float32, -0.5, 0.5) * shard_levels(key_of[8], (CONV + 1, INNER), ((1, 4),), -0.4, 0.0), -0.5, 0.5)
    conv_shared = jnp.clip(jax.random.uniform(key_of[9], (CONV + 1, 2 * STATE), jnp.float32, -0.5, 0.5), -0.5, 0.5)
    step_bias = draw_step_bias(jax.random.fold_in(key_of[14], 71), 0)
    decay_log = draw_decay_log(jax.random.fold_in(key_of[14], 71), 0)
    skip_gain = jnp.clip(1.0 + 0.1 * jax.random.normal(key_of[12], (HEADS,), jnp.float32), 0.5, 1.5)
    gated_gain = jnp.clip(1.0 + 0.18 * jax.random.normal(key_of[13], (INNER,), jnp.float32), 0.1, 1.9)
    return dict(hidden_in=hidden_in, cotangent=cotangent, norm_gain=norm_gain, gate_proj=gate_proj, input_proj=input_proj, step_proj=step_proj, shared_proj=shared_proj, output_proj=output_proj, conv_inner=conv_inner, conv_shared=conv_shared, step_bias=step_bias, decay_log=decay_log, skip_gain=skip_gain, gated_gain=gated_gain)


epsilon = 1e-05
highest = lax.Precision.HIGHEST

@jax.custom_vjp
def low(v):
    return lax.optimization_barrier(v.astype(jnp.bfloat16)).astype(jnp.float32)

@jax.custom_vjp
def low_back(v):
    return v

def low_keep(v):
    return (low(v), None)

def low_pass(kept, grad):
    return (grad,)

def back_keep(v):
    return (v, None)

def back_low(kept, grad):
    return (low(grad),)
low.defvjp(low_keep, low_pass)
low_back.defvjp(back_keep, back_low)

def causal_conv(values, taps_bias):
    length = values.shape[0]
    taps = taps_bias.shape[0] - 1
    padded = jnp.concatenate([jnp.zeros((taps - 1, values.shape[1]), jnp.float32), values], axis=0)
    total = jnp.broadcast_to(taps_bias[taps], values.shape)
    for offset in range(taps):
        total = total + taps_bias[offset] * padded[offset:offset + length]
    return total

def state_scan(inputs, steps, rates, key_rows, read_rows):
    length, heads, head_size = inputs.shape
    count = length // SPAN
    causal = jnp.arange(SPAN)[:, None] >= jnp.arange(SPAN)[None, :]

    def one_block(state, pieces):
        piece_in, piece_step, piece_key, piece_read = pieces
        logdecay = jnp.cumsum(piece_step * rates[None, :], axis=0).T
        gaps = logdecay[:, :, None] - logdecay[:, None, :]
        decay = jnp.exp(jnp.where(causal[None], gaps, -jnp.inf))
        scores = jnp.dot(piece_read, piece_key.T, precision=highest)
        mixing = scores[None] * decay * piece_step.T[:, None, :]
        within = jnp.einsum('hts,shp->thp', mixing, piece_in, precision=highest)
        carried = jnp.einsum('tn,hpn->thp', piece_read, state, precision=highest) * jnp.exp(logdecay).T[:, :, None]
        tail = jnp.exp(logdecay[:, -1:] - logdecay) * piece_step.T
        update = jnp.einsum('hs,shp,sn->hpn', tail, piece_in, piece_key, precision=highest)
        new_state = state * jnp.exp(logdecay[:, -1])[:, None, None] + update
        return (new_state, within + carried)
    pieces = (inputs.reshape(count, SPAN, heads, head_size), steps.reshape(count, SPAN, heads), key_rows.reshape(count, SPAN, -1), read_rows.reshape(count, SPAN, -1))
    initial = jnp.zeros((heads, head_size, key_rows.shape[1]), jnp.float32)
    final, outputs = lax.scan(jax.checkpoint(one_block), initial, pieces)
    return outputs.reshape(length, heads, head_size)

def mixer(gate_rows, input_rows, step_rows, shared_rows, conv_inner, conv_shared, step_bias, decay_log, skip_gain):
    length = input_rows.shape[0]
    heads = step_rows.shape[1]
    mixed_in = jax.nn.silu(causal_conv(input_rows, conv_inner)).reshape(length, heads, HEADDIM)
    shared = jax.nn.silu(causal_conv(shared_rows, conv_shared))
    steps = jax.nn.softplus(step_rows + step_bias)
    rates = -jnp.exp(decay_log)
    scanned = state_scan(mixed_in, steps, rates, shared[:, :STATE], shared[:, STATE:])
    result = scanned + skip_gain[None, :, None] * mixed_in
    return result.reshape(length, heads * HEADDIM) * jax.nn.silu(gate_rows)

def block_forward(hidden, norm_gain, gate_proj, input_proj, step_proj, shared_proj, output_proj, conv_inner, conv_shared, step_bias, decay_log, skip_gain, gated_gain):
    scale = lax.rsqrt(lax.optimization_barrier(jnp.mean(hidden * hidden, axis=1, keepdims=True)) + epsilon)
    normed = low(hidden * scale * norm_gain)
    gate_rows = low_back(jnp.dot(normed, gate_proj, precision=highest))
    input_rows = low_back(jnp.dot(normed, input_proj, precision=highest))
    step_rows = low_back(jnp.dot(normed, step_proj, precision=highest))
    shared_rows = low_back(jnp.dot(normed, shared_proj, precision=highest))
    gated = mixer(gate_rows, input_rows, step_rows, shared_rows, conv_inner, conv_shared, step_bias, decay_log, skip_gain)
    gated_scale = lax.rsqrt(lax.optimization_barrier(jnp.mean(gated * gated, axis=1, keepdims=True)) + epsilon)
    mixed = low(gated * gated_scale * gated_gain)
    return hidden + jnp.dot(mixed, output_proj.T, precision=highest)

def reference(hidden_in, cotangent, norm_gain, gate_proj, input_proj, step_proj, shared_proj, output_proj, conv_inner, conv_shared, step_bias, decay_log, skip_gain, gated_gain):
    weights = tuple((item.astype(jnp.float32) for item in (norm_gain, gate_proj, input_proj, step_proj, shared_proj, output_proj, conv_inner, conv_shared, step_bias, decay_log, skip_gain, gated_gain)))
    count = hidden_in.shape[0] // SEQ_LEN
    inputs = hidden_in.astype(jnp.float32).reshape(count, SEQ_LEN, -1)
    backs = cotangent.astype(jnp.float32).reshape(count, SEQ_LEN, -1)

    def one_sequence(totals, pair):
        hidden, back = pair
        result, pullback = jax.vjp(block_forward, hidden, weights[0], weights[1], weights[2], weights[3], weights[4], weights[5], weights[6], weights[7], weights[8], weights[9], weights[10], weights[11])
        grads = pullback(back)
        return (tuple((total + grad for total, grad in zip(totals, grads[1:]))), (result, grads[0]))
    initial = tuple((jnp.zeros_like(item) for item in weights))
    totals, (results, hidden_grads) = lax.scan(one_sequence, initial, (inputs, backs))
    return (results.reshape(hidden_in.shape).astype(jnp.bfloat16), hidden_grads.reshape(hidden_in.shape).astype(jnp.bfloat16), totals[0], totals[1], totals[2], totals[3], totals[4], totals[5], totals[6], totals[7], totals[8], totals[9], totals[10], totals[11])
```

```python
import functools

import jax
import jax.numpy as jnp
from jax import lax
from jax.experimental import pallas as pl
from jax.experimental.pallas import tpu as pltpu
from jax.sharding import PartitionSpec as P

HEADDIM = 64
STATE = 128
SEQ_LEN = 4096
SPAN = 128
LANES = 128
epsilon = 1e-05
bf16 = jnp.bfloat16
f32 = jnp.float32


def dot(a, b):
    return lax.dot_general(a, b, (((1,), (0,)), ((), ())), preferred_element_type=f32)


def dot_nt(a, b):
    return lax.dot_general(a, b, (((1,), (1,)), ((), ())), preferred_element_type=f32)


def dot_tn(a, b):
    return lax.dot_general(a, b, (((0,), (0,)), ((), ())), preferred_element_type=f32)


def exact_dot(a, b):
    return lax.dot_general(
        a, b, (((1,), (0,)), ((), ())), preferred_element_type=f32, precision=lax.Precision.HIGHEST
    )


def split_dot(values, matrix):
    high = values.astype(bf16)
    low = (values - high.astype(f32)).astype(bf16)
    return dot(high, matrix) + dot(low, matrix)


def sigmoid(v):
    return 1.0 / (1.0 + jnp.exp(-v))


def softplus(v):
    u = jnp.exp(-jnp.abs(v))
    series = u * (1.0 - u * (0.5 - u * (1.0 / 3.0 - 0.25 * u)))
    return jnp.maximum(v, 0.0) + jnp.where(u < 0.01, series, jnp.log(1.0 + u))


def causal_mask(rows):
    at = lax.broadcasted_iota(jnp.int32, (rows, rows), 0)
    to = lax.broadcasted_iota(jnp.int32, (rows, rows), 1)
    return at >= to


def head_lanes(heads):
    return lax.broadcasted_iota(jnp.int32, (1, LANES), 1) < heads


def step_sizes(v, heads):
    return jnp.where(head_lanes(heads), softplus(v), 0.0)


def decay_rates(decay_log, heads):
    return jnp.where(head_lanes(heads), -jnp.exp(decay_log), 0.0)


def pair_stack(pair):
    lane = lax.broadcasted_iota(jnp.int32, pair.shape, 1)
    zero = jnp.zeros_like(pair)
    return jnp.concatenate(
        [jnp.where(lane < HEADDIM, pair, zero), jnp.where(lane >= HEADDIM, pair, zero)], axis=0
    )


def pair_decay(logs, logs_t, causal, pair):
    parts = []
    for head in (2 * pair, 2 * pair + 1):
        gap = logs[:, head : head + 1] - logs_t[head : head + 1, :]
        parts.append(jnp.exp(jnp.where(causal, gap, -1e30)))
    return parts


def first_kernel(
    heads,
    hid_ref, halo_ref, gain_ref, w_ref, cx_ref, cbc_ref, sb_ref, dl_ref, ex_ref,
    nb_ref, xr_ref, xc_ref, bcr_ref, bcc_ref, v_ref, logs_ref, lpre_ref, sloc_ref, fin_ref,
    xext, bext, state, total,
):
    rows = hid_ref.shape[0]
    inner = xr_ref.shape[1]
    gain = gain_ref[...]

    def norm(block):
        h = block.astype(f32)
        scale = lax.rsqrt(jnp.mean(h * h, axis=1, keepdims=True) + epsilon)
        return (h * scale * gain).astype(bf16)

    @pl.when(pl.program_id(0) == 0)
    def _():
        state[...] = jnp.zeros_like(state)
        total[...] = jnp.zeros_like(total)
        before = norm(halo_ref[...])
        xext[0:8, :] = dot(before, w_ref[:, :inner])[8:16]
        bext[0:8, :] = dot(before, w_ref[:, inner + LANES :])[8:16]

    @pl.when(pl.program_id(0) > 0)
    def _():
        xext[0:8, :] = xext[rows : rows + 8, :]
        bext[0:8, :] = bext[rows : rows + 8, :]

    nb = norm(hid_ref[...])
    nb_ref[...] = nb
    xr = dot(nb, w_ref[:, :inner])
    xext[8 : 8 + rows, :] = xr
    xr_ref[...] = xr.astype(bf16)
    bcr = dot(nb, w_ref[:, inner + LANES :])
    bext[8 : 8 + rows, :] = bcr
    bcr_ref[...] = bcr
    v = dot(nb, w_ref[:, inner : inner + LANES]) + sb_ref[...]
    v_ref[...] = v
    xc = jnp.broadcast_to(cx_ref[4:5, :], xr.shape)
    bcc = jnp.broadcast_to(cbc_ref[4:5, :], bcr.shape)
    for tap in range(4):
        xc = xc + cx_ref[tap : tap + 1, :] * xext[5 + tap : 5 + tap + rows, :]
        bcc = bcc + cbc_ref[tap : tap + 1, :] * bext[5 + tap : 5 + tap + rows, :]
    xc_ref[...] = xc
    bcc_ref[...] = bcc
    xs = xc * sigmoid(xc)
    keys = (bcc[:, :STATE] * sigmoid(bcc[:, :STATE])).astype(bf16)
    dt = step_sizes(v, heads)
    la = dt * decay_rates(dl_ref[...], heads)
    ones = causal_mask(SPAN).astype(f32)
    ex = ex_ref[...]
    for at in range(rows // SPAN):
        span = slice(at * SPAN, (at + 1) * SPAN)
        logs = exact_dot(ones, la[span])
        logs_ref[span, :] = logs
        last = logs[SPAN - 1 : SPAN, :]
        lpre_ref[at * 8 : at * 8 + 8, :] = jnp.broadcast_to(total[0:1, :], (8, LANES))
        sloc_ref[at * STATE : (at + 1) * STATE, :] = state[...].astype(bf16)
        tail = split_dot(jnp.exp(last - logs) * dt[span], ex)
        shrink = split_dot(jnp.broadcast_to(jnp.exp(last), (8, LANES)), ex)[0:1]
        update = dot_tn(keys[span], (xs[span] * tail).astype(bf16))
        state[...] = state[...] * shrink + update
        total[...] = total[...] + last

    @pl.when(pl.program_id(0) == pl.num_programs(0) - 1)
    def _():
        fin_ref[0:STATE, :] = state[...].astype(bf16)
        whole = split_dot(jnp.broadcast_to(jnp.exp(total[0:1, :]), (16, LANES)), ex)
        fin_ref[STATE : STATE + 16, :] = whole.astype(bf16)


def within_kernel(heads, xc_ref, bcc_ref, v_ref, logs_ref, ex_ref, yi_ref):
    causal = causal_mask(SPAN)
    for at in range(xc_ref.shape[0] // SPAN):
        span = slice(at * SPAN, (at + 1) * SPAN)
        xc = xc_ref[span, :]
        dt = step_sizes(v_ref[span, :], heads)
        xd = (xc * sigmoid(xc) * split_dot(dt, ex_ref[...])).astype(bf16)
        bcc = bcc_ref[span, :]
        bc = (bcc * sigmoid(bcc)).astype(bf16)
        scores = dot_nt(bc[:, STATE:], bc[:, :STATE])
        logs = logs_ref[span, :]
        logs_t = logs.T
        for pair in range(heads // 2):
            lanes = slice(pair * LANES, (pair + 1) * LANES)
            mixing = [(scores * d).astype(bf16) for d in pair_decay(logs, logs_t, causal, pair)]
            yi_ref[span, lanes] = dot(jnp.concatenate(mixing, axis=1), pair_stack(xd[:, lanes]))


def incoming(refs):
    total = None
    for ref in reversed(refs):
        held = ref[0:STATE, :].astype(f32)
        if total is None:
            total = held
        else:
            total = held + ref[STATE : STATE + 1, :].astype(f32) * total
    return total


def middle_kernel(
    heads, far,
    hid_ref, cot_ref, z_ref, yi_ref, xc_ref, bcc_ref, logs_ref, lpre_ref, sloc_ref, wout_ref, gg_ref,
    skip_ref, ex_ref, *rest,
):
    fins = rest[:far]
    (out_ref, mixed_ref, dz_ref, g_ref, sc_ref, uc_ref, adj_ref, ggg_ref, gskip_ref, sin, acc) = rest[far:]

    @pl.when(pl.program_id(0) == 0)
    def _():
        sin[...] = incoming(fins) if far else jnp.zeros_like(sin)
        acc[...] = jnp.zeros_like(acc)
        ggg_ref[...] = jnp.zeros_like(ggg_ref)
        gskip_ref[...] = jnp.zeros_like(gskip_ref)

    ex = ex_ref[...]
    rows = hid_ref.shape[0]
    inner = z_ref.shape[1]
    skip = split_dot(jnp.broadcast_to(skip_ref[...], (8, LANES)), ex)[0:1]
    xc = xc_ref[...]
    xs = xc * sigmoid(xc)
    reads = bcc_ref[:, STATE:]
    reads = (reads * sigmoid(reads)).astype(bf16)
    carried = []
    grown = []
    befores = []
    for at in range(rows // SPAN):
        span = slice(at * SPAN, (at + 1) * SPAN)
        before = split_dot(jnp.exp(lpre_ref[at * 8 : at * 8 + 8, :]), ex)[0:1]
        befores.append(before)
        states = slice(at * STATE, (at + 1) * STATE)
        held = (sloc_ref[states, :].astype(f32) + before * sin[...]).astype(bf16)
        sc_ref[states, :] = held
        growth = split_dot(jnp.exp(logs_ref[span, :]), ex)
        grown.append(growth)
        carried.append(growth * dot(reads[span], held))
    ssm = yi_ref[...] + jnp.concatenate(carried, axis=0) + skip * xs
    z = z_ref[...]
    sz = sigmoid(z)
    act = z * sz
    gated = ssm * act
    gs = lax.rsqrt(jnp.mean(gated * gated, axis=1, keepdims=True) + epsilon)
    gg = gg_ref[...]
    mixed = (gated * gs * gg).astype(bf16)
    mixed_ref[...] = mixed
    out_ref[...] = (hid_ref[...].astype(f32) + dot_nt(mixed, wout_ref[...])).astype(bf16)
    gm = dot(cot_ref[...], wout_ref[...])
    ggg_ref[...] += jnp.sum(gm * gated * gs, axis=0, keepdims=True)
    weighted = gm * gg
    mean = jnp.sum(weighted * gated, axis=1, keepdims=True) / inner
    dgated = weighted * gs - gated * (gs * gs * gs * mean)
    dz_ref[...] = (dgated * ssm * (sz + act * (1.0 - sz))).astype(bf16)
    g = dgated * act
    g_ref[...] = g.astype(bf16)
    gskip_ref[...] += jnp.sum(g * xs, axis=0, keepdims=True)
    for at in range(rows // SPAN):
        span = slice(at * SPAN, (at + 1) * SPAN)
        u = dot_tn(reads[span], (g[span] * grown[at]).astype(bf16))
        uc_ref[at * STATE : (at + 1) * STATE, :] = u.astype(bf16)
        acc[...] += befores[at] * u

    @pl.when(pl.program_id(0) == pl.num_programs(0) - 1)
    def _():
        adj_ref[...] = acc[...].astype(bf16)


def back_within_kernel(
    heads,
    g_ref, xc_ref, bcc_ref, v_ref, logs_ref, yi_ref, sc_ref, ex_ref, ext_ref,
    dxd_ref, dbc_ref, q_ref,
):
    causal = causal_mask(SPAN)
    for at in range(xc_ref.shape[0] // SPAN):
        span = slice(at * SPAN, (at + 1) * SPAN)
        xc = xc_ref[span, :]
        dt = step_sizes(v_ref[span, :], heads)
        xd = (xc * sigmoid(xc) * split_dot(dt, ex_ref[...])).astype(bf16)
        bcc = bcc_ref[span, :]
        bc = (bcc * sigmoid(bcc)).astype(bf16)
        keys, reads = bc[:, :STATE], bc[:, STATE:]
        scores = dot_nt(reads, keys)
        logs = logs_ref[span, :]
        logs_t = logs.T
        g = g_ref[span, :]
        dscores = jnp.zeros((SPAN, SPAN), f32)
        lane = lax.broadcasted_iota(jnp.int32, (SPAN, LANES), 1)
        for pair in range(heads // 2):
            lanes = slice(pair * LANES, (pair + 1) * LANES)
            decays = pair_decay(logs, logs_t, causal, pair)
            mixing = jnp.concatenate([(scores * d).astype(bf16) for d in decays], axis=1)
            gp = g[:, lanes]
            dmix = dot_nt(gp, pair_stack(xd[:, lanes]))
            dscores = dscores + dmix[:, :SPAN] * decays[0] + dmix[:, SPAN:] * decays[1]
            both = dot_tn(mixing, gp)
            dxd_ref[span, lanes] = jnp.where(lane < HEADDIM, both[:SPAN], both[SPAN:])
        states = slice(at * STATE, (at + 1) * STATE)
        held = sc_ref[states, :]
        gf = g.astype(f32)
        grown = gf * split_dot(jnp.exp(logs), ex_ref[...])
        dscores = dscores.astype(bf16)
        dreads = dot(dscores, keys) + dot_nt(grown.astype(bf16), held)
        dkeys = dot_tn(dscores, reads)
        dbc_ref[span, :STATE] = dkeys
        dbc_ref[span, STATE:] = dreads
        q1 = gf * yi_ref[span, :] - xd.astype(f32) * dxd_ref[span, :]
        q2 = grown * dot(reads, held)
        q_ref[span, :] = split_dot(q1 + q2, ext_ref[...])


def last_kernel(
    heads, far,
    g_ref, xc_ref, bcc_ref, v_ref, logs_ref, sc_ref, uc_ref, dxd_ref, dbc_ref, q_ref, dl_ref, skip_ref,
    ex_ref, ext_ref, *rest,
):
    adjs = rest[:far]
    (dxc_ref, dbcc_ref, dv_ref, gsb_ref, gdl_ref, adj) = rest[far:]

    @pl.when(pl.program_id(0) == 0)
    def _():
        adj[...] = incoming(adjs) if far else jnp.zeros_like(adj)
        gsb_ref[...] = jnp.zeros_like(gsb_ref)
        gdl_ref[...] = jnp.zeros_like(gdl_ref)

    ex = ex_ref[...]
    ext = ext_ref[...]
    causal = causal_mask(SPAN)
    not_after = causal.astype(f32)
    strictly = not_after - jnp.logical_and(causal, causal.T).astype(f32)
    upper = 1.0 - strictly
    rates = decay_rates(dl_ref[...], heads)
    skip = split_dot(jnp.broadcast_to(skip_ref[...], (8, LANES)), ex)[0:1]
    for at in reversed(range(xc_ref.shape[0] // SPAN)):
        span = slice(at * SPAN, (at + 1) * SPAN)
        states = slice(at * STATE, (at + 1) * STATE)
        xc = xc_ref[span, :]
        sx = sigmoid(xc)
        xs = xc * sx
        v = v_ref[span, :]
        dt = step_sizes(v, heads)
        bcc = bcc_ref[span, :]
        sbc = sigmoid(bcc)
        keys = (bcc * sbc)[:, :STATE].astype(bf16)
        logs = logs_ref[span, :]
        last = logs[SPAN - 1 : SPAN, :]
        shrink = split_dot(jnp.broadcast_to(jnp.exp(last), (8, LANES)), ex)[0:1]
        tail = split_dot(jnp.exp(last - logs), ex)
        dte = split_dot(dt, ex)
        held = adj[...]
        held_low = held.astype(bf16)
        dxu = tail * dot(keys, held_low)
        xd = xs * dte
        dkeys = dbc_ref[span, :STATE] + dot_nt((xd * tail).astype(bf16), held_low)
        dbc = jnp.concatenate([dkeys, dbc_ref[span, STATE:]], axis=1)
        dbcc_ref[span, :] = dbc * (sbc + bcc * sbc * (1.0 - sbc))
        inner = jnp.sum(held * sc_ref[states, :].astype(f32), axis=0, keepdims=True) * shrink
        inner = split_dot(jnp.broadcast_to(inner, (8, inner.shape[1])), ext)[0:1]
        q3 = split_dot(xd * dxu, ext)
        dxd = dxd_ref[span, :] + dxu
        q4 = split_dot(xs * dxd, ext)
        dla = exact_dot(upper, q_ref[span, :]) + exact_dot(strictly, q3) + inner
        ddt = rates * dla + q4
        dv = jnp.where(head_lanes(heads), ddt * sigmoid(v), 0.0)
        dv_ref[span, :] = dv.astype(bf16)
        gsb_ref[...] += jnp.sum(dv, axis=0, keepdims=True)
        gdl_ref[...] += jnp.sum(dt * dla, axis=0, keepdims=True) * rates
        dxs = dte * dxd + skip * g_ref[span, :].astype(f32)
        dxc_ref[span, :] = dxs * (sx + xs * (1.0 - sx))
        adj[...] = held * shrink + uc_ref[states, :].astype(f32)


def conv_back_kernel(
    dxc_ref, dbcc_ref, dv_ref, nx_ref, nbc_ref, halo_x_ref, halo_bc_ref, xr_ref, bcr_ref, cx_ref, cbc_ref,
    grad_ref, gcx_ref, gcbc_ref, xext, bext,
):
    rows, inner = dxc_ref.shape
    grad_ref[:, inner : inner + LANES] = dv_ref[...]
    last = pl.program_id(0) == pl.num_programs(0) - 1

    @pl.when(pl.program_id(0) == 0)
    def _():
        gcx_ref[...] = jnp.zeros_like(gcx_ref)
        gcbc_ref[...] = jnp.zeros_like(gcbc_ref)

    for ext, own, after, halo, rows_ref, taps, out, sums in (
        (xext, dxc_ref, nx_ref, halo_x_ref, xr_ref, cx_ref, slice(0, inner), gcx_ref),
        (bext, dbcc_ref, nbc_ref, halo_bc_ref, bcr_ref, cbc_ref, slice(inner + LANES, None), gcbc_ref),
    ):
        ext[0:rows, :] = own[...]
        ext[rows : rows + 8, :] = jnp.where(last, halo[...], after[...])
        before = rows_ref[...].astype(f32)
        total = None
        for tap in range(4):
            moved = ext[3 - tap : 3 - tap + rows, :]
            term = taps[tap : tap + 1, :] * moved
            total = term if total is None else total + term
            sums[tap : tap + 1, :] += jnp.sum(before * moved, axis=0, keepdims=True)
        sums[4:5, :] += jnp.sum(own[...], axis=0, keepdims=True)
        grad_ref[:, out] = total.astype(bf16)


def call(kernel, name, grid, ins, in_specs, outs, out_specs, scratch, flops=10**9, moved=10**7):
    return pl.pallas_call(
        kernel,
        grid=grid,
        in_specs=in_specs,
        out_specs=out_specs,
        out_shape=outs,
        scratch_shapes=scratch,
        name=name,
        compiler_params=pltpu.CompilerParams(vmem_limit_bytes=56 * 2**20),
        cost_estimate=pl.CostEstimate(flops=flops, bytes_accessed=moved, transcendentals=0),
    )(*ins)


def rows_of(block, width):
    return pl.BlockSpec((block, width), lambda i: (i, 0))


def whole_of(array):
    return pl.BlockSpec(array.shape, lambda i: (0, 0), pipeline_mode=pl.Buffered(1))


def kept(shape):
    return pl.BlockSpec(shape, lambda i: (0, 0))


def shape(dims, kind):
    return jax.ShapeDtypeStruct(dims, kind)


def pad_rows(array, count):
    return jnp.pad(array, ((0, count - array.shape[0]), (0, 0)))


def pad_lanes(array):
    return jnp.pad(array, ((0, 0), (0, LANES - array.shape[1])))


def per_device(
    hidden_in, cotangent, norm_gain, gate_proj, input_proj, step_proj, shared_proj, output_proj,
    conv_inner, conv_shared, step_bias, decay_log, skip_gain, gated_gain,
):
    tensor_size = lax.axis_size("tensor")
    chips = lax.axis_size("dp") // 2
    place = lax.axis_index("tensor")
    core = lax.axis_index("dp") % 2
    chip = lax.axis_index("dp") // 2
    rows, width = hidden_in.shape
    heads_local = step_proj.shape[1]
    inner_local = gate_proj.shape[1]
    heads = heads_local * tensor_size
    inner = inner_local * tensor_size
    shared = shared_proj.shape[1]
    per_sequence = SEQ_LEN // rows
    far = per_sequence - 1

    def along(value, step):
        pairs = []
        for start in range(tensor_size):
            end = start + step
            if 0 <= end < tensor_size and start // per_sequence == end // per_sequence:
                pairs.append((start, end))
        return lax.ppermute(value, "tensor", pairs)

    def turn_tensor(value, step):
        return lax.ppermute(value, "tensor", [(i, (i + step) % tensor_size) for i in range(tensor_size)])

    def turn_chip(value, step):
        pairs = [(i, (i // 2 + step) % chips * 2 + i % 2) for i in range(2 * chips)]
        return lax.ppermute(value, "dp", pairs)

    def other_core(value):
        return lax.ppermute(value, "dp", [(i, i ^ 1) for i in range(2 * chips)])

    def in_order(turned, at):
        count = len(turned)
        return [lax.select_n((at - s) % count, *turned) for s in range(count)]

    def all_tensor(value):
        turned = [value] + [turn_tensor(value, k) for k in range(1, tensor_size)]
        return in_order(turned, place)

    def all_chips(value):
        turned = [value] + [turn_chip(value, k) for k in range(1, chips)]
        return jnp.stack(in_order(turned, chip))

    def all_cores(value):
        other = other_core(value)
        first = core == 0
        both = jnp.stack([jnp.where(first, value, other), jnp.where(first, other, value)], axis=1)
        return both.reshape(-1, value.shape[-1])

    small = jnp.concatenate(
        [
            conv_inner,
            gated_gain[None],
            jnp.pad(
                jnp.concatenate([step_bias, decay_log, skip_gain]), (0, inner_local - 3 * heads_local)
            )[None],
        ],
        axis=0,
    )
    small = all_tensor(pad_rows(small, 8))
    halo = along(hidden_in[rows - 16 :], 1)
    first_part = all_tensor(jnp.concatenate([input_proj, pad_lanes(step_proj)], axis=1))
    steps_part = jnp.concatenate([p[:, inner_local : inner_local + heads_local] for p in first_part], axis=1)
    first_part = jnp.concatenate(
        [p[:, :inner_local] for p in first_part]
        + [pad_lanes(jnp.concatenate([steps_part, norm_gain[:, None]], axis=1)), shared_proj],
        axis=1,
    )
    second_part, first_part = lax.optimization_barrier(
        (jnp.concatenate([gate_proj, output_proj], axis=1), first_part)
    )
    first_part = all_chips(first_part)
    second_part = all_tensor(second_part)
    second_part = jnp.concatenate(
        [p[:, :inner_local] for p in second_part] + [p[:, inner_local:] for p in second_part], axis=1
    )
    second_part, first_part = lax.optimization_barrier((second_part, first_part))
    weights = all_cores(first_part)
    second_part = all_cores(all_chips(second_part))
    wz, wout = second_part[:, :inner], second_part[:, inner:]
    gain = weights[:, inner + heads].astype(f32)[None]

    wide = jnp.concatenate(small, axis=1)
    cx = pad_rows(wide[:5], 8)
    gg = wide[5:6]
    cbc = pad_rows(conv_shared, 8)

    def head_row(index):
        at = slice(index * heads_local, (index + 1) * heads_local)
        return pad_lanes(jnp.concatenate([p[6:7, at] for p in small], axis=1))

    sb, dl, sg = head_row(0), head_row(1), head_row(2)
    ex = (
        lax.broadcasted_iota(jnp.int32, (LANES, inner), 0)
        == lax.broadcasted_iota(jnp.int32, (LANES, inner), 1) // HEADDIM
    ).astype(bf16)
    ext = ex.T

    block = 2 * SPAN
    steps = rows // block
    chunks = rows // SPAN
    grid = (steps,)
    nb, xr, xc, bcr, bcc, v, logs, lpre, sloc, fin = call(
        functools.partial(first_kernel, heads),
        "first",
        grid,
        (hidden_in, halo, gain, weights, cx, cbc, sb, dl, ex),
        [rows_of(block, width)] + [whole_of(a) for a in (halo, gain, weights, cx, cbc, sb, dl, ex)],
        [
            shape((rows, width), bf16), shape((rows, inner), bf16), shape((rows, inner), f32),
            shape((rows, shared), f32), shape((rows, shared), f32), shape((rows, LANES), f32),
            shape((rows, LANES), f32), shape((chunks * 8, LANES), f32),
            shape((chunks * STATE, inner), bf16), shape((STATE + 16, inner), bf16),
        ],
        [
            rows_of(block, width), rows_of(block, inner), rows_of(block, inner),
            rows_of(block, shared), rows_of(block, shared), rows_of(block, LANES),
            rows_of(block, LANES), rows_of(16, LANES),
            rows_of(2 * STATE, inner), kept((STATE + 16, inner)),
        ],
        [
            pltpu.VMEM((block + 8, inner), f32), pltpu.VMEM((block + 8, shared), f32),
            pltpu.VMEM((STATE, inner), f32), pltpu.VMEM((8, LANES), f32),
        ],
        flops=2 * rows * width * (inner + shared + LANES),
    )
    fins = [along(fin, step) for step in range(1, far + 1)]
    z = dot(nb, wz)
    (yi,) = call(
        functools.partial(within_kernel, heads),
        "within",
        grid,
        (xc, bcc, v, logs, ex),
        [rows_of(block, inner), rows_of(block, shared), rows_of(block, LANES), rows_of(block, LANES), whole_of(ex)],
        [shape((rows, inner), f32)],
        [rows_of(block, inner)],
        [],
        flops=4 * 10**9,
    )
    state_rows = rows_of(2 * STATE, inner)
    out, mixed, dz, g, sc, uc, adj, ggg, gskip = call(
        functools.partial(middle_kernel, heads, far),
        "middle",
        grid,
        (hidden_in, cotangent, z, yi, xc, bcc, logs, lpre, sloc, wout, gg, sg, ex, *fins),
        [
            rows_of(block, width), rows_of(block, width), rows_of(block, inner), rows_of(block, inner),
            rows_of(block, inner), rows_of(block, shared), rows_of(block, LANES), rows_of(16, LANES), state_rows,
        ]
        + [whole_of(a) for a in (wout, gg, sg, ex, *fins)],
        [
            shape((rows, width), bf16), shape((rows, inner), bf16), shape((rows, inner), bf16),
            shape((rows, inner), bf16), shape((chunks * STATE, inner), bf16), shape((chunks * STATE, inner), bf16),
            shape((STATE, inner), bf16), shape((1, inner), f32), shape((1, inner), f32),
        ],
        [
            rows_of(block, width), rows_of(block, inner), rows_of(block, inner), rows_of(block, inner),
            state_rows, state_rows, kept((STATE, inner)), kept((1, inner)), kept((1, inner)),
        ],
        [pltpu.VMEM((STATE, inner), f32), pltpu.VMEM((STATE, inner), f32)],
        flops=4 * rows * width * inner,
    )
    back = jnp.concatenate([adj, fin[STATE:]], axis=0)
    backs = [along(back, -step) for step in range(1, far + 1)]
    grad_out = dot_tn(cotangent, mixed).astype(bf16)
    grad_gate = dot_tn(nb, dz).astype(bf16)
    dn = dot_nt(dz, wz)
    dxd, dbc, q = call(
        functools.partial(back_within_kernel, heads),
        "back_within",
        grid,
        (g, xc, bcc, v, logs, yi, sc, ex, ext),
        [
            rows_of(block, inner), rows_of(block, inner), rows_of(block, shared), rows_of(block, LANES),
            rows_of(block, LANES), rows_of(block, inner), state_rows, whole_of(ex), whole_of(ext),
        ],
        [shape((rows, inner), f32), shape((rows, shared), f32), shape((rows, LANES), f32)],
        [rows_of(block, inner), rows_of(block, shared), rows_of(block, LANES)],
        [],
        flops=8 * 10**9,
    )

    def turned(size, wide_by):
        return pl.BlockSpec((size, wide_by), lambda i: (steps - 1 - i, 0))

    dxc, dbcc, dv, gsb, gdl = call(
        functools.partial(last_kernel, heads, far),
        "last",
        grid,
        (g, xc, bcc, v, logs, sc, uc, dxd, dbc, q, dl, sg, ex, ext, *backs),
        [
            turned(block, inner), turned(block, inner), turned(block, shared), turned(block, LANES),
            turned(block, LANES), turned(2 * STATE, inner), turned(2 * STATE, inner), turned(block, inner),
            turned(block, shared), turned(block, LANES),
        ]
        + [whole_of(a) for a in (dl, sg, ex, ext, *backs)],
        [
            shape((rows, inner), f32), shape((rows, shared), f32), shape((rows, LANES), bf16),
            shape((1, LANES), f32), shape((1, LANES), f32),
        ],
        [turned(block, inner), turned(block, shared), turned(block, LANES), kept((1, LANES)), kept((1, LANES))],
        [pltpu.VMEM((STATE, inner), f32)],
        flops=2 * 10**9,
    )
    halo_x = along(dxc[:8], -1)
    halo_bc = along(dbcc[:8], -1)

    def next_rows(wide_by):
        return pl.BlockSpec((8, wide_by), lambda i: (jnp.minimum((i + 1) * (block // 8), rows // 8 - 1), 0))

    grad_rows, gcx, gcbc = call(
        conv_back_kernel,
        "conv_back",
        grid,
        (dxc, dbcc, dv, dxc, dbcc, halo_x, halo_bc, xr, bcr, cx, cbc),
        [
            rows_of(block, inner), rows_of(block, shared), rows_of(block, LANES), next_rows(inner), next_rows(shared),
            whole_of(halo_x), whole_of(halo_bc), rows_of(block, inner), rows_of(block, shared), whole_of(cx),
            whole_of(cbc),
        ],
        [shape((rows, inner + LANES + shared), bf16), shape((8, inner), f32), shape((8, shared), f32)],
        [rows_of(block, inner + LANES + shared), kept((8, inner)), kept((8, shared))],
        [pltpu.VMEM((block + 8, inner), f32), pltpu.VMEM((block + 8, shared), f32)],
        flops=10**8,
    )
    grad_first = dot_tn(nb, grad_rows).astype(bf16)
    grad_normed = dn + dot_nt(grad_rows, weights)
    h = hidden_in.astype(f32)
    scale = lax.rsqrt(jnp.mean(h * h, axis=1, keepdims=True) + epsilon)
    weighted = grad_normed * gain
    grad_norm = jnp.sum(grad_normed * h * scale, axis=0)
    grad_hidden = (
        cotangent.astype(f32)
        + weighted * scale
        - h * scale**3 * jnp.mean(weighted * h, axis=1, keepdims=True)
    ).astype(bf16)

    def sum_cores(parts):
        parts = [p.reshape(chips, 2, width // (2 * chips), -1) for p in parts]
        given = jnp.concatenate([lax.dynamic_index_in_dim(p, 1 - core, 1, False) for p in parts], axis=-1)
        held = jnp.concatenate([lax.dynamic_index_in_dim(p, core, 1, False) for p in parts], axis=-1)
        return (held.astype(f32) + other_core(given).astype(f32)).astype(bf16)

    def sum_chips(total):
        parts = [
            lax.dynamic_index_in_dim(total, (chip + k) % chips, 0, False) for k in range(chips)
        ]
        whole = parts[0].astype(f32)
        for k in range(1, chips):
            whole = whole + turn_chip(parts[k], k).astype(f32)
        return whole.astype(bf16)

    def sum_tensor(total, wide_by):
        parts = [
            lax.dynamic_slice_in_dim(total, (place + k) % tensor_size * wide_by, wide_by, 1)
            for k in range(tensor_size)
        ]
        whole = parts[0].astype(f32)
        for k in range(1, tensor_size):
            whole = whole + turn_tensor(parts[k], k).astype(f32)
        return whole

    def by_place(parts, total):
        split = [total[:, start : start + size * tensor_size].reshape(-1, tensor_size, size) for start, size in parts]
        return jnp.concatenate(split, axis=2).reshape(total.shape[0], -1)

    second_sum = sum_chips(sum_cores([grad_gate, grad_out]))
    second_sum = sum_tensor(by_place([(0, inner_local), (inner, inner_local)], second_sum), 2 * inner_local)
    first_sum = sum_chips(sum_cores([grad_first]))
    shared_rows = first_sum.shape[0] // tensor_size
    shared_sum = first_sum[:, inner + LANES :].reshape(tensor_size, shared_rows * shared)
    first_sum = by_place([(0, inner_local), (inner, heads_local)], first_sum)
    first_sum = sum_tensor(
        jnp.concatenate(
            [
                first_sum.reshape(-1, tensor_size, inner_local + heads_local),
                jnp.moveaxis(
                    shared_sum.reshape(tensor_size, first_sum.shape[0], -1), 0, 1
                ),
            ],
            axis=2,
        ).reshape(first_sum.shape[0], -1),
        inner_local + heads_local + shared // tensor_size,
    )
    grad_shared = first_sum[:, inner_local + heads_local :].reshape(shared_rows, shared)

    per_head = jnp.concatenate(
        [gsb[0, :heads], gdl[0, :heads], jnp.sum(gskip.reshape(heads, HEADDIM), axis=1)]
    )
    last_row = jnp.pad(jnp.concatenate([grad_norm, per_head]), (0, inner - width - 3 * heads))
    shared_row = jnp.pad(gcbc[:5].reshape(-1), (0, inner - 5 * shared))
    sums = jnp.concatenate([gcx[:5], ggg, shared_row[None], last_row[None]], axis=0)
    sums = sums + other_core(sums)
    sums = sums + sum(turn_chip(sums, k) for k in range(1, chips))
    sums = sums + sum(turn_tensor(sums, k) for k in range(1, tensor_size))
    grad_cx = lax.dynamic_slice_in_dim(sums[:6], place * inner_local, inner_local, axis=1)
    mine = width // (2 * chips * tensor_size)
    grad_norm = lax.dynamic_slice_in_dim(
        sums[7], (lax.axis_index("dp") * tensor_size + place) * mine, mine
    )

    def head_sum(index):
        return lax.dynamic_slice_in_dim(sums[7], width + index * heads + place * heads_local, heads_local)

    return (
        out,
        grad_hidden,
        grad_norm,
        second_sum[:, :inner_local],
        first_sum[:, :inner_local],
        first_sum[:, inner_local : inner_local + heads_local],
        grad_shared,
        second_sum[:, inner_local:],
        grad_cx[:5],
        sums[6, : 5 * shared].reshape(5, shared),
        head_sum(0),
        head_sum(1),
        head_sum(2),
        grad_cx[5],
    )


def solution(mesh):
    placed = (
        P(("dp", "tensor"), None), P(("dp", "tensor"), None), P("dp"), P("dp", "tensor"), P("dp", "tensor"),
        P("dp", "tensor"), P("dp", None), P("dp", "tensor"), P(None, "tensor"), P(), P("tensor"), P("tensor"),
        P("tensor"), P("tensor"),
    )
    results = (
        P(("dp", "tensor"), None), P(("dp", "tensor"), None), P(("dp", "tensor")), P("dp", "tensor"),
        P("dp", "tensor"), P("dp", "tensor"), P(("dp", "tensor"), None), P("dp", "tensor"), P(None, "tensor"),
        P(), P("tensor"), P("tensor"), P("tensor"), P("tensor"),
    )
    return jax.shard_map(per_device, mesh=mesh, in_specs=placed, out_specs=results, check_vma=False)
```

```python
import functools

import jax
import jax.numpy as jnp
from jax import lax
from jax.experimental import pallas as pl
from jax.experimental.pallas import tpu as pltpu
from jax.sharding import PartitionSpec as P

HEADDIM = 64
STATE = 128
SEQ_LEN = 4096
SPAN = 128
TILE = 64
LANES = 128
epsilon = 1e-05
bf16 = jnp.bfloat16
f32 = jnp.float32


def dot(a, b):
    return lax.dot_general(a, b, (((1,), (0,)), ((), ())), preferred_element_type=f32)


def dot_nt(a, b):
    return lax.dot_general(a, b, (((1,), (1,)), ((), ())), preferred_element_type=f32)


def dot_tn(a, b):
    return lax.dot_general(a, b, (((0,), (0,)), ((), ())), preferred_element_type=f32)


def exact_dot(a, b):
    return lax.dot_general(
        a, b, (((1,), (0,)), ((), ())), preferred_element_type=f32, precision=lax.Precision.HIGHEST
    )


def split_dot(values, matrix):
    high = values.astype(bf16)
    low = (values - high.astype(f32)).astype(bf16)
    return dot(high, matrix) + dot(low, matrix)


def sigmoid(v):
    return 0.5 + 0.5 * jnp.tanh(0.5 * v)


def small_sigmoid(v):
    return 1.0 / (1.0 + jnp.exp(-v))


def expand(values, matrix):
    high = values.astype(bf16).astype(f32)
    lane = lax.broadcasted_iota(jnp.int32, values.shape, 1)
    low = pltpu.roll(values - high, LANES // 2, 1)
    return dot(jnp.where(lane < LANES // 2, high, low).astype(bf16), matrix)


def expand_row(row, matrix):
    return expand(jnp.broadcast_to(row, (8, LANES)), matrix)[0:1]


def tiles(rows, lanes, body):
    def one(index, carry):
        at = pl.ds(pl.multiple_of(index * TILE, TILE), TILE)
        for block in range(lanes // LANES):
            body(at, slice(block * LANES, (block + 1) * LANES))
        return carry

    lax.fori_loop(0, rows // TILE, one, 0)


def add_rows(total, value):
    return total + jnp.sum(value.reshape(-1, 8, value.shape[1]), axis=0)


def softplus(v):
    u = jnp.exp(-jnp.abs(v))
    series = u * (1.0 - u * (0.5 - u * (1.0 / 3.0 - 0.25 * u)))
    return jnp.maximum(v, 0.0) + jnp.where(u < 0.01, series, jnp.log(1.0 + u))


def causal_mask(rows):
    at = lax.broadcasted_iota(jnp.int32, (rows, rows), 0)
    to = lax.broadcasted_iota(jnp.int32, (rows, rows), 1)
    return at >= to


def head_lanes(heads):
    return lax.broadcasted_iota(jnp.int32, (1, LANES), 1) < heads


def step_sizes(v, heads):
    return jnp.where(head_lanes(heads), softplus(v), 0.0)


def decay_rates(decay_log, heads):
    return jnp.where(head_lanes(heads), -jnp.exp(decay_log), 0.0)


def pair_stack(pair):
    lane = lax.broadcasted_iota(jnp.int32, pair.shape, 1)
    zero = jnp.zeros_like(pair)
    return jnp.concatenate(
        [jnp.where(lane < HEADDIM, pair, zero), jnp.where(lane >= HEADDIM, pair, zero)], axis=0
    )


def pair_decay(logs, logs_t, causal, pair):
    parts = []
    for head in (2 * pair, 2 * pair + 1):
        gap = logs[:, head : head + 1] - logs_t[head : head + 1, :]
        parts.append(jnp.exp(jnp.where(causal, gap, -1e30)))
    return parts


def first_kernel(
    heads,
    hid_ref, halo_ref, gain_ref, w_ref, cx_ref, cbc_ref, sb_ref, dl_ref, ex_ref,
    nb_ref, xr_ref, xc_ref, bcr_ref, bcc_ref, v_ref, logs_ref, lpre_ref, sloc_ref, fin_ref,
    xext, bext, state, total, tail, xt,
):
    rows = hid_ref.shape[0]
    inner = xr_ref.shape[1]
    gain = gain_ref[...]

    def norm(block):
        h = block.astype(f32)
        scale = lax.rsqrt(jnp.mean(h * h, axis=1, keepdims=True) + epsilon)
        return (h * scale * gain).astype(bf16)

    @pl.when(pl.program_id(0) == 0)
    def _():
        state[...] = jnp.zeros_like(state)
        total[...] = jnp.zeros_like(total)
        before = norm(halo_ref[...])
        xext[0:8, :] = dot(before, w_ref[:, :inner])[8:16]
        bext[0:8, :] = dot(before, w_ref[:, inner + LANES :])[8:16]

    @pl.when(pl.program_id(0) > 0)
    def _():
        xext[0:8, :] = xext[rows : rows + 8, :]
        bext[0:8, :] = bext[rows : rows + 8, :]

    nb = norm(hid_ref[...])
    nb_ref[...] = nb
    xr = dot(nb, w_ref[:, :inner])
    xext[8 : 8 + rows, :] = xr
    xr_ref[...] = xr.astype(bf16)
    bcr = dot(nb, w_ref[:, inner + LANES :])
    bext[8 : 8 + rows, :] = bcr
    bcr_ref[...] = bcr
    v = dot(nb, w_ref[:, inner : inner + LANES]) + sb_ref[...]
    v_ref[...] = v
    bcc = jnp.broadcast_to(cbc_ref[4:5, :], bcr.shape)
    for tap in range(4):
        bcc = bcc + cbc_ref[tap : tap + 1, :] * bext[5 + tap : 5 + tap + rows, :]
    bcc_ref[...] = bcc
    keys = (bcc[:, :STATE] * sigmoid(bcc[:, :STATE])).astype(bf16)
    dt = step_sizes(v, heads)
    la = dt * decay_rates(dl_ref[...], heads)
    ones = causal_mask(SPAN).astype(f32)
    ex = ex_ref[...]
    for at in range(rows // SPAN):
        span = slice(at * SPAN, (at + 1) * SPAN)
        logs = exact_dot(ones, la[span])
        logs_ref[span, :] = logs
        last = logs[SPAN - 1 : SPAN, :]
        lpre_ref[at * 8 : at * 8 + 8, :] = jnp.broadcast_to(total[0:1, :], (8, LANES))
        tail[...] = expand(jnp.exp(last - logs) * dt[span], ex)
        shrink = expand_row(jnp.exp(last), ex)
        for start in range(0, SPAN, TILE):
            here = slice(at * SPAN + start, at * SPAN + start + TILE)
            for block in range(inner // LANES):
                lanes = slice(block * LANES, (block + 1) * LANES)
                xc = cx_ref[4:5, lanes] + cx_ref[3:4, lanes] * xext[here.start + 8 : here.stop + 8, lanes]
                for tap in range(3):
                    moved = xext[here.start + 5 + tap : here.stop + 5 + tap, lanes]
                    xc = xc + cx_ref[tap : tap + 1, lanes] * moved
                xc = xc.astype(bf16)
                xc_ref[here, lanes] = xc
                xc = xc.astype(f32)
                xs = xc * sigmoid(xc)
                xt[start : start + TILE, lanes] = (xs * tail[start : start + TILE, lanes]).astype(bf16)
        for block in range(inner // (2 * LANES)):
            lanes = slice(block * 2 * LANES, (block + 1) * 2 * LANES)
            held = state[:, lanes]
            sloc_ref[at * STATE : (at + 1) * STATE, lanes] = held.astype(bf16)
            state[:, lanes] = held * shrink[:, lanes] + dot_tn(keys[span], xt[:, lanes])
        total[...] = total[...] + last

    @pl.when(pl.program_id(0) == pl.num_programs(0) - 1)
    def _():
        fin_ref[0:STATE, :] = state[...].astype(bf16)
        whole = expand(jnp.broadcast_to(jnp.exp(total[0:1, :]), (16, LANES)), ex)
        fin_ref[STATE : STATE + 16, :] = whole.astype(bf16)


def within_kernel(heads, xc_ref, bcc_ref, v_ref, logs_ref, ex_ref, yi_ref):
    causal = causal_mask(SPAN)
    for at in range(xc_ref.shape[0] // SPAN):
        span = slice(at * SPAN, (at + 1) * SPAN)
        xc = xc_ref[span, :].astype(f32)
        dt = step_sizes(v_ref[span, :], heads)
        xd = (xc * sigmoid(xc) * expand(dt, ex_ref[...])).astype(bf16)
        bcc = bcc_ref[span, :]
        bc = (bcc * sigmoid(bcc)).astype(bf16)
        scores = dot_nt(bc[:, STATE:], bc[:, :STATE])
        logs = logs_ref[span, :]
        logs_t = logs.T
        for pair in range(heads // 2):
            lanes = slice(pair * LANES, (pair + 1) * LANES)
            mixing = [(scores * d).astype(bf16) for d in pair_decay(logs, logs_t, causal, pair)]
            yi_ref[span, lanes] = dot(jnp.concatenate(mixing, axis=1), pair_stack(xd[:, lanes])).astype(bf16)


def incoming(refs):
    total = None
    for ref in reversed(refs):
        held = ref[0:STATE, :].astype(f32)
        if total is None:
            total = held
        else:
            total = held + ref[STATE : STATE + 1, :].astype(f32) * total
    return total


def middle_kernel(
    heads, far,
    hid_ref, cot_ref, z_ref, yi_ref, xc_ref, bcc_ref, logs_ref, lpre_ref, sloc_ref, wout_ref, gg_ref,
    skip_ref, ex_ref, fin_ref, *rest,
):
    fins = rest[:far]
    (out_ref, mixed_ref, dz_ref, g_ref, sc_ref, uc_ref, adj_ref, ggg_ref, gskip_ref) = rest[far : far + 9]
    (sin, acc, grown, ssm, gated, gm, ge) = rest[far + 9 :]

    @pl.when(pl.program_id(0) == 0)
    def _():
        sin[...] = incoming(fins) if far else jnp.zeros_like(sin)
        acc[...] = jnp.zeros_like(acc)
        ggg_ref[...] = jnp.zeros_like(ggg_ref)
        gskip_ref[...] = jnp.zeros_like(gskip_ref)

    ex = ex_ref[...]
    rows = hid_ref.shape[0]
    inner = z_ref.shape[1]
    count = inner // LANES
    skip = expand_row(skip_ref[...], ex)
    reads = bcc_ref[:, STATE:]
    reads = reads * sigmoid(reads)
    reads_t = [reads[k * SPAN : (k + 1) * SPAN].T.astype(bf16) for k in range(rows // SPAN)]
    reads = reads.astype(bf16)
    befores = []
    for at in range(rows // SPAN):
        span = slice(at * SPAN, (at + 1) * SPAN)
        states = slice(at * STATE, (at + 1) * STATE)
        before = expand_row(jnp.exp(lpre_ref[at * 8 : at * 8 + 1, :]), ex)
        befores.append(before)
        grown[span, :] = expand(jnp.exp(logs_ref[span, :]), ex)
        for block in range(inner // (2 * LANES)):
            lanes = slice(block * 2 * LANES, (block + 1) * 2 * LANES)
            held = (sloc_ref[states, lanes].astype(f32) + before[:, lanes] * sin[:, lanes]).astype(bf16)
            sc_ref[states, lanes] = held
            ssm[span, lanes] = dot(reads[span], held)
    gm[...] = dot(cot_ref[...], wout_ref[...])

    def forward(index, carry):
        at = slice(index * TILE, (index + 1) * TILE)
        squares = jnp.zeros((TILE, LANES), f32)
        for block in range(count):
            lanes = slice(block * LANES, (block + 1) * LANES)
            xc = xc_ref[at, lanes].astype(f32)
            value = yi_ref[at, lanes].astype(f32) + grown[at, lanes] * ssm[at, lanes] + skip[:, lanes] * (xc * sigmoid(xc))
            ssm[at, lanes] = value
            z = z_ref[at, lanes].astype(f32)
            value = value * (z * sigmoid(z))
            gated[at, lanes] = value
            squares = squares + value * value
        gs = lax.rsqrt(jnp.sum(squares, axis=1, keepdims=True) / inner + epsilon)
        cross = jnp.zeros((TILE, LANES), f32)
        for block in range(count):
            lanes = slice(block * LANES, (block + 1) * LANES)
            value = gated[at, lanes]
            scaled = value * gs
            mixed_ref[at, lanes] = (scaled * gg_ref[:, lanes]).astype(bf16)
            gradient = gm[at, lanes]
            ggg_ref[:, lanes] = add_rows(ggg_ref[:, lanes], gradient * scaled)
            weighted = gradient * gg_ref[:, lanes]
            gm[at, lanes] = weighted
            cross = cross + weighted * value
        mean = jnp.sum(cross, axis=1, keepdims=True) * (gs * gs * gs / inner)
        for block in range(count):
            lanes = slice(block * LANES, (block + 1) * LANES)
            dgated = gm[at, lanes] * gs - gated[at, lanes] * mean
            z = z_ref[at, lanes].astype(f32)
            sz = sigmoid(z)
            act = z * sz
            dz_ref[at, lanes] = (dgated * ssm[at, lanes] * (sz + act * (1.0 - sz))).astype(bf16)
            g = dgated * act
            g_ref[at, lanes] = g.astype(bf16)
            xc = xc_ref[at, lanes].astype(f32)
            gskip_ref[:, lanes] = add_rows(gskip_ref[:, lanes], g * (xc * sigmoid(xc)))
            ge[at, lanes] = (g * grown[at, lanes]).astype(bf16)
        return carry

    for index in range(rows // TILE):
        forward(index, 0)
    out_ref[...] = (hid_ref[...].astype(f32) + dot_nt(mixed_ref[...], wout_ref[...])).astype(bf16)
    for at in range(rows // SPAN):
        span = slice(at * SPAN, (at + 1) * SPAN)
        for block in range(inner // (2 * LANES)):
            lanes = slice(block * 2 * LANES, (block + 1) * 2 * LANES)
            u = dot(reads_t[at], ge[span, lanes])
            uc_ref[at * STATE : (at + 1) * STATE, lanes] = u.astype(bf16)
            acc[:, lanes] += befores[at][:, lanes] * u

    @pl.when(pl.program_id(0) == pl.num_programs(0) - 1)
    def _():
        adj_ref[0:STATE, :] = acc[...].astype(bf16)
        adj_ref[STATE:, :] = fin_ref[...]


def back_within_kernel(
    heads,
    g_ref, xc_ref, bcc_ref, v_ref, logs_ref, sc_ref, ex_ref, ext_ref,
    dxd_ref, dbc_ref, q_ref, grown, carried, ge,
):
    causal = causal_mask(SPAN)
    for at in range(xc_ref.shape[0] // SPAN):
        span = slice(at * SPAN, (at + 1) * SPAN)
        xc = xc_ref[span, :].astype(f32)
        dt = step_sizes(v_ref[span, :], heads)
        xd = (xc * sigmoid(xc) * expand(dt, ex_ref[...])).astype(bf16)
        bcc = bcc_ref[span, :]
        bc = (bcc * sigmoid(bcc)).astype(bf16)
        keys, reads = bc[:, :STATE], bc[:, STATE:]
        scores = dot_nt(reads, keys)
        logs = logs_ref[span, :]
        logs_t = logs.T
        states = slice(at * STATE, (at + 1) * STATE)
        held = sc_ref[states, :]
        grown[...] = expand(jnp.exp(logs), ex_ref[...])
        carried[...] = dot(reads, held)
        dscores = jnp.zeros((SPAN, SPAN), f32)
        lane = lax.broadcasted_iota(jnp.int32, (SPAN, LANES), 1)
        for pair in range(heads // 2):
            lanes = slice(pair * LANES, (pair + 1) * LANES)
            decays = pair_decay(logs, logs_t, causal, pair)
            mixing = jnp.concatenate([(scores * d).astype(bf16) for d in decays], axis=1)
            gp = g_ref[span, lanes]
            xp = xd[:, lanes]
            stack = pair_stack(xp)
            dmix = dot_nt(gp, stack)
            dscores = dscores + dmix[:, :SPAN] * decays[0] + dmix[:, SPAN:] * decays[1]
            both = dot_tn(mixing, gp)
            dxd = jnp.where(lane < HEADDIM, both[:SPAN], both[SPAN:])
            dxd_ref[span, lanes] = dxd.astype(bf16)
            gf = gp.astype(f32)
            scaled = gf * grown[:, lanes]
            ge[:, lanes] = scaled.astype(bf16)
            carried[:, lanes] = gf * dot(mixing, stack) - xp.astype(f32) * dxd + scaled * carried[:, lanes]
        dscores = dscores.astype(bf16)
        dbc_ref[span, :STATE] = dot_tn(dscores, reads)
        dbc_ref[span, STATE:] = dot(dscores, keys) + dot_nt(ge[...], held)
        q_ref[span, :] = split_dot(carried[...], ext_ref[...])


def last_kernel(
    heads, far,
    g_ref, xc_ref, bcc_ref, v_ref, logs_ref, sc_ref, uc_ref, dxd_ref, dbc_ref, q_ref, xr_ref, bcr_ref,
    dl_ref, skip_ref, ex_ref, ext_ref, cx_ref, cbc_ref, *rest,
):
    adjs = rest[:far]
    (grad_ref, gsb_ref, gdl_ref, gcx_ref, gcbc_ref, edge_ref) = rest[far : far + 6]
    (adj, tail, dte, dxu, xt, p3, p4, xext, bext) = rest[far + 6 :]
    inner = xc_ref.shape[1]

    @pl.when(pl.program_id(0) == 0)
    def _():
        adj[...] = incoming(adjs) if far else jnp.zeros_like(adj)
        gsb_ref[...] = jnp.zeros_like(gsb_ref)
        gdl_ref[...] = jnp.zeros_like(gdl_ref)
        gcx_ref[...] = jnp.zeros_like(gcx_ref)
        gcbc_ref[...] = jnp.zeros_like(gcbc_ref)
        xext[SPAN:, :] = jnp.zeros((8, inner), f32)
        bext[SPAN:, :] = jnp.zeros((8, bext.shape[1]), f32)

    ex = ex_ref[...]
    ext = ext_ref[...]
    causal = causal_mask(SPAN)
    not_after = causal.astype(f32)
    strictly = not_after - jnp.logical_and(causal, causal.T).astype(f32)
    upper = 1.0 - strictly
    rates = decay_rates(dl_ref[...], heads)
    skip = expand_row(skip_ref[...], ex)
    for at in reversed(range(xc_ref.shape[0] // SPAN)):
        span = slice(at * SPAN, (at + 1) * SPAN)
        states = slice(at * STATE, (at + 1) * STATE)
        v = v_ref[span, :]
        dt = step_sizes(v, heads)
        bcc = bcc_ref[span, :]
        sbc = sigmoid(bcc)
        keys = (bcc * sbc)[:, :STATE].astype(bf16)
        logs = logs_ref[span, :]
        last = logs[SPAN - 1 : SPAN, :]
        shrink = expand_row(jnp.exp(last), ex)
        tail[...] = expand(jnp.exp(last - logs), ex)
        dte[...] = expand(dt, ex)
        held_low = adj[...].astype(bf16)
        dxu[...] = dot(keys, held_low)
        for start in range(0, SPAN, TILE):
            here = slice(start, start + TILE)
            there = slice(at * SPAN + start, at * SPAN + start + TILE)
            for block in range(inner // LANES):
                lanes = slice(block * LANES, (block + 1) * LANES)
                xc = xc_ref[there, lanes].astype(f32)
                sx = sigmoid(xc)
                xs = xc * sx
                tails = tail[here, lanes]
                update = tails * dxu[here, lanes]
                xd = xs * dte[here, lanes]
                xt[here, lanes] = (xd * tails).astype(bf16)
                p3[here, lanes] = (xd * update).astype(bf16)
                dxd = dxd_ref[there, lanes].astype(f32) + update
                p4[here, lanes] = (xs * dxd).astype(bf16)
                dxs = dte[here, lanes] * dxd + skip[:, lanes] * g_ref[there, lanes].astype(f32)
                xext[here, lanes] = dxs * (sx + xs * (1.0 - sx))
        inners = []
        for block in range(inner // LANES):
            lanes = slice(block * LANES, (block + 1) * LANES)
            held = adj[:, lanes]
            inners.append(jnp.sum(held * sc_ref[states, lanes].astype(f32), axis=0, keepdims=True))
            adj[:, lanes] = held * shrink[:, lanes] + uc_ref[states, lanes].astype(f32)
        within = jnp.concatenate(inners, axis=1) * shrink
        within = split_dot(jnp.broadcast_to(within, (8, inner)), ext)[0:1]
        dkeys = dbc_ref[span, :STATE] + dot_nt(xt[...], held_low)
        dbc = jnp.concatenate([dkeys, dbc_ref[span, STATE:]], axis=1)
        bext[0:SPAN, :] = dbc * (sbc + bcc * sbc * (1.0 - sbc))
        dla = exact_dot(upper, q_ref[span, :]) + exact_dot(strictly, dot(p3[...], ext)) + within
        ddt = rates * dla + dot(p4[...], ext)
        dv = jnp.where(head_lanes(heads), ddt * small_sigmoid(v), 0.0)
        grad_ref[span, inner : inner + LANES] = dv.astype(bf16)
        gsb_ref[...] += jnp.sum(dv, axis=0, keepdims=True)
        gdl_ref[...] += jnp.sum(dt * dla, axis=0, keepdims=True) * rates
        for moved_ref, rows_ref, taps, first, sums in (
            (xext, xr_ref, cx_ref, 0, gcx_ref),
            (bext, bcr_ref, cbc_ref, inner + LANES, gcbc_ref),
        ):
            for block in range(moved_ref.shape[1] // LANES):
                lanes = slice(block * LANES, (block + 1) * LANES)
                parts = [jnp.zeros((8, LANES), f32)] * 5
                for start in range(0, SPAN, TILE):
                    there = slice(at * SPAN + start, at * SPAN + start + TILE)
                    before = rows_ref[there, lanes].astype(f32)
                    total = None
                    for tap in range(4):
                        moved = moved_ref[start + 3 - tap : start + 3 - tap + TILE, lanes]
                        term = taps[tap : tap + 1, lanes] * moved
                        total = term if total is None else total + term
                        parts[tap] = add_rows(parts[tap], before * moved)
                    parts[4] = add_rows(parts[4], moved)
                    grad_ref[there, first + lanes.start : first + lanes.stop] = total.astype(bf16)
                for tap in range(5):
                    sums[tap * 8 : tap * 8 + 8, lanes] += parts[tap]
            moved_ref[SPAN:, :] = moved_ref[0:8, :]

    edge_ref[:, :inner] = xext[0:8, :]
    edge_ref[:, inner:] = bext[0:8, :]


def mend_kernel(
    edge_ref, rows_ref, bcr_ref, xr_ref, cx_ref, cbc_ref, gcx_ref, gcbc_ref, ggg_ref, gskip_ref, gsb_ref, gdl_ref,
    ext_ref, grad_ref, sums_ref,
):
    inner = xr_ref.shape[1]
    shared = bcr_ref.shape[1]
    row = lax.broadcasted_iota(jnp.int32, (8, 1), 0)
    sums_ref[...] = jnp.zeros_like(sums_ref)
    grad_ref[...] = rows_ref[...]
    for before, taps, start, first, top, old in (
        (xr_ref, cx_ref, 0, 0, 0, gcx_ref),
        (bcr_ref, cbc_ref, inner, inner + LANES, 6, gcbc_ref),
    ):
        wide_by = before.shape[1]
        late = before[8:16, :].astype(f32)
        total = jnp.zeros((8, wide_by), f32)
        for tap in range(5):
            value = old[tap * 8 : tap * 8 + 8, :]
            if tap < 3:
                moved = pltpu.roll(edge_ref[:, start : start + wide_by], 5 + tap, 0)
                moved = jnp.where(row >= 5 + tap, moved, 0.0)
                total = total + taps[tap : tap + 1, :] * moved
                value = value + late * moved
            sums_ref[top + tap : top + tap + 1, :wide_by] = jnp.sum(value, axis=0, keepdims=True)
        there = slice(first, first + wide_by)
        fixed = rows_ref[8:16, there].astype(f32) + total
        grad_ref[:, there] = jnp.concatenate([rows_ref[0:8, there].astype(f32), fixed], axis=0).astype(bf16)
    sums_ref[5:6, :] = jnp.sum(ggg_ref[...], axis=0, keepdims=True)
    skip = split_dot(gskip_ref[...], ext_ref[...])
    lanes = slice(shared, shared + LANES)
    sums_ref[6:7, lanes] = gsb_ref[...]
    sums_ref[7:8, lanes] = gdl_ref[...]
    sums_ref[8:9, lanes] = jnp.sum(skip, axis=0, keepdims=True)


def call(kernel, name, grid, ins, in_specs, outs, out_specs, scratch, limit=56):
    return pl.pallas_call(
        kernel,
        grid=grid,
        in_specs=in_specs,
        out_specs=out_specs,
        out_shape=outs,
        scratch_shapes=scratch,
        name=name,
        compiler_params=pltpu.CompilerParams(vmem_limit_bytes=limit * 2**20),
        cost_estimate=pl.CostEstimate(flops=10**7, bytes_accessed=10**5, transcendentals=0),
    )(*ins)


def rows_of(block, width):
    return pl.BlockSpec((block, width), lambda i: (i, 0))


def whole_of(array):
    return pl.BlockSpec(array.shape, lambda i: (0, 0), pipeline_mode=pl.Buffered(1))


def kept(shape):
    return pl.BlockSpec(shape, lambda i: (0, 0))


def shape(dims, kind):
    return jax.ShapeDtypeStruct(dims, kind)


def pad_rows(array, count):
    return jnp.pad(array, ((0, count - array.shape[0]), (0, 0)))


def pad_lanes(array):
    return jnp.pad(array, ((0, 0), (0, LANES - array.shape[1])))


def per_device(
    hidden_in, cotangent, norm_gain, gate_proj, input_proj, step_proj, shared_proj, output_proj,
    conv_inner, conv_shared, step_bias, decay_log, skip_gain, gated_gain,
):
    tensor_size = lax.axis_size("tensor")
    chips = lax.axis_size("dp") // 2
    place = lax.axis_index("tensor")
    core = lax.axis_index("dp") % 2
    chip = lax.axis_index("dp") // 2
    rows, width = hidden_in.shape
    heads_local = step_proj.shape[1]
    width_local = input_proj.shape[0]
    inner_local = gate_proj.shape[1]
    heads = heads_local * tensor_size
    inner = inner_local * tensor_size
    shared = shared_proj.shape[1]
    per_sequence = SEQ_LEN // rows
    far = per_sequence - 1

    def along(value, step):
        pairs = []
        for start in range(tensor_size):
            end = start + step
            if 0 <= end < tensor_size and start // per_sequence == end // per_sequence:
                pairs.append((start, end))
        return lax.ppermute(value, "tensor", pairs)

    def turn_tensor(value, step):
        return lax.ppermute(value, "tensor", [(i, (i + step) % tensor_size) for i in range(tensor_size)])

    def turn_chip(value, step):
        pairs = [(i, (i // 2 + step) % chips * 2 + i % 2) for i in range(2 * chips)]
        return lax.ppermute(value, "dp", pairs)

    def other_core(value):
        return lax.ppermute(value, "dp", [(i, i ^ 1) for i in range(2 * chips)])

    def in_order(turned, at):
        count = len(turned)
        return [lax.select_n((at - s) % count, *turned) for s in range(count)]

    def to_tensor(value):
        return [value] + [turn_tensor(value, k) for k in range(1, tensor_size)]

    def to_chips(value):
        return [value] + [turn_chip(value, k) for k in range(1, chips)]

    def by_core(value, other):
        first = core == 0
        both = jnp.stack([jnp.where(first, value, other), jnp.where(first, other, value)], axis=1)
        return both.reshape(-1, value.shape[-1])

    def core_rows(value):
        turned = value.T.reshape(chips, 2, -1, rows)
        return [
            lax.dynamic_index_in_dim(turned, which, 1, False).reshape(-1, rows) for which in (core, 1 - core)
        ]

    def join(first, *others):
        total = first.astype(f32)
        for other in others:
            total = total + other.astype(f32)
        return total.astype(first.dtype)

    def sum_chips_start(total):
        total = total.reshape(chips, -1, total.shape[-1])
        parts = [lax.dynamic_index_in_dim(total, (chip + k) % chips, 0, False) for k in range(chips)]
        return parts[0], [turn_chip(parts[k], k) for k in range(1, chips)]

    def sum_tensor_start(total, wide_by):
        parts = [
            lax.dynamic_slice_in_dim(total, (place + k) % tensor_size * wide_by, wide_by, 1)
            for k in range(tensor_size)
        ]
        return parts[0], [turn_tensor(parts[k], k) for k in range(1, tensor_size)]

    def by_place(parts):
        split = [p.reshape(p.shape[0], tensor_size, -1) for p in parts]
        return jnp.concatenate(split, axis=2).reshape(parts[0].shape[0], -1)

    tie = lax.optimization_barrier

    small = jnp.concatenate(
        [
            conv_inner,
            gated_gain[None],
            jnp.pad(
                jnp.concatenate([step_bias, decay_log, skip_gain]), (0, inner_local - 3 * heads_local)
            )[None],
            jnp.zeros((1, inner_local), f32),
        ],
        axis=0,
    )
    high = tie(small.astype(bf16))
    low = (small - high.astype(f32)).astype(bf16)
    send = jnp.concatenate([input_proj, high, low], axis=0)
    send = jnp.concatenate([send, jnp.pad(step_proj, ((0, 16), (0, LANES - heads_local)))], axis=1)
    ends = hidden_in[rows - 16 :].reshape(-1)
    ends = jnp.pad(ends, (0, -ends.size % (16 * send.shape[1]))).reshape(-1, send.shape[1])
    given = jnp.concatenate([send, ends], axis=0)
    after = turn_tensor(given, 1)
    first_part = [send, after[: send.shape[0]]] + [turn_tensor(send, k) for k in range(2, tensor_size)]
    halo = after[send.shape[0] :].reshape(-1)[: 16 * width].reshape(16, width)
    halo = jnp.where(place % per_sequence == 0, jnp.zeros_like(halo), halo)
    first_part, second_part = tie((first_part, jnp.concatenate([gate_proj, output_proj], axis=1)))
    first_part = in_order(first_part, place)
    small = [
        p[width_local : width_local + 8, :inner_local].astype(f32) + p[width_local + 8 :, :inner_local].astype(f32)
        for p in first_part
    ]
    first_part = [p[:width_local] for p in first_part]
    steps_part = jnp.concatenate([p[:, inner_local : inner_local + heads_local] for p in first_part], axis=1)
    first_part = jnp.concatenate(
        [p[:, :inner_local] for p in first_part]
        + [pad_lanes(jnp.concatenate([steps_part, norm_gain[:, None]], axis=1)), shared_proj],
        axis=1,
    )
    first_part, second_part = tie((to_chips(first_part), to_tensor(second_part)))
    first_part = jnp.stack(in_order(first_part, chip))
    weights = by_core(first_part, other_core(first_part))
    second_part = in_order(second_part, place)
    second_part = jnp.concatenate(
        [p[:, :inner_local] for p in second_part] + [p[:, inner_local:] for p in second_part], axis=1
    )
    second_part = to_chips(second_part)
    gain = weights[:, inner + heads].astype(f32)[None]

    wide = jnp.concatenate(small, axis=1)
    cx = pad_rows(wide[:5], 8)
    gg = wide[5:6]
    cbc = pad_rows(conv_shared, 8)

    def head_row(index):
        at = slice(index * heads_local, (index + 1) * heads_local)
        return pad_lanes(jnp.concatenate([p[6:7, at] for p in small], axis=1))

    sb, dl, sg = head_row(0), head_row(1), head_row(2)
    wide_head = lax.broadcasted_iota(jnp.int32, (LANES, inner), 1) // HEADDIM
    ex = (lax.broadcasted_iota(jnp.int32, (LANES, inner), 0) % (LANES // 2) == wide_head).astype(bf16)
    tall_head = lax.broadcasted_iota(jnp.int32, (inner, LANES), 0) // HEADDIM
    ext = (lax.broadcasted_iota(jnp.int32, (inner, LANES), 1) == tall_head).astype(bf16)

    block = 2 * SPAN
    steps = rows // block
    chunks = rows // SPAN
    grid = (steps,)
    nb, xr, xc, bcr, bcc, v, logs, lpre, sloc, fin = call(
        functools.partial(first_kernel, heads),
        "first",
        grid,
        (hidden_in, halo, gain, weights, cx, cbc, sb, dl, ex),
        [rows_of(block, width)] + [whole_of(a) for a in (halo, gain, weights, cx, cbc, sb, dl, ex)],
        [
            shape((rows, width), bf16), shape((rows, inner), bf16), shape((rows, inner), bf16),
            shape((rows, shared), f32), shape((rows, shared), f32), shape((rows, LANES), f32),
            shape((rows, LANES), f32), shape((chunks * 8, LANES), f32),
            shape((chunks * STATE, inner), bf16), shape((STATE + 16, inner), bf16),
        ],
        [
            rows_of(block, width), rows_of(block, inner), rows_of(block, inner),
            rows_of(block, shared), rows_of(block, shared), rows_of(block, LANES),
            rows_of(block, LANES), rows_of(16, LANES),
            rows_of(2 * STATE, inner), kept((STATE + 16, inner)),
        ],
        [
            pltpu.VMEM((block + 8, inner), f32), pltpu.VMEM((block + 8, shared), f32),
            pltpu.VMEM((STATE, inner), f32), pltpu.VMEM((8, LANES), f32),
            pltpu.VMEM((SPAN, inner), f32), pltpu.VMEM((SPAN, inner), bf16),
        ],
    )
    second_part, fin = tie((second_part, fin))
    nb_own, nb_given = core_rows(nb)
    cot_own, cot_given = core_rows(cotangent)
    fins = [along(fin, step) for step in range(1, far + 1)]
    second_part = jnp.stack(in_order(second_part, chip))
    second_other = other_core(second_part)
    (yi,) = call(
        functools.partial(within_kernel, heads),
        "within",
        grid,
        (xc, bcc, v, logs, ex),
        [rows_of(block, inner), rows_of(block, shared), rows_of(block, LANES), rows_of(block, LANES), whole_of(ex)],
        [shape((rows, inner), bf16)],
        [rows_of(block, inner)],
        [],
    )
    second_other, yi = tie((second_other, yi))
    second_part = by_core(second_part, second_other)
    wz, wout = second_part[:, :inner], second_part[:, inner:]
    z = dot(nb, wz).astype(bf16)
    state_rows = rows_of(2 * STATE, inner)
    out, mixed, dz, g, sc, uc, adj, ggg, gskip = call(
        functools.partial(middle_kernel, heads, far),
        "middle",
        grid,
        (hidden_in, cotangent, z, yi, xc, bcc, logs, lpre, sloc, wout, gg, sg, ex, fin, *fins),
        [
            rows_of(block, width), rows_of(block, width), rows_of(block, inner), rows_of(block, inner),
            rows_of(block, inner), rows_of(block, shared), rows_of(block, LANES), rows_of(16, LANES), state_rows,
        ]
        + [whole_of(a) for a in (wout, gg, sg, ex)]
        + [pl.BlockSpec((16, inner), lambda i: (STATE // 16, 0))]
        + [whole_of(a) for a in fins],
        [
            shape((rows, width), bf16), shape((rows, inner), bf16), shape((rows, inner), bf16),
            shape((rows, inner), bf16), shape((chunks * STATE, inner), bf16), shape((chunks * STATE, inner), bf16),
            shape((STATE + 16, inner), bf16), shape((8, inner), f32), shape((8, inner), f32),
        ],
        [
            rows_of(block, width), rows_of(block, inner), rows_of(block, inner), rows_of(block, inner),
            state_rows, state_rows, kept((STATE + 16, inner)), kept((8, inner)), kept((8, inner)),
        ],
        [pltpu.VMEM((STATE, inner), f32)] * 2 + [pltpu.VMEM((block, inner), f32)] * 4 + [pltpu.VMEM((block, inner), bf16)],
    )
    backs = [along(adj, -step) for step in range(1, far + 1)]
    taken = [other_core(dot(nb_given, dz).astype(bf16)), other_core(dot(cot_given, mixed).astype(bf16))]
    held = [dot(nb_own, dz), dot(cot_own, mixed)]
    dn = dot_nt(dz, wz)
    dxd, dbc, q = call(
        functools.partial(back_within_kernel, heads),
        "back_within",
        grid,
        (g, xc, bcc, v, logs, sc, ex, ext),
        [
            rows_of(block, inner), rows_of(block, inner), rows_of(block, shared), rows_of(block, LANES),
            rows_of(block, LANES), state_rows, whole_of(ex), whole_of(ext),
        ],
        [shape((rows, inner), bf16), shape((rows, shared), f32), shape((rows, LANES), f32)],
        [rows_of(block, inner), rows_of(block, shared), rows_of(block, LANES)],
        [pltpu.VMEM((SPAN, inner), f32), pltpu.VMEM((SPAN, inner), f32), pltpu.VMEM((SPAN, inner), bf16)],
    )

    backs, taken, held, dxd, dn = tie((backs, taken, held, dxd, dn))
    second_parts, second_taken = sum_chips_start(
        jnp.concatenate([join(own, other).astype(bf16) for own, other in zip(held, taken)], axis=1)
    )

    def turned(size, wide_by):
        return pl.BlockSpec((size, wide_by), lambda i: (steps - 1 - i, 0))

    wide_rows = inner + LANES + shared
    grad_rows, gsb, gdl, gcx, gcbc, edge = call(
        functools.partial(last_kernel, heads, far),
        "last",
        grid,
        (g, xc, bcc, v, logs, sc, uc, dxd, dbc, q, xr, bcr, dl, sg, ex, ext, cx, cbc, *backs),
        [
            turned(block, inner), turned(block, inner), turned(block, shared), turned(block, LANES),
            turned(block, LANES), turned(2 * STATE, inner), turned(2 * STATE, inner), turned(block, inner),
            turned(block, shared), turned(block, LANES), turned(block, inner), turned(block, shared),
        ]
        + [whole_of(a) for a in (dl, sg, ex, ext, cx, cbc, *backs)],
        [
            shape((rows, wide_rows), bf16), shape((1, LANES), f32), shape((1, LANES), f32),
            shape((40, inner), f32), shape((40, shared), f32), shape((8, inner + shared), f32),
        ],
        [
            turned(block, wide_rows), kept((1, LANES)), kept((1, LANES)), kept((40, inner)), kept((40, shared)),
            kept((8, inner + shared)),
        ],
        [pltpu.VMEM((STATE, inner), f32)]
        + [pltpu.VMEM((SPAN, inner), f32)] * 3
        + [pltpu.VMEM((SPAN, inner), bf16)] * 3
        + [pltpu.VMEM((SPAN + 8, inner), f32), pltpu.VMEM((SPAN + 8, shared), f32)],
    )
    edge = along(edge, -1)
    edge, second_taken = tie((edge, second_taken))
    second_sum = join(second_parts, *second_taken)
    second_kept, second_last = sum_tensor_start(
        by_place([second_sum[:, :inner], second_sum[:, inner:]]), 2 * inner_local
    )
    ending = rows // 16 - 1

    def end_rows(wide_by):
        return pl.BlockSpec((16, wide_by), lambda i: (ending, 0))

    sums_in = (cx, cbc, gcx, gcbc, ggg, gskip, gsb, gdl, ext)
    grad_rows, sums = pl.pallas_call(
        mend_kernel,
        grid=(1,),
        in_specs=[kept(edge.shape), end_rows(wide_rows), end_rows(shared), end_rows(inner)]
        + [kept(a.shape) for a in sums_in],
        out_specs=[end_rows(wide_rows), kept((16, inner))],
        out_shape=[shape(grad_rows.shape, bf16), shape((16, inner), f32)],
        input_output_aliases={1: 0},
        name="mend",
    )(edge, grad_rows, bcr, xr, *sums_in)
    given = dot(nb_given, grad_rows).astype(bf16)
    taken = other_core(given)
    sums_taken = other_core(sums)
    given, grad_rows = tie((given, grad_rows))
    held = dot(nb_own, grad_rows)
    grad_normed = dn + dot_nt(grad_rows, weights)
    taken, sums_taken, held, grad_normed = tie((taken, sums_taken, held, grad_normed))
    first_kept, first_taken = sum_chips_start(join(held, taken).astype(bf16))
    sums = sums + sums_taken
    sums_taken = [turn_chip(sums, k) for k in range(1, chips)]
    h = hidden_in.astype(f32)
    scale = lax.rsqrt(jnp.mean(h * h, axis=1, keepdims=True) + epsilon)
    weighted = grad_normed * gain
    grad_norm = jnp.sum(grad_normed * h * scale, axis=0, keepdims=True)
    grad_hidden = (
        cotangent.astype(f32)
        + weighted * scale
        - h * scale**3 * jnp.mean(weighted * h, axis=1, keepdims=True)
    ).astype(bf16)
    norm_taken = [
        lax.ppermute(grad_norm, "dp", [(i, (i + k) % (2 * chips)) for i in range(2 * chips)])
        for k in range(1, 2 * chips)
    ]
    first_taken, sums_taken, norm_taken, grad_hidden = tie((first_taken, sums_taken, norm_taken, grad_hidden))
    first_sum = join(first_kept, *first_taken)
    shared_sum = first_sum[:, inner + LANES :].reshape(tensor_size, -1, shared)
    first_sum = by_place(
        [
            first_sum[:, :inner],
            first_sum[:, inner : inner + heads],
            jnp.moveaxis(shared_sum.reshape(tensor_size, first_sum.shape[0], -1), 0, 1).reshape(
                first_sum.shape[0], -1
            ),
        ]
    )
    first_kept, first_taken = sum_tensor_start(first_sum, inner_local + heads_local + shared // tensor_size)
    sums = join(sums, *sums_taken)
    sums = jnp.concatenate([sums, jnp.pad(join(grad_norm, *norm_taken), ((0, 7), (0, inner - width)))], axis=0)
    sums = join(sums, *[turn_tensor(sums, k) for k in range(1, tensor_size)])
    first_sum = join(first_kept.astype(f32), *first_taken)
    second_sum = join(second_kept.astype(f32), *second_last)
    grad_shared = first_sum[:, inner_local + heads_local :].reshape(-1, shared)
    grad_cx = lax.dynamic_slice_in_dim(sums[:6], place * inner_local, inner_local, axis=1)
    mine = width // (2 * chips * tensor_size)
    grad_norm = lax.dynamic_slice_in_dim(
        sums[16], (lax.axis_index("dp") * tensor_size + place) * mine, mine
    )

    def head_sum(index):
        return lax.dynamic_slice_in_dim(sums[6 + index], shared + place * heads_local, heads_local)

    return (
        out,
        grad_hidden,
        grad_norm,
        second_sum[:, :inner_local],
        first_sum[:, :inner_local],
        first_sum[:, inner_local : inner_local + heads_local],
        grad_shared,
        second_sum[:, inner_local:],
        grad_cx[:5],
        sums[6:11, :shared],
        head_sum(0),
        head_sum(1),
        head_sum(2),
        grad_cx[5],
    )


def solution(mesh):
    placed = (
        P(("dp", "tensor"), None), P(("dp", "tensor"), None), P("dp"), P("dp", "tensor"), P("dp", "tensor"),
        P("dp", "tensor"), P("dp", None), P("dp", "tensor"), P(None, "tensor"), P(), P("tensor"), P("tensor"),
        P("tensor"), P("tensor"),
    )
    results = (
        P(("dp", "tensor"), None), P(("dp", "tensor"), None), P(("dp", "tensor")), P("dp", "tensor"),
        P("dp", "tensor"), P("dp", "tensor"), P(("dp", "tensor"), None), P("dp", "tensor"), P(None, "tensor"),
        P(), P("tensor"), P("tensor"), P("tensor"), P("tensor"),
    )
    return jax.shard_map(per_device, mesh=mesh, in_specs=placed, out_specs=results, check_vma=False)
```

```python
import functools

import jax
import jax.numpy as jnp
from jax import lax
from jax.experimental import pallas as pl
from jax.experimental.pallas import tpu as pltpu
from jax.sharding import PartitionSpec as P

HEADDIM = 64
STATE = 128
SEQ_LEN = 4096
SPAN = 128
TILE = 64
BLOCK = 2
LANES = 128
epsilon = 1e-05
bf16 = jnp.bfloat16
f32 = jnp.float32


def dot(a, b):
    return lax.dot_general(a, b, (((1,), (0,)), ((), ())), preferred_element_type=f32)


def dot_nt(a, b):
    return lax.dot_general(a, b, (((1,), (1,)), ((), ())), preferred_element_type=f32)


def dot_tn(a, b):
    return lax.dot_general(a, b, (((0,), (0,)), ((), ())), preferred_element_type=f32)


def exact_dot(a, b):
    return lax.dot_general(
        a, b, (((1,), (0,)), ((), ())), preferred_element_type=f32, precision=lax.Precision.HIGHEST
    )


def split_dot(values, matrix):
    high = values.astype(bf16)
    low = (values - high.astype(f32)).astype(bf16)
    return dot(high, matrix) + dot(low, matrix)


def sigmoid(v):
    return 0.5 + 0.5 * jnp.tanh(0.5 * v)


def small_sigmoid(v):
    return 1.0 / (1.0 + jnp.exp(-v))


def expand(values, matrix):
    high = values.astype(bf16).astype(f32)
    lane = lax.broadcasted_iota(jnp.int32, values.shape, 1)
    low = pltpu.roll(values - high, LANES // 2, 1)
    return dot(jnp.where(lane < LANES // 2, high, low).astype(bf16), matrix)


def expand_row(row, matrix):
    return expand(jnp.broadcast_to(row, (8, LANES)), matrix)[0:1]


def span_sum(matrix, values):
    high = values.astype(bf16).astype(f32)
    rest = values - high
    middle = rest.astype(bf16).astype(f32)
    lane = lax.broadcasted_iota(jnp.int32, values.shape, 1)
    packed = jnp.where(
        lane < 32,
        high,
        jnp.where(lane < 64, pltpu.roll(middle, 32, 1), jnp.where(lane < 96, pltpu.roll(rest - middle, 64, 1), 0.0)),
    )
    total = dot(matrix, packed.astype(bf16))
    total = total + pltpu.roll(total, LANES - 32, 1) + pltpu.roll(total, LANES - 64, 1)
    return jnp.where(lane < 32, total, 0.0)


def in_span(rows):
    at = lax.broadcasted_iota(jnp.int32, (rows, rows), 0)
    to = lax.broadcasted_iota(jnp.int32, (rows, rows), 1)
    return at // SPAN == to // SPAN, at, to


def last_rows(logs):
    return [logs[start + SPAN - 1 : start + SPAN, :] for start in range(0, logs.shape[0], SPAN)]


def stacked(row_list):
    row = lax.broadcasted_iota(jnp.int32, (8, LANES), 0)
    total = jnp.broadcast_to(row_list[0], (8, LANES))
    for index, value in enumerate(row_list[1:]):
        total = jnp.where(row > index, value, total)
    return total


def span_gaps(logs):
    spans = range(0, logs.shape[0], SPAN)
    return jnp.concatenate([last - logs[start : start + SPAN] for last, start in zip(last_rows(logs), spans)], axis=0)


def add_rows(total, value):
    return total + jnp.sum(value.reshape(-1, 8, value.shape[1]), axis=0)


def softplus(v):
    u = jnp.exp(-jnp.abs(v))
    series = u * (1.0 - u * (0.5 - u * (1.0 / 3.0 - 0.25 * u)))
    return jnp.maximum(v, 0.0) + jnp.where(u < 0.01, series, jnp.log(1.0 + u))


def causal_mask(rows):
    at = lax.broadcasted_iota(jnp.int32, (rows, rows), 0)
    to = lax.broadcasted_iota(jnp.int32, (rows, rows), 1)
    return at >= to


def head_lanes(heads):
    return lax.broadcasted_iota(jnp.int32, (1, LANES), 1) < heads


def step_sizes(v, heads):
    return jnp.where(head_lanes(heads), softplus(v), 0.0)


def decay_rates(decay_log, heads):
    return jnp.where(head_lanes(heads), -jnp.exp(decay_log), 0.0)


def pair_stack(pair):
    lane = lax.broadcasted_iota(jnp.int32, pair.shape, 1)
    zero = jnp.zeros_like(pair)
    return jnp.concatenate(
        [jnp.where(lane < HEADDIM, pair, zero), jnp.where(lane >= HEADDIM, pair, zero)], axis=0
    )


def pair_decay(logs, logs_t, causal, pair):
    parts = []
    for head in (2 * pair, 2 * pair + 1):
        gap = logs[:, head : head + 1] - logs_t[head : head + 1, :]
        parts.append(jnp.exp(jnp.where(causal, gap, -1e30)))
    return parts


def first_kernel(
    heads,
    hid_ref, halo_ref, gain_ref, w_ref, cx_ref, cbc_ref, sb_ref, dl_ref, ex_ref,
    nb_ref, nbt_ref, xr_ref, xc_ref, bcr_ref, bcc_ref, v_ref, logs_ref, lpre_ref, sloc_ref, fin_ref,
    xext, bext, state, total, tail, xt,
):
    rows = hid_ref.shape[0]
    inner = xr_ref.shape[1]
    gain = gain_ref[...]

    def norm(block):
        h = block.astype(f32)
        scale = lax.rsqrt(jnp.mean(h * h, axis=1, keepdims=True) + epsilon)
        return (h * scale * gain).astype(bf16)

    @pl.when(pl.program_id(0) == 0)
    def _():
        state[...] = jnp.zeros_like(state)
        total[...] = jnp.zeros_like(total)
        before = norm(halo_ref[...])
        xext[0:8, :] = dot(before, w_ref[:, :inner])[8:16]
        bext[0:8, :] = dot(before, w_ref[:, inner + LANES :])[8:16]

    @pl.when(pl.program_id(0) > 0)
    def _():
        xext[0:8, :] = xext[rows : rows + 8, :]
        bext[0:8, :] = bext[rows : rows + 8, :]

    nb = norm(hid_ref[...])
    nb_ref[...] = nb
    nbt_ref[...] = nb.astype(f32).T.astype(bf16)
    xr = dot(nb, w_ref[:, :inner])
    xext[8 : 8 + rows, :] = xr
    xr_ref[...] = xr.astype(bf16)
    bcr = dot(nb, w_ref[:, inner + LANES :])
    bext[8 : 8 + rows, :] = bcr
    bcr_ref[...] = bcr
    v = dot(nb, w_ref[:, inner : inner + LANES]) + sb_ref[...]
    v_ref[...] = v
    bcc = jnp.broadcast_to(cbc_ref[4:5, :], bcr.shape)
    for tap in range(4):
        bcc = bcc + cbc_ref[tap : tap + 1, :] * bext[5 + tap : 5 + tap + rows, :]
    bcc_ref[...] = bcc
    keys = bcc[:, :STATE] * sigmoid(bcc[:, :STATE])
    dt = step_sizes(v, heads)
    la = dt * decay_rates(dl_ref[...], heads)
    ex = ex_ref[...]
    same, to_row, from_row = in_span(rows)
    logs = span_sum(jnp.logical_and(same, to_row >= from_row).astype(bf16), la)
    logs_ref[...] = logs
    lasts = last_rows(logs)
    tail[...] = expand(jnp.exp(span_gaps(logs)) * dt, ex)
    shrinks = expand(jnp.exp(stacked(lasts)), ex)
    for start in range(0, rows, TILE):
        here = slice(start, start + TILE)
        for block in range(inner // LANES):
            lanes = slice(block * LANES, (block + 1) * LANES)
            wide = xext[start : start + TILE + 8, lanes]
            xc = cx_ref[4:5, lanes] + cx_ref[3:4, lanes] * wide[8:]
            for tap in range(3):
                xc = xc + cx_ref[tap : tap + 1, lanes] * pltpu.roll(wide, 3 - tap, 0)[8:]
            xc = xc.astype(bf16)
            xc_ref[here, lanes] = xc
            xc = xc.astype(f32)
            xt[here, lanes] = (xc * sigmoid(xc) * tail[here, lanes]).astype(bf16)
    for at in range(rows // SPAN):
        span = slice(at * SPAN, (at + 1) * SPAN)
        lpre_ref[at * 8 : at * 8 + 8, :] = jnp.broadcast_to(total[0:1, :], (8, LANES))
        keys_t = keys[span].T.astype(bf16)
        for block in range(inner // (2 * LANES)):
            lanes = slice(block * 2 * LANES, (block + 1) * 2 * LANES)
            held = state[:, lanes]
            sloc_ref[at * STATE : (at + 1) * STATE, lanes] = held.astype(bf16)
            state[:, lanes] = held * shrinks[at : at + 1, lanes] + dot(keys_t, xt[span, lanes])
        total[...] = total[...] + lasts[at]

    @pl.when(pl.program_id(0) == pl.num_programs(0) - 1)
    def _():
        fin_ref[0:STATE, :] = state[...].astype(bf16)
        whole = expand(jnp.broadcast_to(jnp.exp(total[0:1, :]), (16, LANES)), ex)
        fin_ref[STATE : STATE + 16, :] = whole.astype(bf16)


def within_kernel(heads, xc_ref, bcc_ref, v_ref, logs_ref, ex_ref, yi_ref):
    causal = causal_mask(SPAN)
    for at in range(xc_ref.shape[0] // SPAN):
        span = slice(at * SPAN, (at + 1) * SPAN)
        xc = xc_ref[span, :].astype(f32)
        dt = step_sizes(v_ref[span, :], heads)
        xd = (xc * sigmoid(xc) * expand(dt, ex_ref[...])).astype(bf16)
        bcc = bcc_ref[span, :]
        bc = (bcc * sigmoid(bcc)).astype(bf16)
        scores = dot_nt(bc[:, STATE:], bc[:, :STATE])
        logs = logs_ref[span, :]
        logs_t = logs.T
        for pair in range(heads // 2):
            lanes = slice(pair * LANES, (pair + 1) * LANES)
            mixing = [(scores * d).astype(bf16) for d in pair_decay(logs, logs_t, causal, pair)]
            yi_ref[span, lanes] = dot(jnp.concatenate(mixing, axis=1), pair_stack(xd[:, lanes])).astype(bf16)


def incoming(refs):
    total = None
    for ref in reversed(refs):
        held = ref[0:STATE, :].astype(f32)
        if total is None:
            total = held
        else:
            total = held + ref[STATE : STATE + 1, :].astype(f32) * total
    return total


def middle_kernel(
    heads, far,
    hid_ref, cg_ref, z_ref, yi_ref, xc_ref, bcc_ref, logs_ref, lpre_ref, sloc_ref, wout_ref, gg_ref,
    skip_ref, ex_ref, fin_ref, *rest,
):
    fins = rest[:far]
    (out_ref, mixed_ref, dz_ref, g_ref, sc_ref, uc_ref, adj_ref, ggg_ref, gskip_ref) = rest[far : far + 9]
    (sin, acc, grown, ssm, gated, gm, ge) = rest[far + 9 :]

    @pl.when(pl.program_id(0) == 0)
    def _():
        sin[...] = incoming(fins) if far else jnp.zeros_like(sin)
        acc[...] = jnp.zeros_like(acc)
        ggg_ref[...] = jnp.zeros_like(ggg_ref)
        gskip_ref[...] = jnp.zeros_like(gskip_ref)

    ex = ex_ref[...]
    rows = hid_ref.shape[0]
    inner = z_ref.shape[1]
    count = inner // LANES
    skip = expand_row(skip_ref[...], ex)
    reads = bcc_ref[:, STATE:]
    reads = reads * sigmoid(reads)
    reads_t = [reads[k * SPAN : (k + 1) * SPAN].T.astype(bf16) for k in range(rows // SPAN)]
    reads = reads.astype(bf16)
    befores = []
    for at in range(rows // SPAN):
        span = slice(at * SPAN, (at + 1) * SPAN)
        states = slice(at * STATE, (at + 1) * STATE)
        before = expand_row(jnp.exp(lpre_ref[at * 8 : at * 8 + 1, :]), ex)
        befores.append(before)
        grown[span, :] = expand(jnp.exp(logs_ref[span, :]), ex)
        for block in range(inner // (2 * LANES)):
            lanes = slice(block * 2 * LANES, (block + 1) * 2 * LANES)
            held = (sloc_ref[states, lanes].astype(f32) + before[:, lanes] * sin[:, lanes]).astype(bf16)
            sc_ref[states, lanes] = held
            ssm[span, lanes] = dot(reads[span], held)

    def forward(index, carry):
        at = slice(index * TILE, (index + 1) * TILE)
        squares = jnp.zeros((TILE, LANES), f32)
        for block in range(count):
            lanes = slice(block * LANES, (block + 1) * LANES)
            xc = xc_ref[at, lanes].astype(f32)
            value = yi_ref[at, lanes].astype(f32) + grown[at, lanes] * ssm[at, lanes] + skip[:, lanes] * (xc * sigmoid(xc))
            ssm[at, lanes] = value
            z = z_ref[at, lanes].astype(f32)
            value = value * (z * sigmoid(z))
            gated[at, lanes] = value
            squares = squares + value * value
        gs = lax.rsqrt(jnp.sum(squares, axis=1, keepdims=True) / inner + epsilon)
        cross = jnp.zeros((TILE, LANES), f32)
        for block in range(count):
            lanes = slice(block * LANES, (block + 1) * LANES)
            value = gated[at, lanes]
            scaled = value * gs
            mixed_ref[at, lanes] = (scaled * gg_ref[:, lanes]).astype(bf16)
            gradient = cg_ref[at, lanes].astype(f32)
            ggg_ref[:, lanes] = add_rows(ggg_ref[:, lanes], gradient * scaled)
            weighted = gradient * gg_ref[:, lanes]
            gm[at, lanes] = weighted
            cross = cross + weighted * value
        mean = jnp.sum(cross, axis=1, keepdims=True) * (gs * gs * gs / inner)
        for block in range(count):
            lanes = slice(block * LANES, (block + 1) * LANES)
            dgated = gm[at, lanes] * gs - gated[at, lanes] * mean
            z = z_ref[at, lanes].astype(f32)
            sz = sigmoid(z)
            act = z * sz
            dz_ref[at, lanes] = (dgated * ssm[at, lanes] * (sz + act * (1.0 - sz))).astype(bf16)
            g = dgated * act
            g_ref[at, lanes] = g.astype(bf16)
            xc = xc_ref[at, lanes].astype(f32)
            gskip_ref[:, lanes] = add_rows(gskip_ref[:, lanes], g * (xc * sigmoid(xc)))
            ge[at, lanes] = (g * grown[at, lanes]).astype(bf16)
        return carry

    for index in range(rows // TILE):
        forward(index, 0)
    out_ref[...] = (hid_ref[...].astype(f32) + dot_nt(mixed_ref[...], wout_ref[...])).astype(bf16)
    for at in range(rows // SPAN):
        span = slice(at * SPAN, (at + 1) * SPAN)
        for block in range(inner // (2 * LANES)):
            lanes = slice(block * 2 * LANES, (block + 1) * 2 * LANES)
            u = dot(reads_t[at], ge[span, lanes])
            uc_ref[at * STATE : (at + 1) * STATE, lanes] = u.astype(bf16)
            acc[:, lanes] += befores[at][:, lanes] * u

    @pl.when(pl.program_id(0) == pl.num_programs(0) - 1)
    def _():
        adj_ref[0:STATE, :] = acc[...].astype(bf16)
        adj_ref[STATE:, :] = fin_ref[...]


def back_within_kernel(
    heads,
    g_ref, xc_ref, bcc_ref, v_ref, logs_ref, sc_ref, ex_ref, ext_ref,
    dxd_ref, dbc_ref, q_ref, grown, carried, ge,
):
    causal = causal_mask(SPAN)
    for at in range(xc_ref.shape[0] // SPAN):
        span = slice(at * SPAN, (at + 1) * SPAN)
        xc = xc_ref[span, :].astype(f32)
        dt = step_sizes(v_ref[span, :], heads)
        xd = (xc * sigmoid(xc) * expand(dt, ex_ref[...])).astype(bf16)
        bcc = bcc_ref[span, :]
        bc = (bcc * sigmoid(bcc)).astype(bf16)
        keys, reads = bc[:, :STATE], bc[:, STATE:]
        scores = dot_nt(reads, keys)
        logs = logs_ref[span, :]
        logs_t = logs.T
        states = slice(at * STATE, (at + 1) * STATE)
        held = sc_ref[states, :]
        grown[...] = expand(jnp.exp(logs), ex_ref[...])
        carried[...] = dot(reads, held)
        dscores = jnp.zeros((SPAN, SPAN), f32)
        lane = lax.broadcasted_iota(jnp.int32, (SPAN, LANES), 1)
        for pair in range(heads // 2):
            lanes = slice(pair * LANES, (pair + 1) * LANES)
            decays = pair_decay(logs, logs_t, causal, pair)
            mixing = jnp.concatenate([(scores * d).astype(bf16) for d in decays], axis=1)
            gp = g_ref[span, lanes]
            xp = xd[:, lanes]
            stack = pair_stack(xp)
            dmix = dot_nt(gp, stack)
            dscores = dscores + dmix[:, :SPAN] * decays[0] + dmix[:, SPAN:] * decays[1]
            both = dot_tn(mixing, gp)
            dxd = jnp.where(lane < HEADDIM, both[:SPAN], both[SPAN:])
            dxd_ref[span, lanes] = dxd.astype(bf16)
            gf = gp.astype(f32)
            scaled = gf * grown[:, lanes]
            ge[:, lanes] = scaled.astype(bf16)
            carried[:, lanes] = gf * dot(mixing, stack) - xp.astype(f32) * dxd + scaled * carried[:, lanes]
        dscores = dscores.astype(bf16)
        dbc_ref[span, :STATE] = dot_tn(dscores, reads)
        dbc_ref[span, STATE:] = dot(dscores, keys) + dot_nt(ge[...], held)
        q_ref[span, :] = split_dot(carried[...], ext_ref[...])


def last_kernel(
    heads, far,
    g_ref, xc_ref, bcc_ref, v_ref, logs_ref, sc_ref, uc_ref, dxd_ref, dbc_ref, q_ref, xr_ref, bcr_ref,
    dl_ref, skip_ref, ex_ref, ext_ref, cx_ref, cbc_ref, *rest,
):
    adjs = rest[:far]
    (grad_ref, gsb_ref, gdl_ref, gcx_ref, gcbc_ref, edge_ref) = rest[far : far + 6]
    (adj, tail, dte, dxu, xt, p3, p4, xext, bext) = rest[far + 6 :]
    inner = xc_ref.shape[1]

    @pl.when(pl.program_id(0) == 0)
    def _():
        adj[...] = incoming(adjs) if far else jnp.zeros_like(adj)
        gsb_ref[...] = jnp.zeros_like(gsb_ref)
        gdl_ref[...] = jnp.zeros_like(gdl_ref)
        gcx_ref[...] = jnp.zeros_like(gcx_ref)
        gcbc_ref[...] = jnp.zeros_like(gcbc_ref)
        xext[SPAN:, :] = jnp.zeros((8, inner), f32)
        bext[SPAN:, :] = jnp.zeros((8, bext.shape[1]), f32)

    ex = ex_ref[...]
    ext = ext_ref[...]
    causal = causal_mask(SPAN)
    not_after = causal.astype(f32)
    strictly = not_after - jnp.logical_and(causal, causal.T).astype(f32)
    upper = 1.0 - strictly
    rates = decay_rates(dl_ref[...], heads)
    skip = expand_row(skip_ref[...], ex)
    for at in reversed(range(xc_ref.shape[0] // SPAN)):
        span = slice(at * SPAN, (at + 1) * SPAN)
        states = slice(at * STATE, (at + 1) * STATE)
        v = v_ref[span, :]
        dt = step_sizes(v, heads)
        bcc = bcc_ref[span, :]
        sbc = sigmoid(bcc)
        keys = (bcc * sbc)[:, :STATE].astype(bf16)
        logs = logs_ref[span, :]
        last = logs[SPAN - 1 : SPAN, :]
        shrink = expand_row(jnp.exp(last), ex)
        tail[...] = expand(jnp.exp(last - logs), ex)
        dte[...] = expand(dt, ex)
        held_low = adj[...].astype(bf16)
        dxu[...] = dot(keys, held_low)
        for start in range(0, SPAN, TILE):
            here = slice(start, start + TILE)
            there = slice(at * SPAN + start, at * SPAN + start + TILE)
            for block in range(inner // LANES):
                lanes = slice(block * LANES, (block + 1) * LANES)
                xc = xc_ref[there, lanes].astype(f32)
                sx = sigmoid(xc)
                xs = xc * sx
                tails = tail[here, lanes]
                update = tails * dxu[here, lanes]
                xd = xs * dte[here, lanes]
                xt[here, lanes] = (xd * tails).astype(bf16)
                p3[here, lanes] = (xd * update).astype(bf16)
                dxd = dxd_ref[there, lanes].astype(f32) + update
                p4[here, lanes] = (xs * dxd).astype(bf16)
                dxs = dte[here, lanes] * dxd + skip[:, lanes] * g_ref[there, lanes].astype(f32)
                xext[here, lanes] = dxs * (sx + xs * (1.0 - sx))
        inners = []
        for block in range(inner // LANES):
            lanes = slice(block * LANES, (block + 1) * LANES)
            held = adj[:, lanes]
            inners.append(jnp.sum(held * sc_ref[states, lanes].astype(f32), axis=0, keepdims=True))
            adj[:, lanes] = held * shrink[:, lanes] + uc_ref[states, lanes].astype(f32)
        within = jnp.concatenate(inners, axis=1) * shrink
        within = split_dot(jnp.broadcast_to(within, (8, inner)), ext)[0:1]
        dkeys = dbc_ref[span, :STATE] + dot_nt(xt[...], held_low)
        dbc = jnp.concatenate([dkeys, dbc_ref[span, STATE:]], axis=1)
        bext[0:SPAN, :] = dbc * (sbc + bcc * sbc * (1.0 - sbc))
        dla = exact_dot(upper, q_ref[span, :]) + exact_dot(strictly, dot(p3[...], ext)) + within
        ddt = rates * dla + dot(p4[...], ext)
        dv = jnp.where(head_lanes(heads), ddt * small_sigmoid(v), 0.0)
        grad_ref[span, inner : inner + LANES] = dv.astype(bf16)
        gsb_ref[...] += jnp.sum(dv, axis=0, keepdims=True)
        gdl_ref[...] += jnp.sum(dt * dla, axis=0, keepdims=True) * rates
        for moved_ref, rows_ref, taps, first, sums in (
            (xext, xr_ref, cx_ref, 0, gcx_ref),
            (bext, bcr_ref, cbc_ref, inner + LANES, gcbc_ref),
        ):
            for block in range(moved_ref.shape[1] // LANES):
                lanes = slice(block * LANES, (block + 1) * LANES)
                parts = [jnp.zeros((8, LANES), f32)] * 5
                for start in range(0, SPAN, TILE):
                    there = slice(at * SPAN + start, at * SPAN + start + TILE)
                    before = rows_ref[there, lanes].astype(f32)
                    wide = moved_ref[start : start + TILE + 8, lanes]
                    total = None
                    for tap in range(4):
                        moved = (wide if tap == 3 else pltpu.roll(wide, TILE + 8 - (3 - tap), 0))[:TILE]
                        term = taps[tap : tap + 1, lanes] * moved
                        total = term if total is None else total + term
                        parts[tap] = add_rows(parts[tap], before * moved)
                    parts[4] = add_rows(parts[4], moved)
                    grad_ref[there, first + lanes.start : first + lanes.stop] = total.astype(bf16)
                for tap in range(5):
                    sums[tap * 8 : tap * 8 + 8, lanes] += parts[tap]
            moved_ref[SPAN:, :] = moved_ref[0:8, :]

    edge_ref[:, :inner] = xext[0:8, :]
    edge_ref[:, inner:] = bext[0:8, :]


def mend_kernel(
    edge_ref, rows_ref, bcr_ref, xr_ref, cx_ref, cbc_ref, gcx_ref, gcbc_ref, ggg_ref, gskip_ref, gsb_ref, gdl_ref,
    ext_ref, grad_ref, sums_ref,
):
    inner = xr_ref.shape[1]
    shared = bcr_ref.shape[1]
    row = lax.broadcasted_iota(jnp.int32, (8, 1), 0)
    sums_ref[...] = jnp.zeros_like(sums_ref)
    grad_ref[...] = rows_ref[...]
    for before, taps, start, first, top, old in (
        (xr_ref, cx_ref, 0, 0, 0, gcx_ref),
        (bcr_ref, cbc_ref, inner, inner + LANES, 6, gcbc_ref),
    ):
        wide_by = before.shape[1]
        late = before[8:16, :].astype(f32)
        total = jnp.zeros((8, wide_by), f32)
        for tap in range(5):
            value = old[tap * 8 : tap * 8 + 8, :]
            if tap < 3:
                moved = pltpu.roll(edge_ref[:, start : start + wide_by], 5 + tap, 0)
                moved = jnp.where(row >= 5 + tap, moved, 0.0)
                total = total + taps[tap : tap + 1, :] * moved
                value = value + late * moved
            sums_ref[top + tap : top + tap + 1, :wide_by] = jnp.sum(value, axis=0, keepdims=True)
        there = slice(first, first + wide_by)
        fixed = rows_ref[8:16, there].astype(f32) + total
        grad_ref[:, there] = jnp.concatenate([rows_ref[0:8, there].astype(f32), fixed], axis=0).astype(bf16)
    sums_ref[5:6, :] = jnp.sum(ggg_ref[...], axis=0, keepdims=True)
    skip = split_dot(gskip_ref[...], ext_ref[...])
    lanes = slice(shared, shared + LANES)
    sums_ref[6:7, lanes] = gsb_ref[...]
    sums_ref[7:8, lanes] = gdl_ref[...]
    sums_ref[8:9, lanes] = jnp.sum(skip, axis=0, keepdims=True)


def gate_kernel(nb_ref, cot_ref, w_ref, z_ref, cg_ref):
    inner = z_ref.shape[1]
    z_ref[...] = dot(nb_ref[...], w_ref[:, :inner]).astype(bf16)
    cg_ref[...] = dot(cot_ref[...], w_ref[:, inner:]).astype(bf16)


def pair_kernel(a_ref, c_ref, b_ref, d_ref, ab_ref, cd_ref):
    ab_ref[...] = dot(a_ref[...], b_ref[...]).astype(bf16)
    cd_ref[...] = dot(c_ref[...], d_ref[...]).astype(bf16)


def product_kernel(a_ref, b_ref, out_ref):
    out_ref[...] = dot(a_ref[...], b_ref[...]).astype(out_ref.dtype)


def join_kernel(chip_ref, held_ref, taken_ref, sums_ref, sums_taken_ref, *outs):
    sums = sums_ref[...].astype(f32) + sums_taken_ref[...].astype(f32)
    for turn, out in enumerate(outs):
        at = lax.rem(chip_ref[0] + turn, len(outs))
        total = held_ref[at] + taken_ref[at].astype(f32)
        out[...] = jnp.concatenate([total, sums], axis=0).astype(bf16)


def call(kernel, name, grid, ins, in_specs, outs, out_specs, scratch, flops=10**7, limit=56):
    return pl.pallas_call(
        kernel,
        grid=grid,
        in_specs=in_specs,
        out_specs=out_specs,
        out_shape=outs,
        scratch_shapes=scratch,
        name=name,
        compiler_params=pltpu.CompilerParams(vmem_limit_bytes=limit * 2**20),
        cost_estimate=pl.CostEstimate(flops=flops, bytes_accessed=10**5, transcendentals=0),
    )(*ins)


def rows_of(block, width):
    return pl.BlockSpec((block, width), lambda i: (i, 0))


def whole_of(array):
    return pl.BlockSpec(array.shape, lambda i: (0, 0), pipeline_mode=pl.Buffered(1))


def kept(shape):
    return pl.BlockSpec(shape, lambda i: (0, 0))


def shape(dims, kind):
    return jax.ShapeDtypeStruct(dims, kind)


def pad_rows(array, count):
    return jnp.pad(array, ((0, count - array.shape[0]), (0, 0)))


def pad_lanes(array):
    return jnp.pad(array, ((0, 0), (0, LANES - array.shape[1])))


def per_device(
    hidden_in, cotangent, norm_gain, gate_proj, input_proj, step_proj, shared_proj, output_proj,
    conv_inner, conv_shared, step_bias, decay_log, skip_gain, gated_gain,
):
    tensor_size = lax.axis_size("tensor")
    chips = lax.axis_size("dp") // 2
    place = lax.axis_index("tensor")
    core = lax.axis_index("dp") % 2
    chip = lax.axis_index("dp") // 2
    rows, width = hidden_in.shape
    heads_local = step_proj.shape[1]
    width_local = input_proj.shape[0]
    inner_local = gate_proj.shape[1]
    heads = heads_local * tensor_size
    inner = inner_local * tensor_size
    shared = shared_proj.shape[1]
    per_sequence = SEQ_LEN // rows
    far = per_sequence - 1

    def along(value, step):
        pairs = []
        for start in range(tensor_size):
            end = start + step
            if 0 <= end < tensor_size and start // per_sequence == end // per_sequence:
                pairs.append((start, end))
        return lax.ppermute(value, "tensor", pairs)

    def turn_tensor(value, step):
        return lax.ppermute(value, "tensor", [(i, (i + step) % tensor_size) for i in range(tensor_size)])

    def turn_chip(value, step):
        pairs = [(i, (i // 2 + step) % chips * 2 + i % 2) for i in range(2 * chips)]
        return lax.ppermute(value, "dp", pairs)

    def other_core(value):
        return lax.ppermute(value, "dp", [(i, i ^ 1) for i in range(2 * chips)])

    def in_order(turned, at):
        count = len(turned)
        return [lax.select_n((at - s) % count, *turned) for s in range(count)]

    def to_tensor(value):
        return [value] + [turn_tensor(value, k) for k in range(1, tensor_size)]

    def to_chips(value):
        return [value] + [turn_chip(value, k) for k in range(1, chips)]

    def by_core(value, other):
        first = core == 0
        both = jnp.stack([jnp.where(first, value, other), jnp.where(first, other, value)], axis=1)
        return both.reshape(-1, value.shape[-1])

    def core_rows(value):
        turned = value.reshape(chips, 2, -1, rows)
        return [
            lax.dynamic_index_in_dim(turned, which, 1, False).reshape(-1, rows) for which in (core, 1 - core)
        ]

    def join(first, *others):
        total = first.astype(f32)
        for other in others:
            total = total + other.astype(f32)
        return total.astype(first.dtype)

    def sum_chips_start(total):
        total = total.reshape(chips, -1, total.shape[-1])
        parts = [lax.dynamic_index_in_dim(total, (chip + k) % chips, 0, False) for k in range(chips)]
        return parts[0], [turn_chip(parts[k], k) for k in range(1, chips)]

    tie = lax.optimization_barrier

    def exchange(value, way, later):
        if per_sequence != 4:
            return [along(value, way * step) for step in range(1, far + 1)], later
        near, later = tie((along(value, way), later))
        both = value[:STATE].astype(f32) + value[STATE : STATE + 1].astype(f32) * near[:STATE].astype(f32)
        return [near, along(both.astype(bf16), 2 * way)], later

    small = jnp.concatenate(
        [
            conv_inner,
            gated_gain[None],
            jnp.pad(
                jnp.concatenate([step_bias, decay_log, skip_gain]), (0, inner_local - 3 * heads_local)
            )[None],
            jnp.zeros((1, inner_local), f32),
        ],
        axis=0,
    )
    high = tie(small.astype(bf16))
    low = (small - high.astype(f32)).astype(bf16)
    send = jnp.concatenate([input_proj, high, low], axis=0)
    send = jnp.concatenate([send, jnp.pad(step_proj, ((0, 16), (0, LANES - heads_local)))], axis=1)
    ends = hidden_in[rows - 16 :].reshape(-1)
    ends = jnp.pad(ends, (0, -ends.size % (16 * send.shape[1]))).reshape(-1, send.shape[1])
    given = jnp.concatenate([send, ends], axis=0)
    after = turn_tensor(given, 1)
    first_part = [send, after[: send.shape[0]]] + [turn_tensor(send, k) for k in range(2, tensor_size)]
    halo = after[send.shape[0] :].reshape(-1)[: 16 * width].reshape(16, width)
    halo = jnp.where(place % per_sequence == 0, jnp.zeros_like(halo), halo)
    first_part, second_part = tie((first_part, jnp.concatenate([gate_proj, output_proj], axis=1)))
    first_part = in_order(first_part, place)
    small = [
        p[width_local : width_local + 8, :inner_local].astype(f32) + p[width_local + 8 :, :inner_local].astype(f32)
        for p in first_part
    ]
    first_part = [p[:width_local] for p in first_part]
    steps_part = jnp.concatenate([p[:, inner_local : inner_local + heads_local] for p in first_part], axis=1)
    first_part = jnp.concatenate(
        [p[:, :inner_local] for p in first_part]
        + [pad_lanes(jnp.concatenate([steps_part, norm_gain[:, None]], axis=1)), shared_proj],
        axis=1,
    )
    wide_head = lax.broadcasted_iota(jnp.int32, (LANES, inner), 1) // HEADDIM
    ex = (lax.broadcasted_iota(jnp.int32, (LANES, inner), 0) % (LANES // 2) == wide_head).astype(bf16)
    tall_head = lax.broadcasted_iota(jnp.int32, (inner, LANES), 0) // HEADDIM
    ext = (lax.broadcasted_iota(jnp.int32, (inner, LANES), 1) == tall_head).astype(bf16)
    first_part, second_part, (cot_own, cot_given), ex, ext = tie(
        (to_chips(first_part), to_tensor(second_part), core_rows(cotangent.T), ex, ext)
    )
    first_part = jnp.stack(in_order(first_part, chip))
    weights = by_core(first_part, other_core(first_part))
    second_part = in_order(second_part, place)
    second_part = jnp.concatenate(
        [p[:, :inner_local] for p in second_part] + [p[:, inner_local:] for p in second_part], axis=1
    )
    second_part = to_chips(second_part)
    gain = weights[:, inner + heads].astype(f32)[None]

    wide = jnp.concatenate(small, axis=1)
    cx = pad_rows(wide[:5], 8)
    gg = wide[5:6]
    cbc = pad_rows(conv_shared, 8)

    def head_row(index):
        at = slice(index * heads_local, (index + 1) * heads_local)
        return pad_lanes(jnp.concatenate([p[6:7, at] for p in small], axis=1))

    sb, dl, sg = head_row(0), head_row(1), head_row(2)

    block = BLOCK * SPAN
    steps = rows // block
    chunks = rows // SPAN
    grid = (steps,)
    nb, nbt, xr, xc, bcr, bcc, v, logs, lpre, sloc, fin = call(
        functools.partial(first_kernel, heads),
        "first",
        grid,
        (hidden_in, halo, gain, weights, cx, cbc, sb, dl, ex),
        [rows_of(block, width)] + [whole_of(a) for a in (halo, gain, weights, cx, cbc, sb, dl, ex)],
        [
            shape((rows, width), bf16), shape((width, rows), bf16), shape((rows, inner), bf16), shape((rows, inner), bf16),
            shape((rows, shared), f32), shape((rows, shared), f32), shape((rows, LANES), f32),
            shape((rows, LANES), f32), shape((chunks * 8, LANES), f32),
            shape((chunks * STATE, inner), bf16), shape((STATE + 16, inner), bf16),
        ],
        [
            rows_of(block, width), pl.BlockSpec((width, block), lambda i: (0, i)), rows_of(block, inner),
            rows_of(block, inner), rows_of(block, shared), rows_of(block, shared), rows_of(block, LANES),
            rows_of(block, LANES), rows_of(8 * BLOCK, LANES),
            rows_of(BLOCK * STATE, inner), kept((STATE + 16, inner)),
        ],
        [
            pltpu.VMEM((block + 8, inner), f32), pltpu.VMEM((block + 8, shared), f32),
            pltpu.VMEM((STATE, inner), f32), pltpu.VMEM((8, LANES), f32),
            pltpu.VMEM((block, inner), f32), pltpu.VMEM((block, inner), bf16),
        ],
    )
    fins, second_part = exchange(fin, 1, second_part)
    far = len(fins)
    (yi,) = call(
        functools.partial(within_kernel, heads),
        "within",
        grid,
        (xc, bcc, v, logs, ex),
        [rows_of(block, inner), rows_of(block, shared), rows_of(block, LANES), rows_of(block, LANES), whole_of(ex)],
        [shape((rows, inner), bf16)],
        [rows_of(block, inner)],
        [],
        flops=10**10,
    )
    second_part = jnp.stack(in_order(second_part, chip))
    second_other = other_core(second_part)
    second_part = by_core(second_part, second_other)
    second_part, nb_rows = tie((second_part, core_rows(nbt)))
    nb_own, nb_given = nb_rows
    z, cg = call(
        gate_kernel,
        "gate",
        grid,
        (nb, cotangent, second_part),
        [rows_of(block, width), rows_of(block, width), whole_of(second_part)],
        [shape((rows, inner), bf16)] * 2,
        [rows_of(block, inner)] * 2,
        [],
    )
    state_rows = rows_of(BLOCK * STATE, inner)
    out, mixed, dz, g, sc, uc, adj, ggg, gskip = call(
        functools.partial(middle_kernel, heads, far),
        "middle",
        grid,
        (hidden_in, cg, z, yi, xc, bcc, logs, lpre, sloc, second_part, gg, sg, ex, fin, *fins),
        [
            rows_of(block, width), rows_of(block, inner), rows_of(block, inner), rows_of(block, inner),
            rows_of(block, inner), rows_of(block, shared), rows_of(block, LANES), rows_of(8 * BLOCK, LANES), state_rows,
        ]
        + [pl.BlockSpec((width, inner), lambda i: (0, 1), pipeline_mode=pl.Buffered(1))]
        + [whole_of(a) for a in (gg, sg, ex)]
        + [pl.BlockSpec((16, inner), lambda i: (STATE // 16, 0))]
        + [whole_of(a) for a in fins],
        [
            shape((rows, width), bf16), shape((rows, inner), bf16), shape((rows, inner), bf16),
            shape((rows, inner), bf16), shape((chunks * STATE, inner), bf16), shape((chunks * STATE, inner), bf16),
            shape((STATE + 16, inner), bf16), shape((8, inner), f32), shape((8, inner), f32),
        ],
        [
            rows_of(block, width), rows_of(block, inner), rows_of(block, inner), rows_of(block, inner),
            state_rows, state_rows, kept((STATE + 16, inner)), kept((8, inner)), kept((8, inner)),
        ],
        [pltpu.VMEM((STATE, inner), f32)] * 2 + [pltpu.VMEM((block, inner), f32)] * 4 + [pltpu.VMEM((block, inner), bf16)],
    )
    backs, g = exchange(adj, -1, g)
    dxd, dbc, q = call(
        functools.partial(back_within_kernel, heads),
        "back_within",
        grid,
        (g, xc, bcc, v, logs, sc, ex, ext),
        [
            rows_of(block, inner), rows_of(block, inner), rows_of(block, shared), rows_of(block, LANES),
            rows_of(block, LANES), state_rows, whole_of(ex), whole_of(ext),
        ],
        [shape((rows, inner), bf16), shape((rows, shared), f32), shape((rows, LANES), f32)],
        [rows_of(block, inner), rows_of(block, shared), rows_of(block, LANES)],
        [pltpu.VMEM((SPAN, inner), f32), pltpu.VMEM((SPAN, inner), f32), pltpu.VMEM((SPAN, inner), bf16)],
        flops=10**10,
    )

    def pair_product(a, c):
        tile = inner // 3
        tiled = pl.BlockSpec((rows, tile), lambda i: (0, i))
        return call(
            pair_kernel,
            "pair",
            (3,),
            (a, c, dz, mixed),
            [whole_of(a), whole_of(c), tiled, tiled],
            [shape((a.shape[0], inner), bf16)] * 2,
            [pl.BlockSpec((a.shape[0], tile), lambda i: (0, i))] * 2,
            [],
        )

    taken = [other_core(value) for value in pair_product(nb_given, cot_given)]
    held = pair_product(nb_own, cot_own)
    backs, taken, held, dxd = tie((backs, taken, held, dxd))
    second_parts, second_taken = sum_chips_start(
        jnp.concatenate([join(own, other).astype(bf16) for own, other in zip(held, taken)], axis=1)
    )

    def turned(size, wide_by):
        return pl.BlockSpec((size, wide_by), lambda i: (steps - 1 - i, 0))

    wide_rows = inner + LANES + shared
    grad_rows, gsb, gdl, gcx, gcbc, edge = call(
        functools.partial(last_kernel, heads, far),
        "last",
        grid,
        (g, xc, bcc, v, logs, sc, uc, dxd, dbc, q, xr, bcr, dl, sg, ex, ext, cx, cbc, *backs),
        [
            turned(block, inner), turned(block, inner), turned(block, shared), turned(block, LANES),
            turned(block, LANES), turned(BLOCK * STATE, inner), turned(BLOCK * STATE, inner), turned(block, inner),
            turned(block, shared), turned(block, LANES), turned(block, inner), turned(block, shared),
        ]
        + [whole_of(a) for a in (dl, sg, ex, ext, cx, cbc, *backs)],
        [
            shape((rows, wide_rows), bf16), shape((1, LANES), f32), shape((1, LANES), f32),
            shape((40, inner), f32), shape((40, shared), f32), shape((8, inner + shared), f32),
        ],
        [
            turned(block, wide_rows), kept((1, LANES)), kept((1, LANES)), kept((40, inner)), kept((40, shared)),
            kept((8, inner + shared)),
        ],
        [pltpu.VMEM((STATE, inner), f32)]
        + [pltpu.VMEM((SPAN, inner), f32)] * 3
        + [pltpu.VMEM((SPAN, inner), bf16)] * 3
        + [pltpu.VMEM((SPAN + 8, inner), f32), pltpu.VMEM((SPAN + 8, shared), f32)],
        flops=10**10,
    )
    edge, second_taken = tie((along(edge, -1), second_taken))
    second_sum = join(second_parts, *second_taken)
    second_pack = []
    for k in range(tensor_size):
        start = (place + k) % tensor_size * inner_local
        second_pack.append(
            jnp.concatenate(
                [
                    lax.dynamic_slice_in_dim(second_sum[:, :inner], start, inner_local, 1),
                    lax.dynamic_slice_in_dim(second_sum[:, inner:], start, inner_local, 1),
                ],
                axis=1,
            )
        )
    edge, second_pack = tie((edge, second_pack))
    second_kept = second_pack[0]
    second_last = [turn_tensor(second_pack[k], k) for k in range(1, tensor_size)]
    ending = rows // 16 - 1

    def end_rows(wide_by):
        return pl.BlockSpec((16, wide_by), lambda i: (ending, 0))

    sums_in = (cx, cbc, gcx, gcbc, ggg, gskip, gsb, gdl, ext)
    grad_rows, sums = pl.pallas_call(
        mend_kernel,
        grid=(1,),
        in_specs=[kept(edge.shape), end_rows(wide_rows), end_rows(shared), end_rows(inner)]
        + [kept(a.shape) for a in sums_in],
        out_specs=[end_rows(wide_rows), kept((16, inner))],
        out_shape=[shape(grad_rows.shape, bf16), shape((16, inner), f32)],
        input_output_aliases={1: 0},
        name="mend",
    )(edge, grad_rows, bcr, xr, *sums_in)
    def product(a, b, kind, flops=10**7):
        tile = wide_rows // 3
        (value,) = call(
            product_kernel,
            "product",
            (3,),
            (a, b),
            [whole_of(a), pl.BlockSpec((rows, tile), lambda i: (0, i))],
            [shape((a.shape[0], wide_rows), kind)],
            [pl.BlockSpec((a.shape[0], tile), lambda i: (0, i))],
            [],
            flops=flops,
        )
        return value

    given = product(nb_given, grad_rows, bf16)
    sums = jnp.pad(sums, ((0, 0), (0, wide_rows - inner))).astype(bf16)
    taken, sums_taken = other_core(given), other_core(sums)
    given, grad_rows = tie((given, grad_rows))
    held = product(nb_own, grad_rows, f32, 10**10)
    taken, sums_taken, second_last = tie((taken, sums_taken, second_last))
    joined = (
        held.reshape(chips, width_local, wide_rows), taken.reshape(chips, width_local, wide_rows), sums, sums_taken,
    )
    part = (width_local + sums.shape[0], wide_rows)

    def whole_block(dims):
        return pl.BlockSpec(dims, lambda i, at: (0,) * len(dims))

    parts = pl.pallas_call(
        join_kernel,
        grid_spec=pltpu.PrefetchScalarGridSpec(
            num_scalar_prefetch=1,
            grid=(1,),
            in_specs=[whole_block(value.shape) for value in joined],
            out_specs=[whole_block(part)] * chips,
        ),
        out_shape=[shape(part, bf16)] * chips,
        name="join",
        compiler_params=pltpu.CompilerParams(vmem_limit_bytes=40 * 2**20),
    )(chip[None].astype(jnp.int32), *joined)
    _, grad_rows, dz, second_part = tie((parts, grad_rows, dz, second_part))
    wz = second_part[:, :inner]
    first_taken = [turn_chip(parts[k], k) for k in range(1, chips)]
    grad_normed = dot_nt(dz, wz) + dot_nt(grad_rows, weights)
    h = hidden_in.astype(f32)
    scale = lax.rsqrt(jnp.mean(h * h, axis=1, keepdims=True) + epsilon)
    weighted = grad_normed * gain
    grad_hidden = (
        cotangent.astype(f32)
        + weighted * scale
        - h * scale**3 * jnp.mean(weighted * h, axis=1, keepdims=True)
    ).astype(bf16)
    first_taken, grad_hidden = tie((first_taken, grad_hidden))
    first_sum = join(parts[0].astype(f32), *first_taken)
    sums = first_sum[width_local:]
    first_sum = first_sum[:width_local]
    mine = lax.axis_index("dp") * width_local

    def own_rows(value):
        return lax.dynamic_slice_in_dim(value, mine, width_local, axis=0).astype(f32)

    columns = lax.broadcasted_iota(jnp.int32, first_sum.shape, 1)
    counted = jnp.where(columns == inner + heads, 0.0, own_rows(weights) * first_sum)
    norm = jnp.sum(counted, axis=1) + jnp.sum(own_rows(wz) * second_sum[:, :inner].astype(f32), axis=1)
    norm = (norm / norm_gain.astype(f32)).reshape(tensor_size, -1)
    shared_rows = width_local // tensor_size
    wide_by = inner_local + LANES
    step_sum = first_sum[:, inner : inner + LANES]
    first_kept, first_taken = None, []
    for k in range(tensor_size):
        to = (place + k) % tensor_size
        shared_to = lax.dynamic_slice_in_dim(first_sum[:, inner + LANES :], to * shared_rows, shared_rows, 0)
        norm_to = lax.dynamic_slice_in_dim(norm, to, 1, 0)
        block_to = jnp.concatenate(
            [
                lax.dynamic_slice_in_dim(first_sum[:, :inner], to * inner_local, inner_local, 1),
                lax.dynamic_slice_in_dim(sums[:6, :inner], to * inner_local, inner_local, 1),
            ],
            axis=0,
        )
        side = jnp.concatenate([step_sum, sums[6:12, shared : shared + LANES]], axis=0)
        block_to = jnp.concatenate([block_to, side], axis=1)
        low = jnp.concatenate([shared_to, sums[6:11, :shared], jnp.pad(norm_to, ((0, 0), (0, shared - shared_rows)))])
        block_to = jnp.concatenate([block_to, jnp.pad(low, ((0, 0), (0, wide_by - shared)))], axis=0)
        block_to = jnp.pad(block_to, ((0, -block_to.shape[0] % 16), (0, 0))).astype(bf16)
        if k == 0:
            first_kept = block_to
        else:
            first_taken.append(turn_tensor(block_to, k))
    first_sum = join(first_kept.astype(f32), *first_taken)
    second_sum = join(second_kept.astype(f32), *second_last)
    low = first_sum[width_local + 6 :]
    sums = first_sum[width_local : width_local + 6]
    grad_shared = low[:shared_rows, :shared]
    grad_norm = low[shared_rows + 5, :shared_rows]

    def head_cut(value):
        return lax.dynamic_slice_in_dim(value, inner_local + place * heads_local, heads_local, 1)

    head_sums = head_cut(sums)

    return (
        out,
        grad_hidden,
        grad_norm,
        second_sum[:, :inner_local],
        first_sum[:width_local, :inner_local],
        head_cut(first_sum[:width_local]),
        grad_shared,
        second_sum[:, inner_local:],
        sums[:5, :inner_local],
        low[shared_rows : shared_rows + 5, :shared],
        head_sums[0],
        head_sums[1],
        head_sums[2],
        sums[5, :inner_local],
    )


def solution(mesh):
    placed = (
        P(("dp", "tensor"), None), P(("dp", "tensor"), None), P("dp"), P("dp", "tensor"), P("dp", "tensor"),
        P("dp", "tensor"), P("dp", None), P("dp", "tensor"), P(None, "tensor"), P(), P("tensor"), P("tensor"),
        P("tensor"), P("tensor"),
    )
    results = (
        P(("dp", "tensor"), None), P(("dp", "tensor"), None), P(("dp", "tensor")), P("dp", "tensor"),
        P("dp", "tensor"), P("dp", "tensor"), P(("dp", "tensor"), None), P("dp", "tensor"), P(None, "tensor"),
        P(), P("tensor"), P("tensor"), P("tensor"), P("tensor"),
    )
    return jax.shard_map(per_device, mesh=mesh, in_specs=placed, out_specs=results, check_vma=False)
```

```python
import functools

import jax
import jax.numpy as jnp
from jax import lax
from jax.experimental import pallas as pl
from jax.experimental.pallas import tpu as pltpu
from jax.sharding import PartitionSpec as P

HEADDIM = 64
STATE = 128
SEQ_LEN = 4096
SPAN = 128
TILE = 64
BLOCK = 2
LANES = 128
epsilon = 1e-05
bf16 = jnp.bfloat16
f32 = jnp.float32


def dot(a, b):
    return lax.dot_general(a, b, (((1,), (0,)), ((), ())), preferred_element_type=f32)


def dot_nt(a, b):
    return lax.dot_general(a, b, (((1,), (1,)), ((), ())), preferred_element_type=f32)


def dot_tn(a, b):
    return lax.dot_general(a, b, (((0,), (0,)), ((), ())), preferred_element_type=f32)


def exact_dot(a, b):
    return lax.dot_general(
        a, b, (((1,), (0,)), ((), ())), preferred_element_type=f32, precision=lax.Precision.HIGHEST
    )


def split_dot(values, matrix):
    high = values.astype(bf16)
    low = (values - high.astype(f32)).astype(bf16)
    return dot(high, matrix) + dot(low, matrix)


def sigmoid(v):
    return 0.5 + 0.5 * jnp.tanh(0.5 * v)


def small_sigmoid(v):
    return 1.0 / (1.0 + jnp.exp(-v))


def expand(values, matrix):
    high = values.astype(bf16).astype(f32)
    lane = lax.broadcasted_iota(jnp.int32, values.shape, 1)
    low = pltpu.roll(values - high, LANES // 2, 1)
    return dot(jnp.where(lane < LANES // 2, high, low).astype(bf16), matrix)


def expand_row(row, matrix):
    return expand(jnp.broadcast_to(row, (8, LANES)), matrix)[0:1]


def span_sum(matrix, values):
    high = values.astype(bf16).astype(f32)
    rest = values - high
    middle = rest.astype(bf16).astype(f32)
    lane = lax.broadcasted_iota(jnp.int32, values.shape, 1)
    packed = jnp.where(
        lane < 32,
        high,
        jnp.where(lane < 64, pltpu.roll(middle, 32, 1), jnp.where(lane < 96, pltpu.roll(rest - middle, 64, 1), 0.0)),
    )
    total = dot(matrix, packed.astype(bf16))
    total = total + pltpu.roll(total, LANES - 32, 1) + pltpu.roll(total, LANES - 64, 1)
    return jnp.where(lane < 32, total, 0.0)


def in_span(rows):
    at = lax.broadcasted_iota(jnp.int32, (rows, rows), 0)
    to = lax.broadcasted_iota(jnp.int32, (rows, rows), 1)
    return at // SPAN == to // SPAN, at, to


def last_rows(logs):
    return [logs[start + SPAN - 1 : start + SPAN, :] for start in range(0, logs.shape[0], SPAN)]


def stacked(row_list):
    row = lax.broadcasted_iota(jnp.int32, (8, LANES), 0)
    total = jnp.broadcast_to(row_list[0], (8, LANES))
    for index, value in enumerate(row_list[1:]):
        total = jnp.where(row > index, value, total)
    return total


def span_gaps(logs):
    spans = range(0, logs.shape[0], SPAN)
    return jnp.concatenate([last - logs[start : start + SPAN] for last, start in zip(last_rows(logs), spans)], axis=0)


def add_rows(total, value):
    return total + jnp.sum(value.reshape(-1, 8, value.shape[1]), axis=0)


def softplus(v):
    u = jnp.exp(-jnp.abs(v))
    series = u * (1.0 - u * (0.5 - u * (1.0 / 3.0 - 0.25 * u)))
    return jnp.maximum(v, 0.0) + jnp.where(u < 0.01, series, jnp.log(1.0 + u))


def causal_mask(rows):
    at = lax.broadcasted_iota(jnp.int32, (rows, rows), 0)
    to = lax.broadcasted_iota(jnp.int32, (rows, rows), 1)
    return at >= to


def head_lanes(heads):
    return lax.broadcasted_iota(jnp.int32, (1, LANES), 1) < heads


def step_sizes(v, heads):
    return jnp.where(head_lanes(heads), softplus(v), 0.0)


def decay_rates(decay_log, heads):
    return jnp.where(head_lanes(heads), -jnp.exp(decay_log), 0.0)


def pair_stack(pair):
    lane = lax.broadcasted_iota(jnp.int32, pair.shape, 1)
    zero = jnp.zeros_like(pair)
    return jnp.concatenate(
        [jnp.where(lane < HEADDIM, pair, zero), jnp.where(lane >= HEADDIM, pair, zero)], axis=0
    )


def pair_decay(logs, logs_t, causal, pair):
    parts = []
    for head in (2 * pair, 2 * pair + 1):
        gap = logs[:, head : head + 1] - logs_t[head : head + 1, :]
        parts.append(jnp.exp(jnp.where(causal, gap, -1e30)))
    return parts


def first_kernel(
    heads,
    hid_ref, halo_ref, gain_ref, w_ref, cx_ref, cbc_ref, sb_ref, dl_ref, ex_ref,
    nb_ref, nbt_ref, xr_ref, xc_ref, bcr_ref, bcc_ref, v_ref, logs_ref, lpre_ref, sloc_ref, fin_ref,
    xext, bext, state, total, tail, xt,
):
    rows = hid_ref.shape[0]
    inner = xr_ref.shape[1]
    gain = gain_ref[...]

    def norm(block):
        h = block.astype(f32)
        scale = lax.rsqrt(jnp.mean(h * h, axis=1, keepdims=True) + epsilon)
        return (h * scale * gain).astype(bf16)

    @pl.when(pl.program_id(0) == 0)
    def _():
        state[...] = jnp.zeros_like(state)
        total[...] = jnp.zeros_like(total)
        before = norm(halo_ref[...])
        xext[0:8, :] = dot(before, w_ref[:, :inner])[8:16]
        bext[0:8, :] = dot(before, w_ref[:, inner + LANES :])[8:16]

    @pl.when(pl.program_id(0) > 0)
    def _():
        xext[0:8, :] = xext[rows : rows + 8, :]
        bext[0:8, :] = bext[rows : rows + 8, :]

    nb = norm(hid_ref[...])
    nb_ref[...] = nb
    nbt_ref[...] = nb.astype(f32).T.astype(bf16)
    xr = dot(nb, w_ref[:, :inner])
    xext[8 : 8 + rows, :] = xr
    xr_ref[...] = xr.astype(bf16)
    bcr = dot(nb, w_ref[:, inner + LANES :])
    bext[8 : 8 + rows, :] = bcr
    bcr_ref[...] = bcr
    v = dot(nb, w_ref[:, inner : inner + LANES]) + sb_ref[...]
    v_ref[...] = v
    bcc = jnp.broadcast_to(cbc_ref[4:5, :], bcr.shape)
    for tap in range(4):
        bcc = bcc + cbc_ref[tap : tap + 1, :] * bext[5 + tap : 5 + tap + rows, :]
    bcc_ref[...] = bcc
    keys = bcc[:, :STATE] * sigmoid(bcc[:, :STATE])
    dt = step_sizes(v, heads)
    la = dt * decay_rates(dl_ref[...], heads)
    ex = ex_ref[...]
    same, to_row, from_row = in_span(rows)
    logs = span_sum(jnp.logical_and(same, to_row >= from_row).astype(bf16), la)
    logs_ref[...] = logs
    lasts = last_rows(logs)
    tail[...] = expand(jnp.exp(span_gaps(logs)) * dt, ex)
    shrinks = expand(jnp.exp(stacked(lasts)), ex)
    for start in range(0, rows, TILE):
        here = slice(start, start + TILE)
        for block in range(inner // LANES):
            lanes = slice(block * LANES, (block + 1) * LANES)
            wide = xext[start : start + TILE + 8, lanes]
            xc = cx_ref[4:5, lanes] + cx_ref[3:4, lanes] * wide[8:]
            for tap in range(3):
                xc = xc + cx_ref[tap : tap + 1, lanes] * pltpu.roll(wide, 3 - tap, 0)[8:]
            xc = xc.astype(bf16)
            xc_ref[here, lanes] = xc
            xc = xc.astype(f32)
            xt[here, lanes] = (xc * sigmoid(xc) * tail[here, lanes]).astype(bf16)
    for at in range(rows // SPAN):
        span = slice(at * SPAN, (at + 1) * SPAN)
        lpre_ref[at * 8 : at * 8 + 8, :] = jnp.broadcast_to(total[0:1, :], (8, LANES))
        keys_t = keys[span].T.astype(bf16)
        for block in range(inner // (2 * LANES)):
            lanes = slice(block * 2 * LANES, (block + 1) * 2 * LANES)
            held = state[:, lanes]
            sloc_ref[at * STATE : (at + 1) * STATE, lanes] = held.astype(bf16)
            state[:, lanes] = held * shrinks[at : at + 1, lanes] + dot(keys_t, xt[span, lanes])
        total[...] = total[...] + lasts[at]

    @pl.when(pl.program_id(0) == pl.num_programs(0) - 1)
    def _():
        fin_ref[0:STATE, :] = state[...].astype(bf16)
        whole = expand(jnp.broadcast_to(jnp.exp(total[0:1, :]), (16, LANES)), ex)
        fin_ref[STATE : STATE + 16, :] = whole.astype(bf16)


def within_kernel(heads, xc_ref, bcc_ref, v_ref, logs_ref, ex_ref, yi_ref):
    causal = causal_mask(SPAN)
    for at in range(xc_ref.shape[0] // SPAN):
        span = slice(at * SPAN, (at + 1) * SPAN)
        xc = xc_ref[span, :].astype(f32)
        dt = step_sizes(v_ref[span, :], heads)
        xd = (xc * sigmoid(xc) * expand(dt, ex_ref[...])).astype(bf16)
        bcc = bcc_ref[span, :]
        bc = (bcc * sigmoid(bcc)).astype(bf16)
        scores = dot_nt(bc[:, STATE:], bc[:, :STATE])
        logs = logs_ref[span, :]
        logs_t = logs.T
        for pair in range(heads // 2):
            lanes = slice(pair * LANES, (pair + 1) * LANES)
            mixing = [(scores * d).astype(bf16) for d in pair_decay(logs, logs_t, causal, pair)]
            yi_ref[span, lanes] = dot(jnp.concatenate(mixing, axis=1), pair_stack(xd[:, lanes])).astype(bf16)


def incoming(refs):
    total = None
    for ref in reversed(refs):
        held = ref[0:STATE, :].astype(f32)
        if total is None:
            total = held
        else:
            total = held + ref[STATE : STATE + 1, :].astype(f32) * total
    return total


def middle_kernel(
    heads, far,
    hid_ref, cg_ref, z_ref, yi_ref, xc_ref, bcc_ref, logs_ref, lpre_ref, sloc_ref, wout_ref, gg_ref,
    skip_ref, ex_ref, fin_ref, *rest,
):
    fins = rest[:far]
    (out_ref, mixed_ref, dz_ref, g_ref, sc_ref, uc_ref, adj_ref, ggg_ref, gskip_ref) = rest[far : far + 9]
    (sin, acc, grown, ssm, gated, gm, ge) = rest[far + 9 :]

    @pl.when(pl.program_id(0) == 0)
    def _():
        sin[...] = incoming(fins) if far else jnp.zeros_like(sin)
        acc[...] = jnp.zeros_like(acc)
        ggg_ref[...] = jnp.zeros_like(ggg_ref)
        gskip_ref[...] = jnp.zeros_like(gskip_ref)

    ex = ex_ref[...]
    rows = hid_ref.shape[0]
    inner = z_ref.shape[1]
    count = inner // LANES
    skip = expand_row(skip_ref[...], ex)
    reads = bcc_ref[:, STATE:]
    reads = reads * sigmoid(reads)
    reads_t = [reads[k * SPAN : (k + 1) * SPAN].T.astype(bf16) for k in range(rows // SPAN)]
    reads = reads.astype(bf16)
    befores = []
    for at in range(rows // SPAN):
        span = slice(at * SPAN, (at + 1) * SPAN)
        states = slice(at * STATE, (at + 1) * STATE)
        before = expand_row(jnp.exp(lpre_ref[at * 8 : at * 8 + 1, :]), ex)
        befores.append(before)
        grown[span, :] = expand(jnp.exp(logs_ref[span, :]), ex)
        for block in range(inner // (2 * LANES)):
            lanes = slice(block * 2 * LANES, (block + 1) * 2 * LANES)
            held = (sloc_ref[states, lanes].astype(f32) + before[:, lanes] * sin[:, lanes]).astype(bf16)
            sc_ref[states, lanes] = held
            ssm[span, lanes] = dot(reads[span], held)

    def forward(index, carry):
        at = slice(index * TILE, (index + 1) * TILE)
        squares = jnp.zeros((TILE, LANES), f32)
        for block in range(count):
            lanes = slice(block * LANES, (block + 1) * LANES)
            xc = xc_ref[at, lanes].astype(f32)
            value = yi_ref[at, lanes].astype(f32) + grown[at, lanes] * ssm[at, lanes] + skip[:, lanes] * (xc * sigmoid(xc))
            ssm[at, lanes] = value
            z = z_ref[at, lanes].astype(f32)
            value = value * (z * sigmoid(z))
            gated[at, lanes] = value
            squares = squares + value * value
        gs = lax.rsqrt(jnp.sum(squares, axis=1, keepdims=True) / inner + epsilon)
        cross = jnp.zeros((TILE, LANES), f32)
        for block in range(count):
            lanes = slice(block * LANES, (block + 1) * LANES)
            value = gated[at, lanes]
            scaled = value * gs
            mixed_ref[at, lanes] = (scaled * gg_ref[:, lanes]).astype(bf16)
            gradient = cg_ref[at, lanes].astype(f32)
            ggg_ref[:, lanes] = add_rows(ggg_ref[:, lanes], gradient * scaled)
            weighted = gradient * gg_ref[:, lanes]
            gm[at, lanes] = weighted
            cross = cross + weighted * value
        mean = jnp.sum(cross, axis=1, keepdims=True) * (gs * gs * gs / inner)
        for block in range(count):
            lanes = slice(block * LANES, (block + 1) * LANES)
            dgated = gm[at, lanes] * gs - gated[at, lanes] * mean
            z = z_ref[at, lanes].astype(f32)
            sz = sigmoid(z)
            act = z * sz
            dz_ref[at, lanes] = (dgated * ssm[at, lanes] * (sz + act * (1.0 - sz))).astype(bf16)
            g = dgated * act
            g_ref[at, lanes] = g.astype(bf16)
            xc = xc_ref[at, lanes].astype(f32)
            gskip_ref[:, lanes] = add_rows(gskip_ref[:, lanes], g * (xc * sigmoid(xc)))
            ge[at, lanes] = (g * grown[at, lanes]).astype(bf16)
        return carry

    for index in range(rows // TILE):
        forward(index, 0)
    out_ref[...] = (hid_ref[...].astype(f32) + dot_nt(mixed_ref[...], wout_ref[...])).astype(bf16)
    for at in range(rows // SPAN):
        span = slice(at * SPAN, (at + 1) * SPAN)
        for block in range(inner // (2 * LANES)):
            lanes = slice(block * 2 * LANES, (block + 1) * 2 * LANES)
            u = dot(reads_t[at], ge[span, lanes])
            uc_ref[at * STATE : (at + 1) * STATE, lanes] = u.astype(bf16)
            acc[:, lanes] += befores[at][:, lanes] * u

    @pl.when(pl.program_id(0) == pl.num_programs(0) - 1)
    def _():
        adj_ref[0:STATE, :] = acc[...].astype(bf16)
        adj_ref[STATE:, :] = fin_ref[...]


def back_within_kernel(
    heads,
    g_ref, xc_ref, bcc_ref, v_ref, logs_ref, sc_ref, ex_ref, ext_ref,
    dxd_ref, dbc_ref, q_ref, grown, carried, ge,
):
    causal = causal_mask(SPAN)
    for at in range(xc_ref.shape[0] // SPAN):
        span = slice(at * SPAN, (at + 1) * SPAN)
        xc = xc_ref[span, :].astype(f32)
        dt = step_sizes(v_ref[span, :], heads)
        xd = (xc * sigmoid(xc) * expand(dt, ex_ref[...])).astype(bf16)
        bcc = bcc_ref[span, :]
        bc = (bcc * sigmoid(bcc)).astype(bf16)
        keys, reads = bc[:, :STATE], bc[:, STATE:]
        scores = dot_nt(reads, keys)
        logs = logs_ref[span, :]
        logs_t = logs.T
        states = slice(at * STATE, (at + 1) * STATE)
        held = sc_ref[states, :]
        grown[...] = expand(jnp.exp(logs), ex_ref[...])
        carried[...] = dot(reads, held)
        dscores = jnp.zeros((SPAN, SPAN), f32)
        lane = lax.broadcasted_iota(jnp.int32, (SPAN, LANES), 1)
        for pair in range(heads // 2):
            lanes = slice(pair * LANES, (pair + 1) * LANES)
            decays = pair_decay(logs, logs_t, causal, pair)
            mixing = jnp.concatenate([(scores * d).astype(bf16) for d in decays], axis=1)
            gp = g_ref[span, lanes]
            xp = xd[:, lanes]
            stack = pair_stack(xp)
            dmix = dot_nt(gp, stack)
            dscores = dscores + dmix[:, :SPAN] * decays[0] + dmix[:, SPAN:] * decays[1]
            both = dot_tn(mixing, gp)
            dxd = jnp.where(lane < HEADDIM, both[:SPAN], both[SPAN:])
            dxd_ref[span, lanes] = dxd.astype(bf16)
            gf = gp.astype(f32)
            scaled = gf * grown[:, lanes]
            ge[:, lanes] = scaled.astype(bf16)
            carried[:, lanes] = gf * dot(mixing, stack) - xp.astype(f32) * dxd + scaled * carried[:, lanes]
        dscores = dscores.astype(bf16)
        dbc_ref[span, :STATE] = dot_tn(dscores, reads)
        dbc_ref[span, STATE:] = dot(dscores, keys) + dot_nt(ge[...], held)
        q_ref[span, :] = split_dot(carried[...], ext_ref[...])


def last_kernel(
    heads, far,
    g_ref, xc_ref, bcc_ref, v_ref, logs_ref, sc_ref, uc_ref, dxd_ref, dbc_ref, q_ref, xr_ref, bcr_ref,
    dl_ref, skip_ref, ex_ref, ext_ref, cx_ref, cbc_ref, *rest,
):
    adjs = rest[:far]
    (grad_ref, gsb_ref, gdl_ref, gcx_ref, gcbc_ref, edge_ref) = rest[far : far + 6]
    (adj, tail, dte, dxu, xt, p3, p4, xext, bext) = rest[far + 6 :]
    inner = xc_ref.shape[1]

    @pl.when(pl.program_id(0) == 0)
    def _():
        adj[...] = incoming(adjs) if far else jnp.zeros_like(adj)
        gsb_ref[...] = jnp.zeros_like(gsb_ref)
        gdl_ref[...] = jnp.zeros_like(gdl_ref)
        gcx_ref[...] = jnp.zeros_like(gcx_ref)
        gcbc_ref[...] = jnp.zeros_like(gcbc_ref)
        xext[SPAN:, :] = jnp.zeros((8, inner), f32)
        bext[SPAN:, :] = jnp.zeros((8, bext.shape[1]), f32)

    ex = ex_ref[...]
    ext = ext_ref[...]
    causal = causal_mask(SPAN)
    not_after = causal.astype(f32)
    strictly = not_after - jnp.logical_and(causal, causal.T).astype(f32)
    upper = 1.0 - strictly
    rates = decay_rates(dl_ref[...], heads)
    skip = expand_row(skip_ref[...], ex)
    for at in reversed(range(xc_ref.shape[0] // SPAN)):
        span = slice(at * SPAN, (at + 1) * SPAN)
        states = slice(at * STATE, (at + 1) * STATE)
        v = v_ref[span, :]
        dt = step_sizes(v, heads)
        bcc = bcc_ref[span, :]
        sbc = sigmoid(bcc)
        keys = (bcc * sbc)[:, :STATE].astype(bf16)
        logs = logs_ref[span, :]
        last = logs[SPAN - 1 : SPAN, :]
        shrink = expand_row(jnp.exp(last), ex)
        tail[...] = expand(jnp.exp(last - logs), ex)
        dte[...] = expand(dt, ex)
        held_low = adj[...].astype(bf16)
        dxu[...] = dot(keys, held_low)
        for start in range(0, SPAN, TILE):
            here = slice(start, start + TILE)
            there = slice(at * SPAN + start, at * SPAN + start + TILE)
            for block in range(inner // LANES):
                lanes = slice(block * LANES, (block + 1) * LANES)
                xc = xc_ref[there, lanes].astype(f32)
                sx = sigmoid(xc)
                xs = xc * sx
                tails = tail[here, lanes]
                update = tails * dxu[here, lanes]
                xd = xs * dte[here, lanes]
                xt[here, lanes] = (xd * tails).astype(bf16)
                p3[here, lanes] = (xd * update).astype(bf16)
                dxd = dxd_ref[there, lanes].astype(f32) + update
                p4[here, lanes] = (xs * dxd).astype(bf16)
                dxs = dte[here, lanes] * dxd + skip[:, lanes] * g_ref[there, lanes].astype(f32)
                xext[here, lanes] = dxs * (sx + xs * (1.0 - sx))
        inners = []
        for block in range(inner // LANES):
            lanes = slice(block * LANES, (block + 1) * LANES)
            held = adj[:, lanes]
            inners.append(jnp.sum(held * sc_ref[states, lanes].astype(f32), axis=0, keepdims=True))
            adj[:, lanes] = held * shrink[:, lanes] + uc_ref[states, lanes].astype(f32)
        within = jnp.concatenate(inners, axis=1) * shrink
        within = split_dot(jnp.broadcast_to(within, (8, inner)), ext)[0:1]
        dkeys = dbc_ref[span, :STATE] + dot_nt(xt[...], held_low)
        dbc = jnp.concatenate([dkeys, dbc_ref[span, STATE:]], axis=1)
        bext[0:SPAN, :] = dbc * (sbc + bcc * sbc * (1.0 - sbc))
        dla = exact_dot(upper, q_ref[span, :]) + exact_dot(strictly, dot(p3[...], ext)) + within
        ddt = rates * dla + dot(p4[...], ext)
        dv = jnp.where(head_lanes(heads), ddt * small_sigmoid(v), 0.0)
        grad_ref[span, inner : inner + LANES] = dv.astype(bf16)
        gsb_ref[...] += jnp.sum(dv, axis=0, keepdims=True)
        gdl_ref[...] += jnp.sum(dt * dla, axis=0, keepdims=True) * rates
        for moved_ref, rows_ref, taps, first, sums in (
            (xext, xr_ref, cx_ref, 0, gcx_ref),
            (bext, bcr_ref, cbc_ref, inner + LANES, gcbc_ref),
        ):
            for block in range(moved_ref.shape[1] // LANES):
                lanes = slice(block * LANES, (block + 1) * LANES)
                parts = [jnp.zeros((8, LANES), f32)] * 5
                for start in range(0, SPAN, TILE):
                    there = slice(at * SPAN + start, at * SPAN + start + TILE)
                    before = rows_ref[there, lanes].astype(f32)
                    wide = moved_ref[start : start + TILE + 8, lanes]
                    total = None
                    for tap in range(4):
                        moved = (wide if tap == 3 else pltpu.roll(wide, TILE + 8 - (3 - tap), 0))[:TILE]
                        term = taps[tap : tap + 1, lanes] * moved
                        total = term if total is None else total + term
                        parts[tap] = add_rows(parts[tap], before * moved)
                    parts[4] = add_rows(parts[4], moved)
                    grad_ref[there, first + lanes.start : first + lanes.stop] = total.astype(bf16)
                for tap in range(5):
                    sums[tap * 8 : tap * 8 + 8, lanes] += parts[tap]
            moved_ref[SPAN:, :] = moved_ref[0:8, :]

    edge_ref[:, :inner] = xext[0:8, :]
    edge_ref[:, inner:] = bext[0:8, :]


def mend_kernel(
    edge_ref, rows_ref, bcr_ref, xr_ref, cx_ref, cbc_ref, gcx_ref, gcbc_ref, ggg_ref, gskip_ref, gsb_ref, gdl_ref,
    ext_ref, grad_ref, sums_ref,
):
    inner = xr_ref.shape[1]
    shared = bcr_ref.shape[1]
    row = lax.broadcasted_iota(jnp.int32, (8, 1), 0)
    sums_ref[...] = jnp.zeros_like(sums_ref)
    grad_ref[...] = rows_ref[...]
    for before, taps, start, first, top, old in (
        (xr_ref, cx_ref, 0, 0, 0, gcx_ref),
        (bcr_ref, cbc_ref, inner, inner + LANES, 6, gcbc_ref),
    ):
        wide_by = before.shape[1]
        late = before[8:16, :].astype(f32)
        total = jnp.zeros((8, wide_by), f32)
        for tap in range(5):
            value = old[tap * 8 : tap * 8 + 8, :]
            if tap < 3:
                moved = pltpu.roll(edge_ref[:, start : start + wide_by], 5 + tap, 0)
                moved = jnp.where(row >= 5 + tap, moved, 0.0)
                total = total + taps[tap : tap + 1, :] * moved
                value = value + late * moved
            sums_ref[top + tap : top + tap + 1, :wide_by] = jnp.sum(value, axis=0, keepdims=True)
        there = slice(first, first + wide_by)
        fixed = rows_ref[8:16, there].astype(f32) + total
        grad_ref[:, there] = jnp.concatenate([rows_ref[0:8, there].astype(f32), fixed], axis=0).astype(bf16)
    sums_ref[5:6, :] = jnp.sum(ggg_ref[...], axis=0, keepdims=True)
    skip = split_dot(gskip_ref[...], ext_ref[...])
    lanes = slice(shared, shared + LANES)
    for index, value in enumerate((gsb_ref[...], gdl_ref[...], jnp.sum(skip, axis=0, keepdims=True))):
        high = value.astype(bf16).astype(f32)
        sums_ref[6 + index : 7 + index, lanes] = high
        sums_ref[9 + index : 10 + index, lanes] = value - high


def gate_kernel(nb_ref, cot_ref, w_ref, z_ref, cg_ref):
    inner = z_ref.shape[1]
    z_ref[...] = dot(nb_ref[...], w_ref[:, :inner]).astype(bf16)
    cg_ref[...] = dot(cot_ref[...], w_ref[:, inner:]).astype(bf16)


def pair_kernel(a_ref, c_ref, b_ref, d_ref, ab_ref, cd_ref):
    ab_ref[...] = dot(a_ref[...], b_ref[...]).astype(bf16)
    cd_ref[...] = dot(c_ref[...], d_ref[...]).astype(bf16)


def product_kernel(a_ref, b_ref, out_ref):
    out_ref[...] = dot(a_ref[...], b_ref[...]).astype(out_ref.dtype)


def join_kernel(shared, chip_ref, held_ref, taken_ref, sums_ref, sums_taken_ref, *outs):
    sums = sums_ref[...].astype(f32) + sums_taken_ref[...].astype(f32)
    lane = lax.broadcasted_iota(jnp.int32, sums.shape, 1)
    row = lax.broadcasted_iota(jnp.int32, sums.shape, 0)
    whole = sums + pltpu.roll(sums, sums.shape[0] - 3, 0)
    high = whole.astype(bf16).astype(f32)
    low = pltpu.roll(whole - high, 3, 0)
    upper = jnp.logical_and(row >= 6, row < 9)
    lower = jnp.logical_and(row >= 9, row < 12)
    split = jnp.where(upper, high, jnp.where(lower, low, sums))
    sums = jnp.where(jnp.logical_and(lane >= shared, lane < shared + LANES), split, sums)
    for turn, out in enumerate(outs):
        at = lax.rem(chip_ref[0] + turn, len(outs))
        total = held_ref[at] + taken_ref[at].astype(f32)
        out[...] = jnp.concatenate([total, sums], axis=0).astype(bf16)


def call(kernel, name, grid, ins, in_specs, outs, out_specs, scratch, flops=10**7, limit=56):
    return pl.pallas_call(
        kernel,
        grid=grid,
        in_specs=in_specs,
        out_specs=out_specs,
        out_shape=outs,
        scratch_shapes=scratch,
        name=name,
        compiler_params=pltpu.CompilerParams(vmem_limit_bytes=limit * 2**20),
        cost_estimate=pl.CostEstimate(flops=flops, bytes_accessed=10**5, transcendentals=0),
    )(*ins)


def rows_of(block, width):
    return pl.BlockSpec((block, width), lambda i: (i, 0))


def whole_of(array):
    return pl.BlockSpec(array.shape, lambda i: (0, 0), pipeline_mode=pl.Buffered(1))


def kept(shape):
    return pl.BlockSpec(shape, lambda i: (0, 0))


def shape(dims, kind):
    return jax.ShapeDtypeStruct(dims, kind)


def pad_rows(array, count):
    return jnp.pad(array, ((0, count - array.shape[0]), (0, 0)))


def pad_lanes(array):
    return jnp.pad(array, ((0, 0), (0, LANES - array.shape[1])))


def per_device(
    hidden_in, cotangent, norm_gain, gate_proj, input_proj, step_proj, shared_proj, output_proj,
    conv_inner, conv_shared, step_bias, decay_log, skip_gain, gated_gain,
):
    tensor_size = lax.axis_size("tensor")
    chips = lax.axis_size("dp") // 2
    place = lax.axis_index("tensor")
    core = lax.axis_index("dp") % 2
    chip = lax.axis_index("dp") // 2
    rows, width = hidden_in.shape
    heads_local = step_proj.shape[1]
    width_local = input_proj.shape[0]
    inner_local = gate_proj.shape[1]
    heads = heads_local * tensor_size
    inner = inner_local * tensor_size
    shared = shared_proj.shape[1]
    per_sequence = SEQ_LEN // rows
    far = per_sequence - 1

    def along(value, step):
        pairs = []
        for start in range(tensor_size):
            end = start + step
            if 0 <= end < tensor_size and start // per_sequence == end // per_sequence:
                pairs.append((start, end))
        return lax.ppermute(value, "tensor", pairs)

    def turn_tensor(value, step):
        return lax.ppermute(value, "tensor", [(i, (i + step) % tensor_size) for i in range(tensor_size)])

    def turn_chip(value, step):
        pairs = [(i, (i // 2 + step) % chips * 2 + i % 2) for i in range(2 * chips)]
        return lax.ppermute(value, "dp", pairs)

    def other_core(value):
        return lax.ppermute(value, "dp", [(i, i ^ 1) for i in range(2 * chips)])

    def in_order(turned, at):
        count = len(turned)
        return [lax.select_n((at - s) % count, *turned) for s in range(count)]

    def to_tensor(value):
        return [value] + [turn_tensor(value, k) for k in range(1, tensor_size)]

    def to_chips(value):
        return [value] + [turn_chip(value, k) for k in range(1, chips)]

    def by_core(value, other):
        first = core == 0
        both = jnp.stack([jnp.where(first, value, other), jnp.where(first, other, value)], axis=1)
        return both.reshape(-1, value.shape[-1])

    def core_rows(value):
        turned = value.reshape(chips, 2, -1, rows)
        return [
            lax.dynamic_index_in_dim(turned, which, 1, False).reshape(-1, rows) for which in (core, 1 - core)
        ]

    def join(first, *others):
        total = first.astype(f32)
        for other in others:
            total = total + other.astype(f32)
        return total.astype(first.dtype)

    def sum_chips_start(total):
        total = total.reshape(chips, -1, total.shape[-1])
        parts = [lax.dynamic_index_in_dim(total, (chip + k) % chips, 0, False) for k in range(chips)]
        return parts[0], [turn_chip(parts[k], k) for k in range(1, chips)]

    tie = lax.optimization_barrier

    def exchange(value, way, later):
        if per_sequence != 4:
            return [along(value, way * step) for step in range(1, far + 1)], later
        near, later = tie((along(value, way), later))
        both = value[:STATE].astype(f32) + value[STATE : STATE + 1].astype(f32) * near[:STATE].astype(f32)
        return [near, along(both.astype(bf16), 2 * way)], later

    small = jnp.concatenate(
        [
            conv_inner,
            gated_gain[None],
            jnp.pad(
                jnp.concatenate([step_bias, decay_log, skip_gain]), (0, inner_local - 3 * heads_local)
            )[None],
            jnp.zeros((1, inner_local), f32),
        ],
        axis=0,
    )
    high = tie(small.astype(bf16))
    low = (small - high.astype(f32)).astype(bf16)
    send = jnp.concatenate([input_proj, high, low], axis=0)
    send = jnp.concatenate([send, jnp.pad(step_proj, ((0, 16), (0, LANES - heads_local)))], axis=1)
    ends = hidden_in[rows - 16 :].reshape(-1)
    ends = jnp.pad(ends, (0, -ends.size % (16 * send.shape[1]))).reshape(-1, send.shape[1])
    given = jnp.concatenate([send, ends], axis=0)
    after = turn_tensor(given, 1)
    first_part = [send, after[: send.shape[0]]] + [turn_tensor(send, k) for k in range(2, tensor_size)]
    halo = after[send.shape[0] :].reshape(-1)[: 16 * width].reshape(16, width)
    halo = jnp.where(place % per_sequence == 0, jnp.zeros_like(halo), halo)
    first_part, second_part = tie((first_part, jnp.concatenate([gate_proj, output_proj], axis=1)))
    first_part = in_order(first_part, place)
    small = [
        p[width_local : width_local + 8, :inner_local].astype(f32) + p[width_local + 8 :, :inner_local].astype(f32)
        for p in first_part
    ]
    first_part = [p[:width_local] for p in first_part]
    steps_part = jnp.concatenate([p[:, inner_local : inner_local + heads_local] for p in first_part], axis=1)
    first_part = jnp.concatenate(
        [p[:, :inner_local] for p in first_part]
        + [pad_lanes(jnp.concatenate([steps_part, norm_gain[:, None]], axis=1)), shared_proj],
        axis=1,
    )
    wide_head = lax.broadcasted_iota(jnp.int32, (LANES, inner), 1) // HEADDIM
    ex = (lax.broadcasted_iota(jnp.int32, (LANES, inner), 0) % (LANES // 2) == wide_head).astype(bf16)
    tall_head = lax.broadcasted_iota(jnp.int32, (inner, LANES), 0) // HEADDIM
    ext = (lax.broadcasted_iota(jnp.int32, (inner, LANES), 1) == tall_head).astype(bf16)
    first_part, second_part, (cot_own, cot_given), ex, ext = tie(
        (to_chips(first_part), to_tensor(second_part), core_rows(cotangent.T), ex, ext)
    )
    first_part = jnp.stack(in_order(first_part, chip))
    weights = by_core(first_part, other_core(first_part))
    second_part = in_order(second_part, place)
    second_part = jnp.concatenate(
        [p[:, :inner_local] for p in second_part] + [p[:, inner_local:] for p in second_part], axis=1
    )
    second_part = to_chips(second_part)
    gain = weights[:, inner + heads].astype(f32)[None]

    wide = jnp.concatenate(small, axis=1)
    cx = pad_rows(wide[:5], 8)
    gg = wide[5:6]
    cbc = pad_rows(conv_shared, 8)

    def head_row(index):
        at = slice(index * heads_local, (index + 1) * heads_local)
        return pad_lanes(jnp.concatenate([p[6:7, at] for p in small], axis=1))

    sb, dl, sg = head_row(0), head_row(1), head_row(2)

    block = BLOCK * SPAN
    steps = rows // block
    chunks = rows // SPAN
    grid = (steps,)
    nb, nbt, xr, xc, bcr, bcc, v, logs, lpre, sloc, fin = call(
        functools.partial(first_kernel, heads),
        "first",
        grid,
        (hidden_in, halo, gain, weights, cx, cbc, sb, dl, ex),
        [rows_of(block, width)] + [whole_of(a) for a in (halo, gain, weights, cx, cbc, sb, dl, ex)],
        [
            shape((rows, width), bf16), shape((width, rows), bf16), shape((rows, inner), bf16), shape((rows, inner), bf16),
            shape((rows, shared), f32), shape((rows, shared), f32), shape((rows, LANES), f32),
            shape((rows, LANES), f32), shape((chunks * 8, LANES), f32),
            shape((chunks * STATE, inner), bf16), shape((STATE + 16, inner), bf16),
        ],
        [
            rows_of(block, width), pl.BlockSpec((width, block), lambda i: (0, i)), rows_of(block, inner),
            rows_of(block, inner), rows_of(block, shared), rows_of(block, shared), rows_of(block, LANES),
            rows_of(block, LANES), rows_of(8 * BLOCK, LANES),
            rows_of(BLOCK * STATE, inner), kept((STATE + 16, inner)),
        ],
        [
            pltpu.VMEM((block + 8, inner), f32), pltpu.VMEM((block + 8, shared), f32),
            pltpu.VMEM((STATE, inner), f32), pltpu.VMEM((8, LANES), f32),
            pltpu.VMEM((block, inner), f32), pltpu.VMEM((block, inner), bf16),
        ],
    )
    (yi,) = call(
        functools.partial(within_kernel, heads),
        "within",
        grid,
        (xc, bcc, v, logs, ex),
        [rows_of(block, inner), rows_of(block, shared), rows_of(block, LANES), rows_of(block, LANES), whole_of(ex)],
        [shape((rows, inner), bf16)],
        [rows_of(block, inner)],
        [],
        flops=10**10,
    )
    fins, (second_part, yi) = exchange(fin, 1, (second_part, yi))
    far = len(fins)
    second_part = jnp.stack(in_order(second_part, chip))
    second_other = other_core(second_part)
    second_part = by_core(second_part, second_other)
    second_part, nb_rows = tie((second_part, core_rows(nbt)))
    nb_own, nb_given = nb_rows
    z, cg = call(
        gate_kernel,
        "gate",
        grid,
        (nb, cotangent, second_part),
        [rows_of(block, width), rows_of(block, width), whole_of(second_part)],
        [shape((rows, inner), bf16)] * 2,
        [rows_of(block, inner)] * 2,
        [],
    )
    state_rows = rows_of(BLOCK * STATE, inner)
    out, mixed, dz, g, sc, uc, adj, ggg, gskip = call(
        functools.partial(middle_kernel, heads, far),
        "middle",
        grid,
        (hidden_in, cg, z, yi, xc, bcc, logs, lpre, sloc, second_part, gg, sg, ex, fin, *fins),
        [
            rows_of(block, width), rows_of(block, inner), rows_of(block, inner), rows_of(block, inner),
            rows_of(block, inner), rows_of(block, shared), rows_of(block, LANES), rows_of(8 * BLOCK, LANES), state_rows,
        ]
        + [pl.BlockSpec((width, inner), lambda i: (0, 1), pipeline_mode=pl.Buffered(1))]
        + [whole_of(a) for a in (gg, sg, ex)]
        + [pl.BlockSpec((16, inner), lambda i: (STATE // 16, 0))]
        + [whole_of(a) for a in fins],
        [
            shape((rows, width), bf16), shape((rows, inner), bf16), shape((rows, inner), bf16),
            shape((rows, inner), bf16), shape((chunks * STATE, inner), bf16), shape((chunks * STATE, inner), bf16),
            shape((STATE + 16, inner), bf16), shape((8, inner), f32), shape((8, inner), f32),
        ],
        [
            rows_of(block, width), rows_of(block, inner), rows_of(block, inner), rows_of(block, inner),
            state_rows, state_rows, kept((STATE + 16, inner)), kept((8, inner)), kept((8, inner)),
        ],
        [pltpu.VMEM((STATE, inner), f32)] * 2 + [pltpu.VMEM((block, inner), f32)] * 4 + [pltpu.VMEM((block, inner), bf16)],
    )
    backs, g = exchange(adj, -1, g)
    dxd, dbc, q = call(
        functools.partial(back_within_kernel, heads),
        "back_within",
        grid,
        (g, xc, bcc, v, logs, sc, ex, ext),
        [
            rows_of(block, inner), rows_of(block, inner), rows_of(block, shared), rows_of(block, LANES),
            rows_of(block, LANES), state_rows, whole_of(ex), whole_of(ext),
        ],
        [shape((rows, inner), bf16), shape((rows, shared), f32), shape((rows, LANES), f32)],
        [rows_of(block, inner), rows_of(block, shared), rows_of(block, LANES)],
        [pltpu.VMEM((SPAN, inner), f32), pltpu.VMEM((SPAN, inner), f32), pltpu.VMEM((SPAN, inner), bf16)],
        flops=10**10,
    )

    def pair_product(a, c):
        tile = inner // 3
        tiled = pl.BlockSpec((rows, tile), lambda i: (0, i))
        return call(
            pair_kernel,
            "pair",
            (3,),
            (a, c, dz, mixed),
            [whole_of(a), whole_of(c), tiled, tiled],
            [shape((a.shape[0], inner), bf16)] * 2,
            [pl.BlockSpec((a.shape[0], tile), lambda i: (0, i))] * 2,
            [],
        )

    taken = [other_core(value) for value in pair_product(nb_given, cot_given)]
    held = pair_product(nb_own, cot_own)
    backs, taken, held, dxd = tie((backs, taken, held, dxd))
    second_parts, second_taken = sum_chips_start(
        jnp.concatenate([join(own, other).astype(bf16) for own, other in zip(held, taken)], axis=1)
    )

    def turned(size, wide_by):
        return pl.BlockSpec((size, wide_by), lambda i: (steps - 1 - i, 0))

    wide_rows = inner + LANES + shared
    grad_rows, gsb, gdl, gcx, gcbc, edge = call(
        functools.partial(last_kernel, heads, far),
        "last",
        grid,
        (g, xc, bcc, v, logs, sc, uc, dxd, dbc, q, xr, bcr, dl, sg, ex, ext, cx, cbc, *backs),
        [
            turned(block, inner), turned(block, inner), turned(block, shared), turned(block, LANES),
            turned(block, LANES), turned(BLOCK * STATE, inner), turned(BLOCK * STATE, inner), turned(block, inner),
            turned(block, shared), turned(block, LANES), turned(block, inner), turned(block, shared),
        ]
        + [whole_of(a) for a in (dl, sg, ex, ext, cx, cbc, *backs)],
        [
            shape((rows, wide_rows), bf16), shape((1, LANES), f32), shape((1, LANES), f32),
            shape((40, inner), f32), shape((40, shared), f32), shape((8, inner + shared), f32),
        ],
        [
            turned(block, wide_rows), kept((1, LANES)), kept((1, LANES)), kept((40, inner)), kept((40, shared)),
            kept((8, inner + shared)),
        ],
        [pltpu.VMEM((STATE, inner), f32)]
        + [pltpu.VMEM((SPAN, inner), f32)] * 3
        + [pltpu.VMEM((SPAN, inner), bf16)] * 3
        + [pltpu.VMEM((SPAN + 8, inner), f32), pltpu.VMEM((SPAN + 8, shared), f32)],
        flops=10**10,
    )
    edge, second_taken = tie((along(edge, -1), second_taken))
    second_sum = join(second_parts, *second_taken)
    second_pack = []
    for k in range(tensor_size):
        start = (place + k) % tensor_size * inner_local
        second_pack.append(
            jnp.concatenate(
                [
                    lax.dynamic_slice_in_dim(second_sum[:, :inner], start, inner_local, 1),
                    lax.dynamic_slice_in_dim(second_sum[:, inner:], start, inner_local, 1),
                ],
                axis=1,
            )
        )
    edge, second_pack = tie((edge, second_pack))
    second_kept = second_pack[0]
    second_last = [turn_tensor(second_pack[k], k) for k in range(1, tensor_size)]
    ending = rows // 16 - 1

    def end_rows(wide_by):
        return pl.BlockSpec((16, wide_by), lambda i: (ending, 0))

    sums_in = (cx, cbc, gcx, gcbc, ggg, gskip, gsb, gdl, ext)
    grad_rows, sums = pl.pallas_call(
        mend_kernel,
        grid=(1,),
        in_specs=[kept(edge.shape), end_rows(wide_rows), end_rows(shared), end_rows(inner)]
        + [kept(a.shape) for a in sums_in],
        out_specs=[end_rows(wide_rows), kept((16, inner))],
        out_shape=[shape(grad_rows.shape, bf16), shape((16, inner), f32)],
        input_output_aliases={1: 0},
        name="mend",
    )(edge, grad_rows, bcr, xr, *sums_in)
    def product(a, b, kind, flops=10**7):
        tile = wide_rows // 3
        (value,) = call(
            product_kernel,
            "product",
            (3,),
            (a, b),
            [whole_of(a), pl.BlockSpec((rows, tile), lambda i: (0, i))],
            [shape((a.shape[0], wide_rows), kind)],
            [pl.BlockSpec((a.shape[0], tile), lambda i: (0, i))],
            [],
            flops=flops,
        )
        return value

    given = product(nb_given, grad_rows, bf16)
    sums = jnp.pad(sums, ((0, 0), (0, wide_rows - inner))).astype(bf16)
    taken, sums_taken = other_core(given), other_core(sums)
    given, grad_rows = tie((given, grad_rows))
    held = product(nb_own, grad_rows, f32, 10**10)
    taken, sums_taken, second_last = tie((taken, sums_taken, second_last))
    joined = (
        held.reshape(chips, width_local, wide_rows), taken.reshape(chips, width_local, wide_rows), sums, sums_taken,
    )
    part = (width_local + sums.shape[0], wide_rows)

    def whole_block(dims):
        return pl.BlockSpec(dims, lambda i, at: (0,) * len(dims))

    parts = pl.pallas_call(
        functools.partial(join_kernel, shared),
        grid_spec=pltpu.PrefetchScalarGridSpec(
            num_scalar_prefetch=1,
            grid=(1,),
            in_specs=[whole_block(value.shape) for value in joined],
            out_specs=[whole_block(part)] * chips,
        ),
        out_shape=[shape(part, bf16)] * chips,
        name="join",
        compiler_params=pltpu.CompilerParams(vmem_limit_bytes=40 * 2**20),
    )(chip[None].astype(jnp.int32), *joined)
    _, grad_rows, dz, second_part = tie((parts, grad_rows, dz, second_part))
    wz = second_part[:, :inner]
    first_taken = [turn_chip(parts[k], k) for k in range(1, chips)]
    grad_normed = dot_nt(dz, wz) + dot_nt(grad_rows, weights)
    h = hidden_in.astype(f32)
    scale = lax.rsqrt(jnp.mean(h * h, axis=1, keepdims=True) + epsilon)
    weighted = grad_normed * gain
    grad_hidden = (
        cotangent.astype(f32)
        + weighted * scale
        - h * scale**3 * jnp.mean(weighted * h, axis=1, keepdims=True)
    ).astype(bf16)
    first_taken, grad_hidden = tie((first_taken, grad_hidden))
    first_sum = join(parts[0].astype(f32), *first_taken)
    sums = first_sum[width_local:]
    first_sum = first_sum[:width_local]
    mine = lax.axis_index("dp") * width_local

    def own_rows(value):
        return lax.dynamic_slice_in_dim(value, mine, width_local, axis=0).astype(f32)

    columns = lax.broadcasted_iota(jnp.int32, first_sum.shape, 1)
    counted = jnp.where(columns == inner + heads, 0.0, own_rows(weights) * first_sum)
    norm = jnp.sum(counted, axis=1) + jnp.sum(own_rows(wz) * second_sum[:, :inner].astype(f32), axis=1)
    norm = (norm / norm_gain.astype(f32)).reshape(tensor_size, -1)
    shared_rows = width_local // tensor_size
    wide_by = inner_local + LANES
    step_sum = first_sum[:, inner : inner + LANES]
    head_all = sums[6:9, shared : shared + LANES] + sums[9:12, shared : shared + LANES]
    head_high = tie(head_all.astype(bf16)).astype(f32)
    head_low = head_all - head_high
    first_kept, first_taken = None, []
    for k in range(tensor_size):
        to = (place + k) % tensor_size
        shared_to = lax.dynamic_slice_in_dim(first_sum[:, inner + LANES :], to * shared_rows, shared_rows, 0)
        norm_to = lax.dynamic_slice_in_dim(norm, to, 1, 0)
        block_to = jnp.concatenate(
            [
                lax.dynamic_slice_in_dim(first_sum[:, :inner], to * inner_local, inner_local, 1),
                lax.dynamic_slice_in_dim(sums[:6, :inner], to * inner_local, inner_local, 1),
            ],
            axis=0,
        )
        side = jnp.concatenate([step_sum, head_high, head_low], axis=0)
        block_to = jnp.concatenate([block_to, side], axis=1)
        low = jnp.concatenate([shared_to, sums[6:11, :shared], jnp.pad(norm_to, ((0, 0), (0, shared - shared_rows)))])
        block_to = jnp.concatenate([block_to, jnp.pad(low, ((0, 0), (0, wide_by - shared)))], axis=0)
        block_to = jnp.pad(block_to, ((0, -block_to.shape[0] % 16), (0, 0))).astype(bf16)
        if k == 0:
            first_kept = block_to
        else:
            first_taken.append(turn_tensor(block_to, k))
    first_sum = join(first_kept.astype(f32), *first_taken)
    second_sum = join(second_kept.astype(f32), *second_last)
    low = first_sum[width_local + 6 :]
    sums = first_sum[width_local : width_local + 6]
    grad_shared = low[:shared_rows, :shared]
    grad_norm = low[shared_rows + 5, :shared_rows]

    def head_cut(value):
        return lax.dynamic_slice_in_dim(value, inner_local + place * heads_local, heads_local, 1)

    head_sums = head_cut(sums[:3] + sums[3:])

    return (
        out,
        grad_hidden,
        grad_norm,
        second_sum[:, :inner_local],
        first_sum[:width_local, :inner_local],
        head_cut(first_sum[:width_local]),
        grad_shared,
        second_sum[:, inner_local:],
        sums[:5, :inner_local],
        low[shared_rows : shared_rows + 5, :shared],
        head_sums[0],
        head_sums[1],
        head_sums[2],
        sums[5, :inner_local],
    )


def solution(mesh):
    placed = (
        P(("dp", "tensor"), None), P(("dp", "tensor"), None), P("dp"), P("dp", "tensor"), P("dp", "tensor"),
        P("dp", "tensor"), P("dp", None), P("dp", "tensor"), P(None, "tensor"), P(), P("tensor"), P("tensor"),
        P("tensor"), P("tensor"),
    )
    results = (
        P(("dp", "tensor"), None), P(("dp", "tensor"), None), P(("dp", "tensor")), P("dp", "tensor"),
        P("dp", "tensor"), P("dp", "tensor"), P(("dp", "tensor"), None), P("dp", "tensor"), P(None, "tensor"),
        P(), P("tensor"), P("tensor"), P("tensor"), P("tensor"),
    )
    return jax.shard_map(per_device, mesh=mesh, in_specs=placed, out_specs=results, check_vma=False)
```

```python
import functools

import jax
import jax.numpy as jnp
from jax import lax
from jax.experimental import pallas as pl
from jax.experimental.pallas import tpu as pltpu
from jax.sharding import PartitionSpec as P

HEADDIM = 64
STATE = 128
SEQ_LEN = 4096
SPAN = 128
TILE = 64
BLOCK = 2
LANES = 128
epsilon = 1e-05
bf16 = jnp.bfloat16
f32 = jnp.float32


def dot(a, b):
    return lax.dot_general(a, b, (((1,), (0,)), ((), ())), preferred_element_type=f32)


def dot_nt(a, b):
    return lax.dot_general(a, b, (((1,), (1,)), ((), ())), preferred_element_type=f32)


def dot_tn(a, b):
    return lax.dot_general(a, b, (((0,), (0,)), ((), ())), preferred_element_type=f32)


def exact_dot(a, b):
    return lax.dot_general(
        a, b, (((1,), (0,)), ((), ())), preferred_element_type=f32, precision=lax.Precision.HIGHEST
    )


def split_dot(values, matrix):
    high = values.astype(bf16)
    low = (values - high.astype(f32)).astype(bf16)
    return dot(high, matrix) + dot(low, matrix)


def sigmoid(v):
    return 0.5 + 0.5 * jnp.tanh(0.5 * v)


def small_sigmoid(v):
    return 1.0 / (1.0 + jnp.exp(-v))


def expand(values, matrix):
    high = values.astype(bf16).astype(f32)
    lane = lax.broadcasted_iota(jnp.int32, values.shape, 1)
    low = pltpu.roll(values - high, LANES // 2, 1)
    return dot(jnp.where(lane < LANES // 2, high, low).astype(bf16), matrix)


def expand_row(row, matrix):
    return expand(jnp.broadcast_to(row, (8, LANES)), matrix)[0:1]


def span_sum(matrix, values):
    high = values.astype(bf16).astype(f32)
    rest = values - high
    middle = rest.astype(bf16).astype(f32)
    lane = lax.broadcasted_iota(jnp.int32, values.shape, 1)
    packed = jnp.where(
        lane < 32,
        high,
        jnp.where(lane < 64, pltpu.roll(middle, 32, 1), jnp.where(lane < 96, pltpu.roll(rest - middle, 64, 1), 0.0)),
    )
    total = dot(matrix, packed.astype(bf16))
    total = total + pltpu.roll(total, LANES - 32, 1) + pltpu.roll(total, LANES - 64, 1)
    return jnp.where(lane < 32, total, 0.0)


def in_span(rows):
    at = lax.broadcasted_iota(jnp.int32, (rows, rows), 0)
    to = lax.broadcasted_iota(jnp.int32, (rows, rows), 1)
    return at // SPAN == to // SPAN, at, to


def last_rows(logs):
    return [logs[start + SPAN - 1 : start + SPAN, :] for start in range(0, logs.shape[0], SPAN)]


def stacked(row_list):
    row = lax.broadcasted_iota(jnp.int32, (8, LANES), 0)
    total = jnp.broadcast_to(row_list[0], (8, LANES))
    for index, value in enumerate(row_list[1:]):
        total = jnp.where(row > index, value, total)
    return total


def span_gaps(logs):
    spans = range(0, logs.shape[0], SPAN)
    return jnp.concatenate([last - logs[start : start + SPAN] for last, start in zip(last_rows(logs), spans)], axis=0)


def add_rows(total, value):
    return total + jnp.sum(value.reshape(-1, 8, value.shape[1]), axis=0)


def softplus(v):
    u = jnp.exp(-jnp.abs(v))
    series = u * (1.0 - u * (0.5 - u * (1.0 / 3.0 - 0.25 * u)))
    return jnp.maximum(v, 0.0) + jnp.where(u < 0.01, series, jnp.log(1.0 + u))


def causal_mask(rows):
    at = lax.broadcasted_iota(jnp.int32, (rows, rows), 0)
    to = lax.broadcasted_iota(jnp.int32, (rows, rows), 1)
    return at >= to


def head_lanes(heads):
    return lax.broadcasted_iota(jnp.int32, (1, LANES), 1) < heads


def step_sizes(v, heads):
    return jnp.where(head_lanes(heads), softplus(v), 0.0)


def decay_rates(decay_log, heads):
    return jnp.where(head_lanes(heads), -jnp.exp(decay_log), 0.0)


def pair_stack(pair):
    lane = lax.broadcasted_iota(jnp.int32, pair.shape, 1)
    zero = jnp.zeros_like(pair)
    return jnp.concatenate(
        [jnp.where(lane < HEADDIM, pair, zero), jnp.where(lane >= HEADDIM, pair, zero)], axis=0
    )


def pair_decay(logs, logs_t, causal, pair):
    parts = []
    for head in (2 * pair, 2 * pair + 1):
        gap = logs[:, head : head + 1] - logs_t[head : head + 1, :]
        parts.append(jnp.exp(jnp.where(causal, gap, -1e30)))
    return parts


def first_kernel(
    heads,
    hid_ref, halo_ref, gain_ref, w_ref, cx_ref, cbc_ref, sb_ref, dl_ref, ex_ref,
    nb_ref, nbt_ref, xr_ref, xc_ref, bcr_ref, bcc_ref, v_ref, logs_ref, lpre_ref, sloc_ref, fin_ref,
    xext, bext, state, total, tail, xt,
):
    rows = hid_ref.shape[0]
    inner = xr_ref.shape[1]
    gain = gain_ref[...]

    def norm(block):
        h = block.astype(f32)
        scale = lax.rsqrt(jnp.mean(h * h, axis=1, keepdims=True) + epsilon)
        return (h * scale * gain).astype(bf16)

    @pl.when(pl.program_id(0) == 0)
    def _():
        state[...] = jnp.zeros_like(state)
        total[...] = jnp.zeros_like(total)
        before = norm(halo_ref[...])
        xext[0:8, :] = dot(before, w_ref[:, :inner])[8:16]
        bext[0:8, :] = dot(before, w_ref[:, inner + LANES :])[8:16]

    @pl.when(pl.program_id(0) > 0)
    def _():
        xext[0:8, :] = xext[rows : rows + 8, :]
        bext[0:8, :] = bext[rows : rows + 8, :]

    nb = norm(hid_ref[...])
    nb_ref[...] = nb
    nbt_ref[...] = nb.astype(f32).T.astype(bf16)
    xr = dot(nb, w_ref[:, :inner])
    xext[8 : 8 + rows, :] = xr
    xr_ref[...] = xr.astype(bf16)
    bcr = dot(nb, w_ref[:, inner + LANES :])
    bext[8 : 8 + rows, :] = bcr
    bcr_ref[...] = bcr
    v = dot(nb, w_ref[:, inner : inner + LANES]) + sb_ref[...]
    v_ref[...] = v
    bcc = jnp.broadcast_to(cbc_ref[4:5, :], bcr.shape)
    for tap in range(4):
        bcc = bcc + cbc_ref[tap : tap + 1, :] * bext[5 + tap : 5 + tap + rows, :]
    bcc_ref[...] = bcc
    keys = bcc[:, :STATE] * sigmoid(bcc[:, :STATE])
    dt = step_sizes(v, heads)
    la = dt * decay_rates(dl_ref[...], heads)
    ex = ex_ref[...]
    same, to_row, from_row = in_span(rows)
    logs = span_sum(jnp.logical_and(same, to_row >= from_row).astype(bf16), la)
    logs_ref[...] = logs
    lasts = last_rows(logs)
    tail[...] = expand(jnp.exp(span_gaps(logs)) * dt, ex)
    shrinks = expand(jnp.exp(stacked(lasts)), ex)
    for start in range(0, rows, TILE):
        here = slice(start, start + TILE)
        for block in range(inner // LANES):
            lanes = slice(block * LANES, (block + 1) * LANES)
            wide = xext[start : start + TILE + 8, lanes]
            xc = cx_ref[4:5, lanes] + cx_ref[3:4, lanes] * wide[8:]
            for tap in range(3):
                xc = xc + cx_ref[tap : tap + 1, lanes] * pltpu.roll(wide, 3 - tap, 0)[8:]
            xc = xc.astype(bf16)
            xc_ref[here, lanes] = xc
            xc = xc.astype(f32)
            xt[here, lanes] = (xc * sigmoid(xc) * tail[here, lanes]).astype(bf16)
    for at in range(rows // SPAN):
        span = slice(at * SPAN, (at + 1) * SPAN)
        lpre_ref[at * 8 : at * 8 + 8, :] = jnp.broadcast_to(total[0:1, :], (8, LANES))
        keys_t = keys[span].T.astype(bf16)
        for block in range(inner // (2 * LANES)):
            lanes = slice(block * 2 * LANES, (block + 1) * 2 * LANES)
            held = state[:, lanes]
            sloc_ref[at * STATE : (at + 1) * STATE, lanes] = held.astype(bf16)
            state[:, lanes] = held * shrinks[at : at + 1, lanes] + dot(keys_t, xt[span, lanes])
        total[...] = total[...] + lasts[at]

    @pl.when(pl.program_id(0) == pl.num_programs(0) - 1)
    def _():
        fin_ref[0:STATE, :] = state[...].astype(bf16)
        whole = expand(jnp.broadcast_to(jnp.exp(total[0:1, :]), (16, LANES)), ex)
        fin_ref[STATE : STATE + 16, :] = whole.astype(bf16)


def within_kernel(heads, xc_ref, bcc_ref, v_ref, logs_ref, ex_ref, yi_ref):
    causal = causal_mask(SPAN)
    for at in range(xc_ref.shape[0] // SPAN):
        span = slice(at * SPAN, (at + 1) * SPAN)
        xc = xc_ref[span, :].astype(f32)
        dt = step_sizes(v_ref[span, :], heads)
        xd = (xc * sigmoid(xc) * expand(dt, ex_ref[...])).astype(bf16)
        bcc = bcc_ref[span, :]
        bc = (bcc * sigmoid(bcc)).astype(bf16)
        scores = dot_nt(bc[:, STATE:], bc[:, :STATE])
        logs = logs_ref[span, :]
        logs_t = logs.T
        for pair in range(heads // 2):
            lanes = slice(pair * LANES, (pair + 1) * LANES)
            mixing = [(scores * d).astype(bf16) for d in pair_decay(logs, logs_t, causal, pair)]
            yi_ref[span, lanes] = dot(jnp.concatenate(mixing, axis=1), pair_stack(xd[:, lanes])).astype(bf16)


def incoming(refs):
    total = None
    for ref in reversed(refs):
        held = ref[0:STATE, :].astype(f32)
        if total is None:
            total = held
        else:
            total = held + ref[STATE : STATE + 1, :].astype(f32) * total
    return total


def middle_kernel(
    heads, far,
    hid_ref, cg_ref, z_ref, yi_ref, xc_ref, bcc_ref, logs_ref, lpre_ref, sloc_ref, wout_ref, gg_ref,
    skip_ref, ex_ref, fin_ref, *rest,
):
    fins = rest[:far]
    (out_ref, mixed_ref, dz_ref, g_ref, sc_ref, uc_ref, adj_ref, ggg_ref, gskip_ref) = rest[far : far + 9]
    (sin, acc, grown, ssm, gated, gm, ge) = rest[far + 9 :]

    @pl.when(pl.program_id(0) == 0)
    def _():
        sin[...] = incoming(fins) if far else jnp.zeros_like(sin)
        acc[...] = jnp.zeros_like(acc)
        ggg_ref[...] = jnp.zeros_like(ggg_ref)
        gskip_ref[...] = jnp.zeros_like(gskip_ref)

    ex = ex_ref[...]
    rows = hid_ref.shape[0]
    inner = z_ref.shape[1]
    count = inner // LANES
    skip = expand_row(skip_ref[...], ex)
    reads = bcc_ref[:, STATE:]
    reads = reads * sigmoid(reads)
    reads_t = [reads[k * SPAN : (k + 1) * SPAN].T.astype(bf16) for k in range(rows // SPAN)]
    reads = reads.astype(bf16)
    befores = []
    for at in range(rows // SPAN):
        span = slice(at * SPAN, (at + 1) * SPAN)
        states = slice(at * STATE, (at + 1) * STATE)
        before = expand_row(jnp.exp(lpre_ref[at * 8 : at * 8 + 1, :]), ex)
        befores.append(before)
        grown[span, :] = expand(jnp.exp(logs_ref[span, :]), ex)
        for block in range(inner // (2 * LANES)):
            lanes = slice(block * 2 * LANES, (block + 1) * 2 * LANES)
            held = (sloc_ref[states, lanes].astype(f32) + before[:, lanes] * sin[:, lanes]).astype(bf16)
            sc_ref[states, lanes] = held
            ssm[span, lanes] = dot(reads[span], held)

    def forward(index, carry):
        at = slice(index * TILE, (index + 1) * TILE)
        squares = jnp.zeros((TILE, LANES), f32)
        for block in range(count):
            lanes = slice(block * LANES, (block + 1) * LANES)
            xc = xc_ref[at, lanes].astype(f32)
            xs = xc * sigmoid(xc)
            ge[at, lanes] = xs.astype(bf16)
            value = yi_ref[at, lanes].astype(f32) + grown[at, lanes] * ssm[at, lanes] + skip[:, lanes] * xs
            ssm[at, lanes] = value
            z = z_ref[at, lanes].astype(f32)
            value = value * (z * sigmoid(z))
            gated[at, lanes] = value
            squares = squares + value * value
        gs = lax.rsqrt(jnp.sum(squares, axis=1, keepdims=True) / inner + epsilon)
        cross = jnp.zeros((TILE, LANES), f32)
        for block in range(count):
            lanes = slice(block * LANES, (block + 1) * LANES)
            value = gated[at, lanes]
            scaled = value * gs
            mixed_ref[at, lanes] = (scaled * gg_ref[:, lanes]).astype(bf16)
            gradient = cg_ref[at, lanes].astype(f32)
            ggg_ref[:, lanes] = add_rows(ggg_ref[:, lanes], gradient * scaled)
            weighted = gradient * gg_ref[:, lanes]
            gm[at, lanes] = weighted
            cross = cross + weighted * value
        mean = jnp.sum(cross, axis=1, keepdims=True) * (gs * gs * gs / inner)
        for block in range(count):
            lanes = slice(block * LANES, (block + 1) * LANES)
            dgated = gm[at, lanes] * gs - gated[at, lanes] * mean
            z = z_ref[at, lanes].astype(f32)
            sz = sigmoid(z)
            act = z * sz
            dz_ref[at, lanes] = (dgated * ssm[at, lanes] * (sz + act * (1.0 - sz))).astype(bf16)
            g = dgated * act
            g_ref[at, lanes] = g.astype(bf16)
            gskip_ref[:, lanes] = add_rows(gskip_ref[:, lanes], g * ge[at, lanes].astype(f32))
            ge[at, lanes] = (g * grown[at, lanes]).astype(bf16)
        return carry

    for index in range(rows // TILE):
        forward(index, 0)
    out_ref[...] = (hid_ref[...].astype(f32) + dot_nt(mixed_ref[...], wout_ref[...])).astype(bf16)
    for at in range(rows // SPAN):
        span = slice(at * SPAN, (at + 1) * SPAN)
        for block in range(inner // (2 * LANES)):
            lanes = slice(block * 2 * LANES, (block + 1) * 2 * LANES)
            u = dot(reads_t[at], ge[span, lanes])
            uc_ref[at * STATE : (at + 1) * STATE, lanes] = u.astype(bf16)
            acc[:, lanes] += befores[at][:, lanes] * u

    @pl.when(pl.program_id(0) == pl.num_programs(0) - 1)
    def _():
        adj_ref[0:STATE, :] = acc[...].astype(bf16)
        adj_ref[STATE:, :] = fin_ref[...]


def back_within_kernel(
    heads,
    g_ref, xc_ref, bcc_ref, v_ref, logs_ref, sc_ref, ex_ref, ext_ref,
    dxd_ref, dbc_ref, q_ref, grown, carried, ge,
):
    causal = causal_mask(SPAN)
    for at in range(xc_ref.shape[0] // SPAN):
        span = slice(at * SPAN, (at + 1) * SPAN)
        xc = xc_ref[span, :].astype(f32)
        dt = step_sizes(v_ref[span, :], heads)
        xd = (xc * sigmoid(xc) * expand(dt, ex_ref[...])).astype(bf16)
        bcc = bcc_ref[span, :]
        bc = (bcc * sigmoid(bcc)).astype(bf16)
        keys, reads = bc[:, :STATE], bc[:, STATE:]
        scores = dot_nt(reads, keys)
        logs = logs_ref[span, :]
        logs_t = logs.T
        states = slice(at * STATE, (at + 1) * STATE)
        held = sc_ref[states, :]
        grown[...] = expand(jnp.exp(logs), ex_ref[...])
        carried[...] = dot(reads, held)
        dscores = jnp.zeros((SPAN, SPAN), f32)
        lane = lax.broadcasted_iota(jnp.int32, (SPAN, LANES), 1)
        for pair in range(heads // 2):
            lanes = slice(pair * LANES, (pair + 1) * LANES)
            decays = pair_decay(logs, logs_t, causal, pair)
            mixing = jnp.concatenate([(scores * d).astype(bf16) for d in decays], axis=1)
            gp = g_ref[span, lanes]
            xp = xd[:, lanes]
            stack = pair_stack(xp)
            dmix = dot_nt(gp, stack)
            dscores = dscores + dmix[:, :SPAN] * decays[0] + dmix[:, SPAN:] * decays[1]
            both = dot_tn(mixing, gp)
            dxd = jnp.where(lane < HEADDIM, both[:SPAN], both[SPAN:])
            dxd_ref[span, lanes] = dxd.astype(bf16)
            gf = gp.astype(f32)
            scaled = gf * grown[:, lanes]
            ge[:, lanes] = scaled.astype(bf16)
            carried[:, lanes] = gf * dot(mixing, stack) - xp.astype(f32) * dxd + scaled * carried[:, lanes]
        dscores = dscores.astype(bf16)
        dbc_ref[span, :STATE] = dot_tn(dscores, reads)
        dbc_ref[span, STATE:] = dot(dscores, keys) + dot_nt(ge[...], held)
        q_ref[span, :] = split_dot(carried[...], ext_ref[...])


def last_kernel(
    heads, far,
    g_ref, xc_ref, bcc_ref, v_ref, logs_ref, sc_ref, uc_ref, dxd_ref, dbc_ref, q_ref, xr_ref, bcr_ref,
    dl_ref, skip_ref, ex_ref, ext_ref, cx_ref, cbc_ref, *rest,
):
    adjs = rest[:far]
    (grad_ref, gsb_ref, gdl_ref, gcx_ref, gcbc_ref, edge_ref) = rest[far : far + 6]
    (adj, tail, dte, dxu, xt, p3, p4, xext, bext) = rest[far + 6 :]
    inner = xc_ref.shape[1]

    @pl.when(pl.program_id(0) == 0)
    def _():
        adj[...] = incoming(adjs) if far else jnp.zeros_like(adj)
        gsb_ref[...] = jnp.zeros_like(gsb_ref)
        gdl_ref[...] = jnp.zeros_like(gdl_ref)
        gcx_ref[...] = jnp.zeros_like(gcx_ref)
        gcbc_ref[...] = jnp.zeros_like(gcbc_ref)
        xext[SPAN:, :] = jnp.zeros((8, inner), f32)
        bext[SPAN:, :] = jnp.zeros((8, bext.shape[1]), f32)

    ex = ex_ref[...]
    ext = ext_ref[...]
    causal = causal_mask(SPAN)
    not_after = causal.astype(f32)
    strictly = not_after - jnp.logical_and(causal, causal.T).astype(f32)
    upper = 1.0 - strictly
    rates = decay_rates(dl_ref[...], heads)
    skip = expand_row(skip_ref[...], ex)
    for at in reversed(range(xc_ref.shape[0] // SPAN)):
        span = slice(at * SPAN, (at + 1) * SPAN)
        states = slice(at * STATE, (at + 1) * STATE)
        v = v_ref[span, :]
        dt = step_sizes(v, heads)
        bcc = bcc_ref[span, :]
        sbc = sigmoid(bcc)
        keys = (bcc * sbc)[:, :STATE].astype(bf16)
        logs = logs_ref[span, :]
        last = logs[SPAN - 1 : SPAN, :]
        shrink = expand_row(jnp.exp(last), ex)
        tail[...] = expand(jnp.exp(last - logs), ex)
        dte[...] = expand(dt, ex)
        held_low = adj[...].astype(bf16)
        dxu[...] = dot(keys, held_low)
        for start in range(0, SPAN, TILE):
            here = slice(start, start + TILE)
            there = slice(at * SPAN + start, at * SPAN + start + TILE)
            for block in range(inner // LANES):
                lanes = slice(block * LANES, (block + 1) * LANES)
                xc = xc_ref[there, lanes].astype(f32)
                sx = sigmoid(xc)
                xs = xc * sx
                tails = tail[here, lanes]
                update = tails * dxu[here, lanes]
                xd = xs * dte[here, lanes]
                xt[here, lanes] = (xd * tails).astype(bf16)
                p3[here, lanes] = (xd * update).astype(bf16)
                dxd = dxd_ref[there, lanes].astype(f32) + update
                p4[here, lanes] = (xs * dxd).astype(bf16)
                dxs = dte[here, lanes] * dxd + skip[:, lanes] * g_ref[there, lanes].astype(f32)
                xext[here, lanes] = dxs * (sx + xs * (1.0 - sx))
        inners = []
        for block in range(inner // LANES):
            lanes = slice(block * LANES, (block + 1) * LANES)
            held = adj[:, lanes]
            inners.append(jnp.sum(held * sc_ref[states, lanes].astype(f32), axis=0, keepdims=True))
            adj[:, lanes] = held * shrink[:, lanes] + uc_ref[states, lanes].astype(f32)
        within = jnp.concatenate(inners, axis=1) * shrink
        within = split_dot(jnp.broadcast_to(within, (8, inner)), ext)[0:1]
        dkeys = dbc_ref[span, :STATE] + dot_nt(xt[...], held_low)
        dbc = jnp.concatenate([dkeys, dbc_ref[span, STATE:]], axis=1)
        bext[0:SPAN, :] = dbc * (sbc + bcc * sbc * (1.0 - sbc))
        dla = exact_dot(upper, q_ref[span, :]) + exact_dot(strictly, dot(p3[...], ext)) + within
        ddt = rates * dla + dot(p4[...], ext)
        dv = jnp.where(head_lanes(heads), ddt * small_sigmoid(v), 0.0)
        grad_ref[span, inner : inner + LANES] = dv.astype(bf16)
        gsb_ref[...] += jnp.sum(dv, axis=0, keepdims=True)
        gdl_ref[...] += jnp.sum(dt * dla, axis=0, keepdims=True) * rates
        for moved_ref, rows_ref, taps, first, sums in (
            (xext, xr_ref, cx_ref, 0, gcx_ref),
            (bext, bcr_ref, cbc_ref, inner + LANES, gcbc_ref),
        ):
            for block in range(moved_ref.shape[1] // LANES):
                lanes = slice(block * LANES, (block + 1) * LANES)
                parts = [jnp.zeros((8, LANES), f32)] * 5
                for start in range(0, SPAN, TILE):
                    there = slice(at * SPAN + start, at * SPAN + start + TILE)
                    before = rows_ref[there, lanes].astype(f32)
                    wide = moved_ref[start : start + TILE + 8, lanes]
                    total = None
                    for tap in range(4):
                        moved = (wide if tap == 3 else pltpu.roll(wide, TILE + 8 - (3 - tap), 0))[:TILE]
                        term = taps[tap : tap + 1, lanes] * moved
                        total = term if total is None else total + term
                        parts[tap] = add_rows(parts[tap], before * moved)
                    parts[4] = add_rows(parts[4], moved)
                    grad_ref[there, first + lanes.start : first + lanes.stop] = total.astype(bf16)
                for tap in range(5):
                    sums[tap * 8 : tap * 8 + 8, lanes] += parts[tap]
            moved_ref[SPAN:, :] = moved_ref[0:8, :]

    edge_ref[:, :inner] = xext[0:8, :]
    edge_ref[:, inner:] = bext[0:8, :]


def mend_kernel(
    edge_ref, rows_ref, bcr_ref, xr_ref, cx_ref, cbc_ref, gcx_ref, gcbc_ref, ggg_ref, gskip_ref, gsb_ref, gdl_ref,
    ext_ref, grad_ref, sums_ref,
):
    inner = xr_ref.shape[1]
    shared = bcr_ref.shape[1]
    row = lax.broadcasted_iota(jnp.int32, (8, 1), 0)
    sums_ref[...] = jnp.zeros_like(sums_ref)
    grad_ref[...] = rows_ref[...]
    for before, taps, start, first, top, old in (
        (xr_ref, cx_ref, 0, 0, 0, gcx_ref),
        (bcr_ref, cbc_ref, inner, inner + LANES, 6, gcbc_ref),
    ):
        wide_by = before.shape[1]
        late = before[8:16, :].astype(f32)
        total = jnp.zeros((8, wide_by), f32)
        for tap in range(5):
            value = old[tap * 8 : tap * 8 + 8, :]
            if tap < 3:
                moved = pltpu.roll(edge_ref[:, start : start + wide_by], 5 + tap, 0)
                moved = jnp.where(row >= 5 + tap, moved, 0.0)
                total = total + taps[tap : tap + 1, :] * moved
                value = value + late * moved
            sums_ref[top + tap : top + tap + 1, :wide_by] = jnp.sum(value, axis=0, keepdims=True)
        there = slice(first, first + wide_by)
        fixed = rows_ref[8:16, there].astype(f32) + total
        grad_ref[:, there] = jnp.concatenate([rows_ref[0:8, there].astype(f32), fixed], axis=0).astype(bf16)
    sums_ref[5:6, :] = jnp.sum(ggg_ref[...], axis=0, keepdims=True)
    skip = split_dot(gskip_ref[...], ext_ref[...])
    lanes = slice(shared, shared + LANES)
    for index, value in enumerate((gsb_ref[...], gdl_ref[...], jnp.sum(skip, axis=0, keepdims=True))):
        high = value.astype(bf16).astype(f32)
        sums_ref[6 + index : 7 + index, lanes] = high
        sums_ref[9 + index : 10 + index, lanes] = value - high


def gate_kernel(nb_ref, cot_ref, w_ref, z_ref, cg_ref):
    inner = z_ref.shape[1]
    z_ref[...] = dot(nb_ref[...], w_ref[:, :inner]).astype(bf16)
    cg_ref[...] = dot(cot_ref[...], w_ref[:, inner:]).astype(bf16)


def pair_kernel(a_ref, c_ref, b_ref, d_ref, ab_ref, cd_ref):
    ab_ref[...] = dot(a_ref[...], b_ref[...]).astype(bf16)
    cd_ref[...] = dot(c_ref[...], d_ref[...]).astype(bf16)


def product_kernel(a_ref, b_ref, out_ref):
    out_ref[...] = dot(a_ref[...], b_ref[...]).astype(out_ref.dtype)


def join_kernel(shared, chip_ref, held_ref, taken_ref, sums_ref, sums_taken_ref, *outs):
    sums = sums_ref[...].astype(f32) + sums_taken_ref[...].astype(f32)
    lane = lax.broadcasted_iota(jnp.int32, sums.shape, 1)
    row = lax.broadcasted_iota(jnp.int32, sums.shape, 0)
    whole = sums + pltpu.roll(sums, sums.shape[0] - 3, 0)
    high = whole.astype(bf16).astype(f32)
    low = pltpu.roll(whole - high, 3, 0)
    upper = jnp.logical_and(row >= 6, row < 9)
    lower = jnp.logical_and(row >= 9, row < 12)
    split = jnp.where(upper, high, jnp.where(lower, low, sums))
    sums = jnp.where(jnp.logical_and(lane >= shared, lane < shared + LANES), split, sums)
    for turn, out in enumerate(outs):
        at = lax.rem(chip_ref[0] + turn, len(outs))
        total = held_ref[at] + taken_ref[at].astype(f32)
        out[...] = jnp.concatenate([total, sums], axis=0).astype(bf16)


def call(kernel, name, grid, ins, in_specs, outs, out_specs, scratch, flops=10**7, limit=56):
    return pl.pallas_call(
        kernel,
        grid=grid,
        in_specs=in_specs,
        out_specs=out_specs,
        out_shape=outs,
        scratch_shapes=scratch,
        name=name,
        compiler_params=pltpu.CompilerParams(vmem_limit_bytes=limit * 2**20),
        cost_estimate=pl.CostEstimate(flops=flops, bytes_accessed=10**5, transcendentals=0),
    )(*ins)


def rows_of(block, width):
    return pl.BlockSpec((block, width), lambda i: (i, 0))


def whole_of(array):
    return pl.BlockSpec(array.shape, lambda i: (0, 0), pipeline_mode=pl.Buffered(1))


def kept(shape):
    return pl.BlockSpec(shape, lambda i: (0, 0))


def shape(dims, kind):
    return jax.ShapeDtypeStruct(dims, kind)


def pad_rows(array, count):
    return jnp.pad(array, ((0, count - array.shape[0]), (0, 0)))


def pad_lanes(array):
    return jnp.pad(array, ((0, 0), (0, LANES - array.shape[1])))


def per_device(
    hidden_in, cotangent, norm_gain, gate_proj, input_proj, step_proj, shared_proj, output_proj,
    conv_inner, conv_shared, step_bias, decay_log, skip_gain, gated_gain,
):
    tensor_size = lax.axis_size("tensor")
    chips = lax.axis_size("dp") // 2
    place = lax.axis_index("tensor")
    core = lax.axis_index("dp") % 2
    chip = lax.axis_index("dp") // 2
    rows, width = hidden_in.shape
    heads_local = step_proj.shape[1]
    width_local = input_proj.shape[0]
    inner_local = gate_proj.shape[1]
    heads = heads_local * tensor_size
    inner = inner_local * tensor_size
    shared = shared_proj.shape[1]
    per_sequence = SEQ_LEN // rows
    far = per_sequence - 1

    def along(value, step):
        pairs = []
        for start in range(tensor_size):
            end = start + step
            if 0 <= end < tensor_size and start // per_sequence == end // per_sequence:
                pairs.append((start, end))
        return lax.ppermute(value, "tensor", pairs)

    def turn_tensor(value, step):
        return lax.ppermute(value, "tensor", [(i, (i + step) % tensor_size) for i in range(tensor_size)])

    def turn_chip(value, step):
        pairs = [(i, (i // 2 + step) % chips * 2 + i % 2) for i in range(2 * chips)]
        return lax.ppermute(value, "dp", pairs)

    def other_core(value):
        return lax.ppermute(value, "dp", [(i, i ^ 1) for i in range(2 * chips)])

    def in_order(turned, at):
        count = len(turned)
        return [lax.select_n((at - s) % count, *turned) for s in range(count)]

    def to_tensor(value):
        return [value] + [turn_tensor(value, k) for k in range(1, tensor_size)]

    def to_chips(value):
        return [value] + [turn_chip(value, k) for k in range(1, chips)]

    def by_core(value, other):
        first = core == 0
        both = jnp.stack([jnp.where(first, value, other), jnp.where(first, other, value)], axis=1)
        return both.reshape(-1, value.shape[-1])

    def core_rows(value):
        turned = value.reshape(chips, 2, -1, rows)
        return [
            lax.dynamic_index_in_dim(turned, which, 1, False).reshape(-1, rows) for which in (core, 1 - core)
        ]

    def join(first, *others):
        total = first.astype(f32)
        for other in others:
            total = total + other.astype(f32)
        return total.astype(first.dtype)

    def sum_chips_start(total):
        total = total.reshape(chips, -1, total.shape[-1])
        parts = [lax.dynamic_index_in_dim(total, (chip + k) % chips, 0, False) for k in range(chips)]
        return parts[0], [turn_chip(parts[k], k) for k in range(1, chips)]

    tie = lax.optimization_barrier

    def exchange(value, way, later):
        if per_sequence != 4:
            return [along(value, way * step) for step in range(1, far + 1)], later
        near, later = tie((along(value, way), later))
        both = value[:STATE].astype(f32) + value[STATE : STATE + 1].astype(f32) * near[:STATE].astype(f32)
        return [near, along(both.astype(bf16), 2 * way)], later

    small = jnp.concatenate(
        [
            conv_inner,
            gated_gain[None],
            jnp.pad(
                jnp.concatenate([step_bias, decay_log, skip_gain]), (0, inner_local - 3 * heads_local)
            )[None],
            jnp.zeros((1, inner_local), f32),
        ],
        axis=0,
    )
    high = tie(small.astype(bf16))
    low = (small - high.astype(f32)).astype(bf16)
    send = jnp.concatenate([input_proj, high, low], axis=0)
    send = jnp.concatenate([send, jnp.pad(step_proj, ((0, 16), (0, LANES - heads_local)))], axis=1)
    ends = hidden_in[rows - 16 :].reshape(-1)
    ends = jnp.pad(ends, (0, -ends.size % (16 * send.shape[1]))).reshape(-1, send.shape[1])
    given = jnp.concatenate([send, ends], axis=0)
    after = turn_tensor(given, 1)
    first_part = [send, after[: send.shape[0]]] + [turn_tensor(send, k) for k in range(2, tensor_size)]
    halo = after[send.shape[0] :].reshape(-1)[: 16 * width].reshape(16, width)
    halo = jnp.where(place % per_sequence == 0, jnp.zeros_like(halo), halo)
    first_part, second_part = tie((first_part, jnp.concatenate([gate_proj, output_proj], axis=1)))
    first_part = in_order(first_part, place)
    small = [
        p[width_local : width_local + 8, :inner_local].astype(f32) + p[width_local + 8 :, :inner_local].astype(f32)
        for p in first_part
    ]
    first_part = [p[:width_local] for p in first_part]
    steps_part = jnp.concatenate([p[:, inner_local : inner_local + heads_local] for p in first_part], axis=1)
    first_part = jnp.concatenate(
        [p[:, :inner_local] for p in first_part]
        + [pad_lanes(jnp.concatenate([steps_part, norm_gain[:, None]], axis=1)), shared_proj],
        axis=1,
    )
    wide_head = lax.broadcasted_iota(jnp.int32, (LANES, inner), 1) // HEADDIM
    ex = (lax.broadcasted_iota(jnp.int32, (LANES, inner), 0) % (LANES // 2) == wide_head).astype(bf16)
    tall_head = lax.broadcasted_iota(jnp.int32, (inner, LANES), 0) // HEADDIM
    ext = (lax.broadcasted_iota(jnp.int32, (inner, LANES), 1) == tall_head).astype(bf16)
    first_part, second_part, (cot_own, cot_given), ex, ext = tie(
        (to_chips(first_part), to_tensor(second_part), core_rows(cotangent.T), ex, ext)
    )
    first_part = jnp.stack(in_order(first_part, chip))
    weights = by_core(first_part, other_core(first_part))
    second_part = in_order(second_part, place)
    second_part = jnp.concatenate(
        [p[:, :inner_local] for p in second_part] + [p[:, inner_local:] for p in second_part], axis=1
    )
    second_part = to_chips(second_part)
    gain = weights[:, inner + heads].astype(f32)[None]

    wide = jnp.concatenate(small, axis=1)
    cx = pad_rows(wide[:5], 8)
    gg = wide[5:6]
    cbc = pad_rows(conv_shared, 8)

    def head_row(index):
        at = slice(index * heads_local, (index + 1) * heads_local)
        return pad_lanes(jnp.concatenate([p[6:7, at] for p in small], axis=1))

    sb, dl, sg = head_row(0), head_row(1), head_row(2)

    block = BLOCK * SPAN
    steps = rows // block
    chunks = rows // SPAN
    grid = (steps,)
    nb, nbt, xr, xc, bcr, bcc, v, logs, lpre, sloc, fin = call(
        functools.partial(first_kernel, heads),
        "first",
        grid,
        (hidden_in, halo, gain, weights, cx, cbc, sb, dl, ex),
        [rows_of(block, width)] + [whole_of(a) for a in (halo, gain, weights, cx, cbc, sb, dl, ex)],
        [
            shape((rows, width), bf16), shape((width, rows), bf16), shape((rows, inner), bf16), shape((rows, inner), bf16),
            shape((rows, shared), f32), shape((rows, shared), f32), shape((rows, LANES), f32),
            shape((rows, LANES), f32), shape((chunks * 8, LANES), f32),
            shape((chunks * STATE, inner), bf16), shape((STATE + 16, inner), bf16),
        ],
        [
            rows_of(block, width), pl.BlockSpec((width, block), lambda i: (0, i)), rows_of(block, inner),
            rows_of(block, inner), rows_of(block, shared), rows_of(block, shared), rows_of(block, LANES),
            rows_of(block, LANES), rows_of(8 * BLOCK, LANES),
            rows_of(BLOCK * STATE, inner), kept((STATE + 16, inner)),
        ],
        [
            pltpu.VMEM((block + 8, inner), f32), pltpu.VMEM((block + 8, shared), f32),
            pltpu.VMEM((STATE, inner), f32), pltpu.VMEM((8, LANES), f32),
            pltpu.VMEM((block, inner), f32), pltpu.VMEM((block, inner), bf16),
        ],
    )
    (yi,) = call(
        functools.partial(within_kernel, heads),
        "within",
        grid,
        (xc, bcc, v, logs, ex),
        [rows_of(block, inner), rows_of(block, shared), rows_of(block, LANES), rows_of(block, LANES), whole_of(ex)],
        [shape((rows, inner), bf16)],
        [rows_of(block, inner)],
        [],
        flops=10**10,
    )
    fins, (second_part, yi) = exchange(fin, 1, (second_part, yi))
    far = len(fins)
    second_part = jnp.stack(in_order(second_part, chip))
    second_other = other_core(second_part)
    second_part = by_core(second_part, second_other)
    second_part, nb_rows = tie((second_part, core_rows(nbt)))
    nb_own, nb_given = nb_rows
    z, cg = call(
        gate_kernel,
        "gate",
        grid,
        (nb, cotangent, second_part),
        [rows_of(block, width), rows_of(block, width), whole_of(second_part)],
        [shape((rows, inner), bf16)] * 2,
        [rows_of(block, inner)] * 2,
        [],
    )
    state_rows = rows_of(BLOCK * STATE, inner)
    out, mixed, dz, g, sc, uc, adj, ggg, gskip = call(
        functools.partial(middle_kernel, heads, far),
        "middle",
        grid,
        (hidden_in, cg, z, yi, xc, bcc, logs, lpre, sloc, second_part, gg, sg, ex, fin, *fins),
        [
            rows_of(block, width), rows_of(block, inner), rows_of(block, inner), rows_of(block, inner),
            rows_of(block, inner), rows_of(block, shared), rows_of(block, LANES), rows_of(8 * BLOCK, LANES), state_rows,
        ]
        + [pl.BlockSpec((width, inner), lambda i: (0, 1), pipeline_mode=pl.Buffered(1))]
        + [whole_of(a) for a in (gg, sg, ex)]
        + [pl.BlockSpec((16, inner), lambda i: (STATE // 16, 0))]
        + [whole_of(a) for a in fins],
        [
            shape((rows, width), bf16), shape((rows, inner), bf16), shape((rows, inner), bf16),
            shape((rows, inner), bf16), shape((chunks * STATE, inner), bf16), shape((chunks * STATE, inner), bf16),
            shape((STATE + 16, inner), bf16), shape((8, inner), f32), shape((8, inner), f32),
        ],
        [
            rows_of(block, width), rows_of(block, inner), rows_of(block, inner), rows_of(block, inner),
            state_rows, state_rows, kept((STATE + 16, inner)), kept((8, inner)), kept((8, inner)),
        ],
        [pltpu.VMEM((STATE, inner), f32)] * 2 + [pltpu.VMEM((block, inner), f32)] * 4 + [pltpu.VMEM((block, inner), bf16)],
    )
    backs, g = exchange(adj, -1, g)
    dxd, dbc, q = call(
        functools.partial(back_within_kernel, heads),
        "back_within",
        grid,
        (g, xc, bcc, v, logs, sc, ex, ext),
        [
            rows_of(block, inner), rows_of(block, inner), rows_of(block, shared), rows_of(block, LANES),
            rows_of(block, LANES), state_rows, whole_of(ex), whole_of(ext),
        ],
        [shape((rows, inner), bf16), shape((rows, shared), f32), shape((rows, LANES), f32)],
        [rows_of(block, inner), rows_of(block, shared), rows_of(block, LANES)],
        [pltpu.VMEM((SPAN, inner), f32), pltpu.VMEM((SPAN, inner), f32), pltpu.VMEM((SPAN, inner), bf16)],
        flops=10**10,
    )

    def pair_product(a, c):
        tile = inner // 3
        tiled = pl.BlockSpec((rows, tile), lambda i: (0, i))
        return call(
            pair_kernel,
            "pair",
            (3,),
            (a, c, dz, mixed),
            [whole_of(a), whole_of(c), tiled, tiled],
            [shape((a.shape[0], inner), bf16)] * 2,
            [pl.BlockSpec((a.shape[0], tile), lambda i: (0, i))] * 2,
            [],
        )

    taken = [other_core(value) for value in pair_product(nb_given, cot_given)]
    held = pair_product(nb_own, cot_own)
    backs, taken, held, dxd = tie((backs, taken, held, dxd))
    second_parts, second_taken = sum_chips_start(
        jnp.concatenate([join(own, other).astype(bf16) for own, other in zip(held, taken)], axis=1)
    )

    def turned(size, wide_by):
        return pl.BlockSpec((size, wide_by), lambda i: (steps - 1 - i, 0))

    wide_rows = inner + LANES + shared
    grad_rows, gsb, gdl, gcx, gcbc, edge = call(
        functools.partial(last_kernel, heads, far),
        "last",
        grid,
        (g, xc, bcc, v, logs, sc, uc, dxd, dbc, q, xr, bcr, dl, sg, ex, ext, cx, cbc, *backs),
        [
            turned(block, inner), turned(block, inner), turned(block, shared), turned(block, LANES),
            turned(block, LANES), turned(BLOCK * STATE, inner), turned(BLOCK * STATE, inner), turned(block, inner),
            turned(block, shared), turned(block, LANES), turned(block, inner), turned(block, shared),
        ]
        + [whole_of(a) for a in (dl, sg, ex, ext, cx, cbc, *backs)],
        [
            shape((rows, wide_rows), bf16), shape((1, LANES), f32), shape((1, LANES), f32),
            shape((40, inner), f32), shape((40, shared), f32), shape((8, inner + shared), f32),
        ],
        [
            turned(block, wide_rows), kept((1, LANES)), kept((1, LANES)), kept((40, inner)), kept((40, shared)),
            kept((8, inner + shared)),
        ],
        [pltpu.VMEM((STATE, inner), f32)]
        + [pltpu.VMEM((SPAN, inner), f32)] * 3
        + [pltpu.VMEM((SPAN, inner), bf16)] * 3
        + [pltpu.VMEM((SPAN + 8, inner), f32), pltpu.VMEM((SPAN + 8, shared), f32)],
        flops=10**10,
    )
    edge, second_taken = tie((along(edge, -1), second_taken))
    second_sum = join(second_parts, *second_taken)
    second_pack = []
    for k in range(tensor_size):
        start = (place + k) % tensor_size * inner_local
        second_pack.append(
            jnp.concatenate(
                [
                    lax.dynamic_slice_in_dim(second_sum[:, :inner], start, inner_local, 1),
                    lax.dynamic_slice_in_dim(second_sum[:, inner:], start, inner_local, 1),
                ],
                axis=1,
            )
        )
    edge, second_pack = tie((edge, second_pack))
    second_kept = second_pack[0]
    second_last = [turn_tensor(second_pack[k], k) for k in range(1, tensor_size)]
    ending = rows // 16 - 1

    def end_rows(wide_by):
        return pl.BlockSpec((16, wide_by), lambda i: (ending, 0))

    sums_in = (cx, cbc, gcx, gcbc, ggg, gskip, gsb, gdl, ext)
    grad_rows, sums = pl.pallas_call(
        mend_kernel,
        grid=(1,),
        in_specs=[kept(edge.shape), end_rows(wide_rows), end_rows(shared), end_rows(inner)]
        + [kept(a.shape) for a in sums_in],
        out_specs=[end_rows(wide_rows), kept((16, inner))],
        out_shape=[shape(grad_rows.shape, bf16), shape((16, inner), f32)],
        input_output_aliases={1: 0},
        name="mend",
    )(edge, grad_rows, bcr, xr, *sums_in)
    def product(a, b, kind, flops=10**7):
        tile = wide_rows // 3
        (value,) = call(
            product_kernel,
            "product",
            (3,),
            (a, b),
            [whole_of(a), pl.BlockSpec((rows, tile), lambda i: (0, i))],
            [shape((a.shape[0], wide_rows), kind)],
            [pl.BlockSpec((a.shape[0], tile), lambda i: (0, i))],
            [],
            flops=flops,
        )
        return value

    given = product(nb_given, grad_rows, bf16)
    sums = jnp.pad(sums, ((0, 0), (0, wide_rows - inner))).astype(bf16)
    taken, sums_taken = other_core(given), other_core(sums)
    given, grad_rows = tie((given, grad_rows))
    held = product(nb_own, grad_rows, f32, 10**10)
    taken, sums_taken, second_last = tie((taken, sums_taken, second_last))
    joined = (
        held.reshape(chips, width_local, wide_rows), taken.reshape(chips, width_local, wide_rows), sums, sums_taken,
    )
    part = (width_local + sums.shape[0], wide_rows)

    def whole_block(dims):
        return pl.BlockSpec(dims, lambda i, at: (0,) * len(dims))

    parts = pl.pallas_call(
        functools.partial(join_kernel, shared),
        grid_spec=pltpu.PrefetchScalarGridSpec(
            num_scalar_prefetch=1,
            grid=(1,),
            in_specs=[whole_block(value.shape) for value in joined],
            out_specs=[whole_block(part)] * chips,
        ),
        out_shape=[shape(part, bf16)] * chips,
        name="join",
        compiler_params=pltpu.CompilerParams(vmem_limit_bytes=40 * 2**20),
    )(chip[None].astype(jnp.int32), *joined)
    _, grad_rows, dz, second_part = tie((parts, grad_rows, dz, second_part))
    wz = second_part[:, :inner]
    first_taken = [turn_chip(parts[k], k) for k in range(1, chips)]
    grad_normed = dot_nt(dz, wz) + dot_nt(grad_rows, weights)
    h = hidden_in.astype(f32)
    scale = lax.rsqrt(jnp.mean(h * h, axis=1, keepdims=True) + epsilon)
    weighted = grad_normed * gain
    grad_hidden = (
        cotangent.astype(f32)
        + weighted * scale
        - h * scale**3 * jnp.mean(weighted * h, axis=1, keepdims=True)
    ).astype(bf16)
    first_taken, grad_hidden = tie((first_taken, grad_hidden))
    first_sum = join(parts[0].astype(f32), *first_taken)
    sums = first_sum[width_local:]
    first_sum = first_sum[:width_local]
    mine = lax.axis_index("dp") * width_local

    def own_rows(value):
        return lax.dynamic_slice_in_dim(value, mine, width_local, axis=0).astype(f32)

    columns = lax.broadcasted_iota(jnp.int32, first_sum.shape, 1)
    counted = jnp.where(columns == inner + heads, 0.0, own_rows(weights) * first_sum)
    norm = jnp.sum(counted, axis=1) + jnp.sum(own_rows(wz) * second_sum[:, :inner].astype(f32), axis=1)
    norm = (norm / norm_gain.astype(f32)).reshape(tensor_size, -1)
    shared_rows = width_local // tensor_size
    wide_by = inner_local + LANES
    step_sum = first_sum[:, inner : inner + LANES]
    head_all = sums[6:9, shared : shared + LANES] + sums[9:12, shared : shared + LANES]
    head_high = tie(head_all.astype(bf16)).astype(f32)
    head_low = head_all - head_high
    first_kept, first_taken = None, []
    for k in range(tensor_size):
        to = (place + k) % tensor_size
        shared_to = lax.dynamic_slice_in_dim(first_sum[:, inner + LANES :], to * shared_rows, shared_rows, 0)
        norm_to = lax.dynamic_slice_in_dim(norm, to, 1, 0)
        block_to = jnp.concatenate(
            [
                lax.dynamic_slice_in_dim(first_sum[:, :inner], to * inner_local, inner_local, 1),
                lax.dynamic_slice_in_dim(sums[:6, :inner], to * inner_local, inner_local, 1),
            ],
            axis=0,
        )
        side = jnp.concatenate([step_sum, head_high, head_low], axis=0)
        block_to = jnp.concatenate([block_to, side], axis=1)
        low = jnp.concatenate([shared_to, sums[6:11, :shared], jnp.pad(norm_to, ((0, 0), (0, shared - shared_rows)))])
        block_to = jnp.concatenate([block_to, jnp.pad(low, ((0, 0), (0, wide_by - shared)))], axis=0)
        block_to = jnp.pad(block_to, ((0, -block_to.shape[0] % 16), (0, 0))).astype(bf16)
        if k == 0:
            first_kept = block_to
        else:
            first_taken.append(turn_tensor(block_to, k))
    first_sum = join(first_kept.astype(f32), *first_taken)
    second_sum = join(second_kept.astype(f32), *second_last)
    low = first_sum[width_local + 6 :]
    sums = first_sum[width_local : width_local + 6]
    grad_shared = low[:shared_rows, :shared]
    grad_norm = low[shared_rows + 5, :shared_rows]

    def head_cut(value):
        return lax.dynamic_slice_in_dim(value, inner_local + place * heads_local, heads_local, 1)

    head_sums = head_cut(sums[:3] + sums[3:])

    return (
        out,
        grad_hidden,
        grad_norm,
        second_sum[:, :inner_local],
        first_sum[:width_local, :inner_local],
        head_cut(first_sum[:width_local]),
        grad_shared,
        second_sum[:, inner_local:],
        sums[:5, :inner_local],
        low[shared_rows : shared_rows + 5, :shared],
        head_sums[0],
        head_sums[1],
        head_sums[2],
        sums[5, :inner_local],
    )


def solution(mesh):
    placed = (
        P(("dp", "tensor"), None), P(("dp", "tensor"), None), P("dp"), P("dp", "tensor"), P("dp", "tensor"),
        P("dp", "tensor"), P("dp", None), P("dp", "tensor"), P(None, "tensor"), P(), P("tensor"), P("tensor"),
        P("tensor"), P("tensor"),
    )
    results = (
        P(("dp", "tensor"), None), P(("dp", "tensor"), None), P(("dp", "tensor")), P("dp", "tensor"),
        P("dp", "tensor"), P("dp", "tensor"), P(("dp", "tensor"), None), P("dp", "tensor"), P(None, "tensor"),
        P(), P("tensor"), P("tensor"), P("tensor"), P("tensor"),
    )
    return jax.shard_map(per_device, mesh=mesh, in_specs=placed, out_specs=results, check_vma=False)
```
